32 devices in a mesh: seq: 8 (over z, y), wt: 4 (over x, core).
Axes of the slice: x: 2, y: 2, z: 4, core: 2. Of those that a mesh axis runs over, the one named last changes fastest.
Arguments:
- tokens: bfloat16 [4, 1024, 1024], P('wt', 'seq'), may hold values from -6 to 6
- w_qkv: bfloat16 [1024, 3072], P(('seq', 'wt')), may hold values from -0.25 to 0.25
- w_attn_out: bfloat16 [1024, 1024], P(('seq', 'wt')), may hold values from -1 to 1
- w_in: bfloat16 [1024, 2, 2624], P('seq', None, 'wt'), may hold values from -0.1875 to 0.1875
- w_mlp_out: bfloat16 [1024, 2624], P('seq', 'wt'), may hold values from -0.15625 to 0.15625
- gain_one: bfloat16 [1024], P(('seq', 'wt')), may hold values from 0.5 to 1.5
- gain_two: bfloat16 [1024], P(('seq', 'wt')), may hold values from 0.5 to 1.5
- cotangent: bfloat16 [4, 1024, 1024], P('wt', 'seq'), may hold values from -6 to 6
Outputs:
- activations: bfloat16 [4, 1024, 1024], P('wt', 'seq')
- input_grad: bfloat16 [4, 1024, 1024], P('wt', 'seq')
- grad_qkv: float32 [1024, 3072], P(('seq', 'wt'))
- grad_attn_out: float32 [1024, 1024], P(('seq', 'wt'))
- grad_in: float32 [1024, 2, 2624], P('seq', None, 'wt')
- grad_mlp_out: float32 [1024, 2624], P('seq', 'wt')
- grad_gain_one: float32 [1024], P(('seq', 'wt'))
- grad_gain_two: float32 [1024], P(('seq', 'wt'))
The draws below stay inside these ranges and needn't reach their ends.
All inputs are finite; a program needn't handle non-finite values.
Results may differ from the reference program's by a relative error of at most 0.02.
Values may be sent and summed in bfloat16 or wider, within the bound.
No kernel may reach another device: no remote copies, remote signals or barrier semaphores. Data moves between devices by JAX's collectives and lax.ppermute only.
A program may use at most 128 MiB of HBM per device.

```python
import math
import jax
import jax.numpy as jnp
from jax import lax

D = 1024
H = 16
HD = 64
FF = 2624
HALVES = 4
SLICE = 1024
LENGTH = 2048


def block_levels(key, extent, shards, least, largest):
    factor_of = 1.0
    for position, shards_of in shards:
        steps = jax.random.uniform(jax.random.fold_in(jax.random.fold_in(key, 6), position), (shards_of,), jnp.float32, least / len(shards), largest / len(shards))
        factor_of = factor_of * jnp.repeat(jnp.exp(steps), extent[position] // shards_of).reshape((-1,) + (1,) * (len(extent) - 1 - position))
    return factor_of


def gaussian(stream_key, shape, deviation, reach, cuts=(), kind=jnp.bfloat16):
    array = jax.random.normal(stream_key, shape, jnp.float32) * deviation
    if len(cuts) > 0:
        array = block_levels(stream_key, shape, cuts, -0.22, 0.18) * array
    return jnp.clip(array, min=-reach, max=reach).astype(kind)


def setup_inputs(seed: int = 0) -> dict:
    streams_of = jax.random.split(jax.random.key(seed), 9)
    return {
        "tokens": gaussian(streams_of[0], (HALVES, SLICE, D), 1.0, 6.0, ((0, 4), (1, 8))),
        "w_qkv": gaussian(streams_of[1], (D, 3 * D), (D // 2) ** -0.5, 0.25, ((0, 32),)),
        "w_attn_out": gaussian(streams_of[2], (D, D), (max(D * 64 // LENGTH, 1)) ** -0.5, 1.0, ((0, 32),)),
        "w_in": gaussian(streams_of[3], (D, 2, FF), D ** -0.5, 0.1875, ((0, 8), (2, 4))),
        "w_mlp_out": gaussian(streams_of[4], (D, FF), (FF // 2) ** -0.5, 0.15625, ((0, 8), (1, 4))),
        "gain_one": jnp.clip(1.0 + 0.1 * jax.random.normal(streams_of[5], (D,), jnp.float32), 0.5, 1.5).astype(jnp.bfloat16),
        "gain_two": jnp.clip(1.0 + 0.1 * jax.random.normal(streams_of[6], (D,), jnp.float32), 0.5, 1.5).astype(jnp.bfloat16),
        "cotangent": gaussian(streams_of[7], (HALVES, SLICE, D), 1.0, 6.0, ((0, 4), (1, 8))),
    }


@jax.custom_vjp
def low(v):
    return lax.optimization_barrier(v.astype(jnp.bfloat16)).astype(jnp.float32)

@jax.custom_vjp
def low_back(v):
    return v

def low_keep(v):
    return (low(v), None)

def low_pass(kept, grad):
    return (grad,)

def back_keep(v):
    return (v, None)

def back_low(kept, grad):
    return (low(grad),)
low.defvjp(low_keep, low_pass)
low_back.defvjp(back_keep, back_low)
highest = lax.Precision.HIGHEST
epsilon = 1e-05
rope_base = 160000.0

def layer_norm(features, scaling):
    average = lax.optimization_barrier(jnp.mean(features, axis=-1, keepdims=True))
    centred = features - average
    spread = lax.optimization_barrier(jnp.mean(centred * centred, axis=-1, keepdims=True))
    return centred * lax.rsqrt(spread + epsilon) * scaling

def rotary_tables(positions, head_width):
    half_width = head_width // 2
    frequency = jnp.exp(jnp.arange(half_width).astype(positions.dtype) * (-2.0 * math.log(rope_base) / head_width))
    angles = positions[:, None] * frequency[None, :]
    cosine = jnp.concatenate([jnp.cos(angles), jnp.cos(angles)], axis=-1)
    sine_table = jnp.concatenate([jnp.sin(angles), jnp.sin(angles)], axis=-1)
    return (cosine, sine_table)

def rotate(vectors, cosine, sine_table):
    half_width = vectors.shape[-1] // 2
    turned = jnp.concatenate([-vectors[..., half_width:], vectors[..., :half_width]], axis=-1)
    return vectors * cosine[:, None, :] + turned * sine_table[:, None, :]

def exact_gelu(inner):
    return jax.nn.gelu(inner, approximate=False)

def forward(tokens, w_qkv, w_attn_out, w_in, w_mlp_out, gain_one, gain_two):

    def one_sequence(seq_tokens):
        length = seq_tokens.shape[0]
        normed = low(layer_norm(seq_tokens, gain_one))
        packed = low_back(jnp.dot(normed, w_qkv, precision=highest)).reshape(length, H, 3 * HD)
        cosine, sine_table = rotary_tables(jnp.arange(length).astype(seq_tokens.dtype), HD)
        queries = low(rotate(packed[..., :HD], cosine, sine_table))
        keys = low(rotate(packed[..., HD:2 * HD], cosine, sine_table))
        values = low(packed[..., 2 * HD:])
        query_span = math.gcd(length, 512)
        score_scale = 1.0 / math.sqrt(HD)

        def attend(query_block):
            scores = low_back(jnp.einsum('qhd,khd->hqk', query_block, keys, precision=highest) * score_scale)
            top_score = lax.optimization_barrier(jnp.max(scores, axis=-1, keepdims=True))
            raised = jnp.exp(scores - top_score)
            probs = low(raised / lax.optimization_barrier(jnp.sum(raised, axis=-1, keepdims=True)))
            return jnp.einsum('hqk,khd->qhd', probs, values, precision=highest)
        attended = lax.map(jax.checkpoint(attend), queries.reshape(length // query_span, query_span, H, HD))
        attended = low_back(low(attended.reshape(length, H * HD)))
        middle = seq_tokens + jnp.dot(attended, w_attn_out, precision=highest)
        normed_two = low(layer_norm(middle, gain_two))
        projected = low_back(jnp.einsum('td,dcf->tcf', normed_two, w_in, precision=highest))
        hidden = low(exact_gelu(projected[:, 0]) * projected[:, 1])
        return middle + jnp.dot(hidden, w_mlp_out.T, precision=highest)
    halves, slice_len, width = tokens.shape
    whole = tokens.reshape(halves // 2, 2 * slice_len, width)
    return lax.map(jax.checkpoint(one_sequence), whole).reshape(halves, slice_len, width)

def reference(tokens, w_qkv, w_attn_out, w_in, w_mlp_out, gain_one, gain_two, cotangent):
    inputs = tuple((item.astype(jnp.float32) for item in (tokens, w_qkv, w_attn_out, w_in, w_mlp_out, gain_one, gain_two)))
    output, pull = jax.vjp(forward, *inputs)
    grads = pull(cotangent.astype(jnp.float32))
    return (output.astype(jnp.bfloat16), grads[0].astype(jnp.bfloat16), grads[1], grads[2], grads[3], grads[4], grads[5], grads[6])
```

```python
import math

import jax
import jax.numpy as jnp
from jax import lax
from jax.sharding import PartitionSpec as P

H = 16
HD = 64


epsilon = 1e-05
rope_base = 160000.0
half_type = jnp.bfloat16


def ring_order(count):
    half = count // 2
    return [2 * p if p < half else 2 * (count - 1 - p) + 1 for p in range(count)]


def ring_pairs(count):
    order = ring_order(count)
    right = [(order[p], order[(p + 1) % count]) for p in range(count)]
    left = [(target, source) for source, target in right]
    return right, left


def cut_rows(rows):
    return rows // 32 * 16 if rows >= 32 else rows // 2


def ring_gather(block, axis="seq"):
    count = lax.axis_size(axis)
    right, left = ring_pairs(count)
    half = count // 2
    behind, ahead = [block], [block]
    for _ in range(1, half):
        behind.append(lax.ppermute(behind[-1], axis, right))
        ahead.append(lax.ppermute(ahead[-1], axis, left))
    cut = cut_rows(block.shape[0])
    far = jnp.concatenate(
        [
            lax.ppermute(behind[-1][:cut], axis, right),
            lax.ppermute(ahead[-1][cut:], axis, left),
        ],
        axis=0,
    )
    return ahead[:half] + [far] + [behind[count - k] for k in range(half + 1, count)]


def ring_sum(parts, axis="seq"):
    count = lax.axis_size(axis)
    right, left = ring_pairs(count)
    half = count // 2
    cut = cut_rows(parts[0].shape[0])
    top = lax.ppermute(parts[half][:cut].astype(half_type), axis, right)
    bottom = lax.ppermute(parts[half][cut:].astype(half_type), axis, left)
    for off in range(half - 1, 0, -1):
        up = parts[off].astype(jnp.float32)
        down = parts[count - off].astype(jnp.float32)
        if off == half - 1:
            up = jnp.concatenate([up[:cut] + top.astype(jnp.float32), up[cut:]], axis=0)
            down = jnp.concatenate([down[:cut], down[cut:] + bottom.astype(jnp.float32)], axis=0)
        else:
            up = up + top.astype(jnp.float32)
            down = down + bottom.astype(jnp.float32)
        top = lax.ppermute(up.astype(half_type), axis, right)
        bottom = lax.ppermute(down.astype(half_type), axis, left)
    return parts[0].astype(jnp.float32) + top.astype(jnp.float32) + bottom.astype(jnp.float32)


def from_partner(value, axis, bit):
    mask = 2**bit
    pairs = [(source, source ^ mask) for source in range(lax.axis_size(axis))]
    return lax.ppermute(value, axis, pairs)


def bits_of(axis):
    return int(math.log2(lax.axis_size(axis)))


def cube_gather(block, axis="wt"):
    place = lax.axis_index(axis)
    bits = bits_of(axis)
    value = block
    for done, bit in enumerate(range(bits - 1, -1, -1)):
        other = from_partner(value, axis, bit)
        low = (place >> bit) % 2 == 0
        value = jnp.stack([jnp.where(low, value, other), jnp.where(low, other, value)], axis=done)
    return value.reshape((2**bits,) + block.shape)


def cube_sum(value, axis="wt"):
    place = lax.axis_index(axis)
    bits = bits_of(axis)
    value = value.reshape((2,) * bits + value.shape[1:])
    for bit in range(bits):
        at = bits - 1 - bit
        mine = (place >> bit) % 2
        keep = lax.dynamic_index_in_dim(value, mine, at, keepdims=False)
        give = lax.dynamic_index_in_dim(value, 1 - mine, at, keepdims=False)
        value = keep.astype(jnp.float32) + from_partner(give.astype(half_type), axis, bit).astype(
            jnp.float32
        )
    return value


def group_gather(rows, axis="wt"):
    for bit in range(bits_of(axis) - 1, -1, -1):
        rows = jnp.concatenate([rows, from_partner(rows, axis, bit)], axis=0)
    return rows


def group_sum(rows, axis="wt"):
    for bit in range(bits_of(axis)):
        half = rows.shape[0] // 2
        got = from_partner(rows[half:].astype(half_type), axis, bit)
        rows = rows[:half].astype(jnp.float32) + got.astype(jnp.float32)
    return rows


def normalize(features):
    average = jnp.mean(features, axis=-1, keepdims=True)
    centred = features - average
    spread = jnp.mean(centred * centred, axis=-1, keepdims=True)
    scale = lax.rsqrt(spread + epsilon)
    return centred * scale, scale


def normalize_back(d_unit, unit, scale):
    return scale * (
        d_unit
        - jnp.mean(d_unit, axis=-1, keepdims=True)
        - unit * jnp.mean(d_unit * unit, axis=-1, keepdims=True)
    )


def rotary_tables(positions, head_width):
    half_width = head_width // 2
    frequency = jnp.exp(
        jnp.arange(half_width).astype(jnp.float32) * (-2.0 * math.log(rope_base) / head_width)
    )
    angles = positions[:, None] * frequency[None, :]
    cosine = jnp.concatenate([jnp.cos(angles), jnp.cos(angles)], axis=-1)
    sine_table = jnp.concatenate([jnp.sin(angles), jnp.sin(angles)], axis=-1)
    return (cosine, sine_table)


def rotate(vectors, cosine, sine_table):
    half_width = vectors.shape[-1] // 2
    turned = jnp.concatenate([-vectors[..., half_width:], vectors[..., :half_width]], axis=-1)
    return vectors * cosine[:, None, :] + turned * sine_table[:, None, :]


def exact_gelu(inner):
    return jax.nn.gelu(inner, approximate=False)


def dot_on(left, right, left_dim, right_dim):
    return lax.dot_general(
        left, right, (((left_dim,), (right_dim,)), ((), ())), preferred_element_type=jnp.float32
    )


def attention_forward(queries, pairs, score_scale):
    head_rows, local_heads, head_width = queries.shape
    key_rows = pairs.shape[0]
    key_span = math.gcd(key_rows, 512)
    pair_blocks = pairs.reshape(key_rows // key_span, key_span, local_heads, 2 * head_width)

    def forward_step(carry, pair_block):
        top_score, weight_sum, accum = carry
        scores = (
            jnp.einsum(
                "qhd,khd->hqk",
                queries,
                pair_block[..., :head_width],
                preferred_element_type=jnp.float32,
            )
            * score_scale
        )
        new_top = jnp.maximum(top_score, jnp.max(scores, axis=-1))
        raised = jnp.exp(scores - new_top[..., None])
        shrink = jnp.exp(top_score - new_top)
        weight_sum = weight_sum * shrink + jnp.sum(raised, axis=-1)
        accum = accum * shrink.T[..., None] + jnp.einsum(
            "hqk,khd->qhd",
            raised.astype(jnp.bfloat16),
            pair_block[..., head_width:],
            preferred_element_type=jnp.float32,
        )
        return ((new_top, weight_sum, accum), None)

    start_carry = (
        jnp.full((local_heads, head_rows), -jnp.inf, jnp.float32),
        jnp.zeros((local_heads, head_rows), jnp.float32),
        jnp.zeros((head_rows, local_heads, head_width), jnp.float32),
    )
    (top_score, weight_sum, accum), _ = lax.scan(forward_step, start_carry, pair_blocks)
    return accum / weight_sum.T[..., None], top_score + jnp.log(weight_sum)


def attention_backward(queries, pairs, attended_raw, log_total, d_heads, score_scale):
    head_rows, local_heads, head_width = queries.shape
    key_rows = pairs.shape[0]
    key_span = math.gcd(key_rows, 512)
    pair_blocks = pairs.reshape(key_rows // key_span, key_span, local_heads, 2 * head_width)
    row_delta = jnp.sum(d_heads.astype(jnp.float32) * attended_raw, axis=-1).T

    def backward_step(d_query, pair_block):
        key_block = pair_block[..., :head_width]
        value_block = pair_block[..., head_width:]
        scores = (
            jnp.einsum("qhd,khd->hqk", queries, key_block, preferred_element_type=jnp.float32)
            * score_scale
        )
        probs = jnp.exp(scores - log_total[..., None])
        d_probs = jnp.einsum(
            "qhd,khd->hqk", d_heads, value_block, preferred_element_type=jnp.float32
        )
        d_scores = (probs * (d_probs - row_delta[..., None])).astype(jnp.bfloat16)
        d_value = jnp.einsum(
            "hqk,qhd->khd", probs.astype(jnp.bfloat16), d_heads, preferred_element_type=jnp.float32
        )
        d_key = (
            jnp.einsum("hqk,qhd->khd", d_scores, queries, preferred_element_type=jnp.float32)
            * score_scale
        )
        d_query = (
            d_query
            + jnp.einsum("hqk,khd->qhd", d_scores, key_block, preferred_element_type=jnp.float32)
            * score_scale
        )
        return (d_query, jnp.concatenate([d_key, d_value], axis=-1))

    d_query, d_pairs = lax.scan(
        backward_step, jnp.zeros((head_rows, local_heads, head_width), jnp.float32), pair_blocks
    )
    return d_query, d_pairs.reshape(key_rows, local_heads, 2 * head_width)


def shards(tokens, w_qkv, w_attn_out, w_in, w_mlp_out, gain_one, gain_two, cotangent):
    seq_tokens = tokens[0]
    seq_cot = cotangent[0]
    tok_rows, model_width = seq_tokens.shape
    seq_count = lax.axis_size("seq")
    wt_count = lax.axis_size("wt")
    seq_place = lax.axis_index("seq")
    wt_place = lax.axis_index("wt")
    half_place = wt_place % 2
    slice_len = tok_rows * seq_count
    local_heads = H // seq_count
    local_width = 3 * model_width // seq_count
    own_rows = w_qkv.shape[0]
    hidden_units = w_mlp_out.shape[1]
    score_scale = 1.0 / math.sqrt(HD)
    order = ring_order(seq_count)
    where_in_ring = [order.index(s) for s in range(seq_count)]
    ring_place = jnp.array(where_in_ring, jnp.int32)[seq_place]
    ahead_places = [
        jnp.array(order, jnp.int32)[(ring_place + k) % seq_count] for k in range(seq_count)
    ]

    token_blocks = ring_gather(seq_tokens)
    gain_own = gain_one.astype(jnp.float32)[:, None]
    scaled_qkv = (gain_own * w_qkv.astype(jnp.float32)).astype(half_type)
    qkv_pieces = lax.all_to_all(
        scaled_qkv.reshape(own_rows, seq_count, local_width).transpose(1, 0, 2),
        "seq",
        split_axis=0,
        concat_axis=0,
        tiled=True,
    )
    qkv_heads = cube_gather(qkv_pieces).transpose(1, 0, 2, 3).reshape(model_width, local_width)
    out_heads = cube_gather(w_attn_out).reshape(wt_count * own_rows, model_width)
    gain_rows = cube_gather(gain_two.reshape(1, own_rows)).reshape(wt_count * own_rows)
    gain_rows = gain_rows.astype(jnp.float32)

    half_tokens = jnp.concatenate(token_blocks, axis=0)
    unit_half, _ = normalize(half_tokens.astype(jnp.float32))
    unit_half = unit_half.astype(half_type)
    packed = dot_on(unit_half, qkv_heads, 1, 0).reshape(slice_len, local_heads, 3 * HD)
    positions = jnp.concatenate(
        [half_place * slice_len + place * tok_rows + jnp.arange(tok_rows) for place in ahead_places]
    ).astype(jnp.float32)
    cosine, sine_table = rotary_tables(positions, HD)
    queries = rotate(packed[..., :HD], cosine, sine_table).astype(half_type)
    own_pairs = jnp.concatenate(
        [rotate(packed[..., HD : 2 * HD], cosine, sine_table), packed[..., 2 * HD :]], axis=-1
    ).astype(half_type)
    pairs = jnp.concatenate([own_pairs, from_partner(own_pairs, "wt", 0)], axis=0)

    scaled_in = gain_rows[:, None, None] * w_in.astype(jnp.float32)
    mixed = jnp.concatenate(
        [
            scaled_in[:, 0].astype(half_type).T,
            scaled_in[:, 1].astype(half_type).T,
            w_mlp_out.T,
        ],
        axis=0,
    )
    mixed, group_cot, pairs = lax.optimization_barrier((mixed, seq_cot, pairs))
    mixed_full = jnp.zeros((3 * hidden_units, model_width), half_type)
    for place, block in zip(ahead_places, ring_gather(mixed)):
        mixed_full = lax.dynamic_update_slice(mixed_full, block, (0, place * w_in.shape[0]))
    group_cot = group_gather(group_cot)

    attended_raw, log_total = attention_forward(queries, pairs, score_scale)
    attended = attended_raw.astype(half_type).reshape(slice_len, local_heads * HD)
    branch = dot_on(attended, out_heads, 1, 0)
    inputs = seq_tokens.astype(jnp.float32)
    middle = inputs + ring_sum(
        [branch[k * tok_rows : (k + 1) * tok_rows] for k in range(seq_count)]
    )
    unit_two, scale_two = normalize(middle)
    group_unit = group_gather(unit_two.astype(half_type))

    in_rows, out_rows = mixed_full[: 2 * hidden_units], mixed_full[2 * hidden_units :]
    projected = dot_on(in_rows, group_unit, 1, 1)
    activated, gelu_pull = jax.vjp(exact_gelu, projected[:hidden_units])
    gate = projected[hidden_units:]
    hidden = (activated * gate).astype(half_type)
    d_hidden = dot_on(out_rows, group_cot, 1, 1)
    d_projected = jnp.concatenate(
        [gelu_pull(d_hidden * gate)[0], d_hidden * activated], axis=0
    ).astype(half_type)
    d_unit_two = group_sum(dot_on(d_projected, in_rows, 0, 0))
    output = (middle + group_sum(dot_on(hidden, out_rows, 0, 0))).astype(half_type)
    d_middle = seq_cot.astype(jnp.float32) + normalize_back(d_unit_two, unit_two, scale_two)

    d_branch = jnp.concatenate(ring_gather(d_middle.astype(half_type)), axis=0)
    d_heads = dot_on(d_branch, out_heads, 1, 1).astype(half_type)
    grad_out = dot_on(attended, d_branch, 0, 0)

    grad_mixed = jnp.concatenate(
        [dot_on(d_projected, group_unit, 1, 0), dot_on(hidden, group_cot, 1, 0)], axis=0
    ).astype(half_type)
    grad_mixed, d_heads = lax.optimization_barrier((grad_mixed, d_heads))
    feed_rows = w_in.shape[0]
    mixed_owned = ring_sum(
        [
            lax.dynamic_slice(
                grad_mixed, (0, place * feed_rows), (3 * hidden_units, feed_rows)
            )
            for place in ahead_places
        ]
    )
    in_unscaled = jnp.stack(
        [mixed_owned[:hidden_units].T, mixed_owned[hidden_units : 2 * hidden_units].T], axis=1
    )
    in_owned = in_unscaled * gain_rows[:, None, None]
    mlp_owned = mixed_owned[2 * hidden_units :].T
    gain_two_part = jnp.sum(in_unscaled * w_in.astype(jnp.float32), axis=(1, 2))
    attn_owned = cube_sum(grad_out.reshape(wt_count, own_rows, model_width))

    d_query, d_pairs = attention_backward(
        queries, pairs, attended_raw, log_total, d_heads.reshape(queries.shape), score_scale
    )
    d_own = d_pairs[:slice_len] + from_partner(
        d_pairs[slice_len:].astype(half_type), "wt", 0
    ).astype(jnp.float32)
    d_packed = (
        jnp.concatenate(
            [
                rotate(d_query, cosine, -sine_table),
                rotate(d_own[..., :HD], cosine, -sine_table),
                d_own[..., HD:],
            ],
            axis=-1,
        )
        .astype(half_type)
        .reshape(slice_len, local_width)
    )
    d_unit_parts = dot_on(d_packed, qkv_heads, 1, 1)
    d_unit = ring_sum(
        [d_unit_parts[k * tok_rows : (k + 1) * tok_rows] for k in range(seq_count)]
    )
    unit_one, scale_one = normalize(inputs)
    input_grad = (d_middle + normalize_back(d_unit, unit_one, scale_one)).astype(half_type)

    grad_heads = dot_on(unit_half, d_packed, 0, 0).reshape(
        seq_count, wt_count, own_rows, local_width
    )
    grad_pieces = cube_sum(grad_heads.transpose(1, 0, 2, 3)).astype(half_type)
    grad_rows = lax.all_to_all(
        grad_pieces, "seq", split_axis=0, concat_axis=0, tiled=True
    ).transpose(1, 0, 2)
    qkv_unscaled = grad_rows.reshape(own_rows, 3 * model_width).astype(jnp.float32)
    qkv_owned = qkv_unscaled * gain_own
    gain_one_owned = jnp.sum(qkv_unscaled * w_qkv.astype(jnp.float32), axis=1)
    gain_two_owned = cube_sum(gain_two_part.reshape(wt_count, 1, own_rows)).reshape(own_rows)
    return (
        output.reshape(1, tok_rows, model_width),
        input_grad.reshape(1, tok_rows, model_width),
        qkv_owned,
        attn_owned,
        in_owned,
        mlp_owned,
        gain_one_owned,
        gain_two_owned,
    )


def solution(mesh):
    in_specs = (
        P("wt", "seq", None),
        P(("seq", "wt"), None),
        P(("seq", "wt"), None),
        P("seq", None, "wt"),
        P("seq", "wt"),
        P(("seq", "wt")),
        P(("seq", "wt")),
        P("wt", "seq", None),
    )
    out_specs = (
        P("wt", "seq", None),
        P("wt", "seq", None),
        P(("seq", "wt"), None),
        P(("seq", "wt"), None),
        P("seq", None, "wt"),
        P("seq", "wt"),
        P(("seq", "wt")),
        P(("seq", "wt")),
    )
    return jax.shard_map(shards, mesh=mesh, in_specs=in_specs, out_specs=out_specs, check_vma=False)
```

```python
import functools
import math

import jax
import jax.numpy as jnp
from jax import lax
from jax.experimental import pallas as pl
from jax.experimental.pallas import tpu as pltpu
from jax.sharding import PartitionSpec as P

H = 16
HD = 64


epsilon = 1e-05
rope_base = 160000.0
half_type = jnp.bfloat16


def ring_order(count):
    half = count // 2
    return [2 * p if p < half else 2 * (count - 1 - p) + 1 for p in range(count)]


def ring_pairs(count):
    order = ring_order(count)
    right = [(order[p], order[(p + 1) % count]) for p in range(count)]
    left = [(target, source) for source, target in right]
    return right, left


def cut_rows(rows):
    return rows // 32 * 16 if rows >= 32 else rows // 2


def ring_gather(block, axis="seq"):
    count = lax.axis_size(axis)
    right, left = ring_pairs(count)
    half = count // 2
    behind, ahead = [block], [block]
    for _ in range(1, half):
        behind.append(lax.ppermute(behind[-1], axis, right))
        ahead.append(lax.ppermute(ahead[-1], axis, left))
    cut = cut_rows(block.shape[0])
    far = jnp.concatenate(
        [
            lax.ppermute(behind[-1][:cut], axis, right),
            lax.ppermute(ahead[-1][cut:], axis, left),
        ],
        axis=0,
    )
    return ahead[:half] + [far] + [behind[count - k] for k in range(half + 1, count)]


def ring_sum(parts, axis="seq"):
    count = lax.axis_size(axis)
    right, left = ring_pairs(count)
    half = count // 2
    cut = cut_rows(parts[0].shape[0])
    top = lax.ppermute(parts[half][:cut].astype(half_type), axis, right)
    bottom = lax.ppermute(parts[half][cut:].astype(half_type), axis, left)
    for off in range(half - 1, 0, -1):
        up = parts[off].astype(jnp.float32)
        down = parts[count - off].astype(jnp.float32)
        if off == half - 1:
            up = jnp.concatenate([up[:cut] + top.astype(jnp.float32), up[cut:]], axis=0)
            down = jnp.concatenate([down[:cut], down[cut:] + bottom.astype(jnp.float32)], axis=0)
        else:
            up = up + top.astype(jnp.float32)
            down = down + bottom.astype(jnp.float32)
        top = lax.ppermute(up.astype(half_type), axis, right)
        bottom = lax.ppermute(down.astype(half_type), axis, left)
    return parts[0].astype(jnp.float32) + top.astype(jnp.float32) + bottom.astype(jnp.float32)


def from_partner(value, axis, bit):
    mask = 2**bit
    pairs = [(source, source ^ mask) for source in range(lax.axis_size(axis))]
    return lax.ppermute(value, axis, pairs)


def bits_of(axis):
    return int(math.log2(lax.axis_size(axis)))


def cube_gather(block, axis="wt"):
    place = lax.axis_index(axis)
    bits = bits_of(axis)
    value = block
    for done, bit in enumerate(range(bits - 1, -1, -1)):
        other = from_partner(value, axis, bit)
        low = (place >> bit) % 2 == 0
        value = jnp.stack([jnp.where(low, value, other), jnp.where(low, other, value)], axis=done)
    return value.reshape((2**bits,) + block.shape)


def cube_sum(value, axis="wt"):
    place = lax.axis_index(axis)
    bits = bits_of(axis)
    value = value.reshape((2,) * bits + value.shape[1:])
    for bit in range(bits):
        at = bits - 1 - bit
        mine = (place >> bit) % 2
        keep = lax.dynamic_index_in_dim(value, mine, at, keepdims=False)
        give = lax.dynamic_index_in_dim(value, 1 - mine, at, keepdims=False)
        value = keep.astype(jnp.float32) + from_partner(give.astype(half_type), axis, bit).astype(
            jnp.float32
        )
    return value


def group_gather(rows, axis="wt"):
    for bit in range(bits_of(axis) - 1, -1, -1):
        rows = jnp.concatenate([rows, from_partner(rows, axis, bit)], axis=0)
    return rows


def group_sum(rows, axis="wt"):
    for bit in range(bits_of(axis)):
        half = rows.shape[0] // 2
        got = from_partner(rows[half:].astype(half_type), axis, bit)
        rows = rows[:half].astype(jnp.float32) + got.astype(jnp.float32)
    return rows


def normalize(features):
    average = jnp.mean(features, axis=-1, keepdims=True)
    centred = features - average
    spread = jnp.mean(centred * centred, axis=-1, keepdims=True)
    scale = lax.rsqrt(spread + epsilon)
    return centred * scale, scale


def normalize_back(d_unit, unit, scale):
    return scale * (
        d_unit
        - jnp.mean(d_unit, axis=-1, keepdims=True)
        - unit * jnp.mean(d_unit * unit, axis=-1, keepdims=True)
    )


def rotary_tables(positions, head_width):
    half_width = head_width // 2
    frequency = jnp.exp(
        jnp.arange(half_width).astype(jnp.float32) * (-2.0 * math.log(rope_base) / head_width)
    )
    angles = frequency[:, None] * positions[None, :]
    return jnp.cos(angles), jnp.sin(angles)


def rotate(vectors, cosine, sine_table):
    features, count = vectors.shape
    half_width = cosine.shape[0]
    split = vectors.reshape(features // (2 * half_width), 2, half_width, count)
    first, second = split[:, 0], split[:, 1]
    return jnp.stack(
        [first * cosine - second * sine_table, second * cosine + first * sine_table], axis=1
    ).reshape(features, count)


def exact_gelu(inner):
    return jax.nn.gelu(inner, approximate=False)


def dot_on(left, right, left_dim, right_dim):
    return lax.dot_general(
        left, right, (((left_dim,), (right_dim,)), ((), ())), preferred_element_type=jnp.float32
    )


def matmul(left, right):
    return jnp.dot(left, right, preferred_element_type=jnp.float32)


def head_rows(value, head):
    blank = jnp.zeros((HD, value.shape[1]), value.dtype)
    heads = value.shape[0] // HD
    if heads == 1:
        return value
    return jnp.concatenate(
        [value[h * HD : (h + 1) * HD] if h == head else blank for h in range(heads)], axis=0
    )


def head_columns(value, head):
    if value.shape[1] == HD:
        return value
    lane = lax.broadcasted_iota(jnp.int32, value.shape, 1)
    inside = (lane >= head * HD) & (lane < (head + 1) * HD)
    return jnp.where(inside, value, jnp.zeros_like(value))


def forward_kernel(q_ref, k_ref, vt_ref, out_ref, lse_ref):
    features, count = q_ref.shape
    length = k_ref.shape[0]
    span = math.gcd(length, 512)
    for head in range(features // HD):
        rows = slice(head * HD, (head + 1) * HD)
        query = head_rows(q_ref[...], head)
        top = total = accum = None
        for start in range(0, length, span):
            scores = matmul(k_ref[start : start + span, :], query)
            block_top = jnp.max(scores, axis=0, keepdims=True)
            new_top = block_top if top is None else jnp.maximum(top, block_top)
            raised = jnp.exp(scores - new_top)
            weight = jnp.sum(raised, axis=0, keepdims=True)
            part = matmul(vt_ref[rows, start : start + span], raised.astype(half_type))
            if top is None:
                total, accum = weight, part
            else:
                shrink = jnp.exp(top - new_top)
                total = total * shrink + weight
                accum = accum * shrink + part
            top = new_top
        out_ref[rows, :] = accum / total
        lse_ref[head : head + 1, :] = top + jnp.log(total)


def backward_kernel(first, *refs):
    q_ref, qn_ref, do_ref, don_ref, out_ref, lse_ref, k_ref, kt_ref, v_ref = refs[:9]
    dk_in, dv_in = (None, None) if first else refs[9:11]
    dq_ref, dk_ref, dv_ref = refs[-3:]
    features, count = q_ref.shape
    length = k_ref.shape[0]
    span = math.gcd(length, 512)
    heads = features // HD
    queries = [head_rows(q_ref[...], h) for h in range(heads)]
    d_outs = [head_rows(do_ref[...], h) for h in range(heads)]
    query_columns = [head_columns(qn_ref[...], h) for h in range(heads)]
    d_out_columns = [head_columns(don_ref[...], h) for h in range(heads)]
    weighed = do_ref[...].astype(jnp.float32) * out_ref[...]
    deltas = [
        jnp.sum(weighed[h * HD : (h + 1) * HD], axis=0, keepdims=True) for h in range(heads)
    ]
    d_query = [None] * heads
    for start in range(0, length, span):
        stop = start + span
        d_key = None if first else dk_in[start:stop, :]
        d_value = None if first else dv_in[start:stop, :]
        for h in range(heads):
            scores = matmul(k_ref[start:stop, :], queries[h])
            probs = jnp.exp(scores - lse_ref[h : h + 1, :])
            d_probs = matmul(v_ref[start:stop, :], d_outs[h])
            d_scores = (probs * (d_probs - deltas[h])).astype(half_type)
            value_part = matmul(probs.astype(half_type), d_out_columns[h])
            key_part = matmul(d_scores, query_columns[h])
            d_value = value_part if d_value is None else d_value + value_part
            d_key = key_part if d_key is None else d_key + key_part
            part = matmul(kt_ref[h * HD : (h + 1) * HD, start:stop], d_scores)
            d_query[h] = part if d_query[h] is None else d_query[h] + part
        dk_ref[start:stop, :] = d_key
        dv_ref[start:stop, :] = d_value
    for h in range(heads):
        dq_ref[h * HD : (h + 1) * HD, :] = d_query[h] * (1.0 / math.sqrt(HD))


kernel_params = pltpu.CompilerParams(vmem_limit_bytes=48 * 2**20)


def attention_forward(queries, keys, values_t):
    features, count = queries.shape
    length = keys.shape[0]
    heads = features // HD
    return pl.pallas_call(
        forward_kernel,
        out_shape=(
            jax.ShapeDtypeStruct((features, count), jnp.float32),
            jax.ShapeDtypeStruct((heads, count), jnp.float32),
        ),
        compiler_params=kernel_params,
        cost_estimate=pl.CostEstimate(
            flops=16 * features * count * length,
            bytes_accessed=4 * features * length + 6 * features * count,
            transcendentals=heads * count * length,
        ),
    )(queries, keys, values_t)


def attention_backward(queries, query_rows, d_out, d_out_rows, out, lse, keys, keys_t, values, sums):
    features, count = queries.shape
    length = keys.shape[0]
    heads = features // HD
    first = sums is None
    total = jax.ShapeDtypeStruct((length, features), jnp.float32)
    return pl.pallas_call(
        functools.partial(backward_kernel, first),
        out_shape=(jax.ShapeDtypeStruct((features, count), jnp.float32), total, total),
        input_output_aliases={} if first else {9: 1, 10: 2},
        compiler_params=kernel_params,
        cost_estimate=pl.CostEstimate(
            flops=40 * features * count * length,
            bytes_accessed=22 * features * length,
            transcendentals=heads * count * length,
        ),
    )(
        queries, query_rows, d_out, d_out_rows, out, lse, keys, keys_t, values, *(sums or ())
    )


def shards(tokens, w_qkv, w_attn_out, w_in, w_mlp_out, gain_one, gain_two, cotangent):
    seq_tokens = tokens[0]
    seq_cot = cotangent[0]
    tok_rows, model_width = seq_tokens.shape
    seq_count = lax.axis_size("seq")
    wt_count = lax.axis_size("wt")
    seq_place = lax.axis_index("seq")
    wt_place = lax.axis_index("wt")
    half_place = wt_place % 2
    slice_len = tok_rows * seq_count
    local_heads = H // seq_count
    local_width = 3 * model_width // seq_count
    own_rows = w_qkv.shape[0]
    hidden_units = w_mlp_out.shape[1]
    score_scale = 1.0 / math.sqrt(HD)
    half_ring = seq_count // 2
    along, side = seq_place // 2, seq_place % 2
    ring_place = jnp.where(side == 0, along, seq_count - 1 - along)

    def ahead(k):
        at = (ring_place + k) % seq_count
        return jnp.where(at < half_ring, 2 * at, 2 * (seq_count - 1 - at) + 1)

    arrival = [0]
    for k in range(1, half_ring):
        arrival += [k, seq_count - k]
    arrival.append(half_ring)
    chunks = [tuple(arrival[c : c + 2]) for c in range(0, seq_count, 2)]
    span = 2 * tok_rows

    token_blocks = ring_gather(seq_tokens)
    gain_own = gain_one.astype(jnp.float32)[:, None]
    scaled_qkv = (gain_own * w_qkv.astype(jnp.float32)).astype(half_type)
    qkv_pieces = lax.all_to_all(
        scaled_qkv.reshape(own_rows, seq_count, local_heads, 3, HD)
        .transpose(1, 0, 3, 2, 4)
        .reshape(seq_count, own_rows, local_width),
        "seq",
        split_axis=0,
        concat_axis=0,
        tiled=True,
    )
    qkv_heads = cube_gather(qkv_pieces).transpose(1, 0, 2, 3).reshape(model_width, local_width)
    out_heads = cube_gather(w_attn_out).reshape(wt_count * own_rows, model_width)
    gain_rows = cube_gather(gain_two.reshape(1, own_rows)).reshape(wt_count * own_rows)
    gain_rows = gain_rows.astype(jnp.float32)

    scaled_in = gain_rows[:, None, None] * w_in.astype(jnp.float32)
    mixed = jnp.concatenate(
        [
            scaled_in[:, 0].astype(half_type).T,
            scaled_in[:, 1].astype(half_type).T,
            w_mlp_out.T,
        ],
        axis=0,
    )
    feed_rows = w_in.shape[0]
    mixed_full = (
        lax.all_gather(mixed, "seq", axis=0)
        .transpose(1, 0, 2)
        .reshape(3 * hidden_units, model_width)
    )
    group_cot = group_gather(seq_cot)

    half_tokens = jnp.concatenate([token_blocks[k] for k in arrival], axis=0)
    unit_half, _ = normalize(half_tokens.astype(jnp.float32))
    unit_half = unit_half.astype(half_type)
    packed = dot_on(qkv_heads, unit_half, 0, 1)
    positions = jnp.concatenate(
        [half_place * slice_len + ahead(k) * tok_rows + jnp.arange(tok_rows) for k in arrival]
    ).astype(jnp.float32)
    cosine, sine_table = rotary_tables(positions, HD)
    third = local_width // 3
    queries = (rotate(packed[:third], cosine, sine_table).astype(half_type) * score_scale).astype(
        half_type
    )
    own_pairs = jnp.concatenate(
        [rotate(packed[third : 2 * third], cosine, sine_table), packed[2 * third :]], axis=0
    ).astype(half_type)
    pairs = jnp.concatenate([own_pairs, from_partner(own_pairs, "wt", 0)], axis=1)
    keys_t, values_t = pairs[:third], pairs[third:]
    keys, values = keys_t.T, values_t.T

    attended_raw, log_totals, parts = {}, {}, {}
    for c in range(len(chunks) - 1, -1, -1):
        attended_raw[c], log_totals[c] = attention_forward(
            queries[:, c * span : (c + 1) * span], keys, values_t
        )
        branch = dot_on(attended_raw[c].astype(half_type), out_heads, 0, 0)
        for at, k in enumerate(chunks[c]):
            parts[k] = branch[at * tok_rows : (at + 1) * tok_rows]
    inputs = seq_tokens.astype(jnp.float32)
    middle = inputs + ring_sum([parts[k] for k in range(seq_count)])
    unit_two, scale_two = normalize(middle)
    group_unit = group_gather(unit_two.astype(half_type))

    in_rows, out_rows = mixed_full[: 2 * hidden_units], mixed_full[2 * hidden_units :]
    projected = dot_on(in_rows, group_unit, 1, 1)
    activated, gelu_pull = jax.vjp(exact_gelu, projected[:hidden_units])
    gate = projected[hidden_units:]
    hidden = (activated * gate).astype(half_type)
    d_hidden = dot_on(out_rows, group_cot, 1, 1)
    d_projected = jnp.concatenate(
        [gelu_pull(d_hidden * gate)[0], d_hidden * activated], axis=0
    ).astype(half_type)
    d_unit_two = group_sum(dot_on(d_projected, in_rows, 0, 0))
    output = (middle + group_sum(dot_on(hidden, out_rows, 0, 0))).astype(half_type)
    d_middle = seq_cot.astype(jnp.float32) + normalize_back(d_unit_two, unit_two, scale_two)

    d_blocks = ring_gather(d_middle.astype(half_type))
    query_rows = queries.T
    d_queries, sums = [], None
    for c, chunk in enumerate(chunks):
        d_branch = jnp.concatenate([d_blocks[k] for k in chunk], axis=0)
        d_out = dot_on(out_heads, d_branch, 1, 1).astype(half_type)
        d_query, *sums = attention_backward(
            queries[:, c * span : (c + 1) * span],
            query_rows[c * span : (c + 1) * span],
            d_out,
            d_out.T,
            attended_raw[c],
            log_totals[c],
            keys,
            keys_t,
            values,
            sums,
        )
        d_queries.append(d_query)
    d_query = jnp.concatenate(d_queries, axis=1)
    d_branch = jnp.concatenate([d_blocks[k] for k in arrival], axis=0)
    attended = jnp.concatenate(
        [attended_raw[c].astype(half_type) for c in range(len(chunks))], axis=1
    )
    grad_out = dot_on(attended, d_branch, 1, 0)

    grad_mixed = jnp.concatenate(
        [dot_on(d_projected, group_unit, 1, 0), dot_on(hidden, group_cot, 1, 0)], axis=0
    ).astype(half_type)
    mixed_owned = ring_sum(
        [
            lax.dynamic_slice(
                grad_mixed, (0, ahead(k) * feed_rows), (3 * hidden_units, feed_rows)
            )
            for k in range(seq_count)
        ]
    )
    in_unscaled = jnp.stack(
        [mixed_owned[:hidden_units].T, mixed_owned[hidden_units : 2 * hidden_units].T], axis=1
    )
    in_owned = in_unscaled * gain_rows[:, None, None]
    mlp_owned = mixed_owned[2 * hidden_units :].T
    gain_two_part = jnp.sum(in_unscaled * w_in.astype(jnp.float32), axis=(1, 2))
    attn_owned = cube_sum(grad_out.reshape(wt_count, own_rows, model_width))

    d_pairs = jnp.concatenate(sums, axis=1).T
    d_own = d_pairs[:, :slice_len] + from_partner(
        d_pairs[:, slice_len:].astype(half_type), "wt", 0
    ).astype(jnp.float32)
    d_packed = jnp.concatenate(
        [
            rotate(d_query, cosine, -sine_table),
            rotate(d_own[:third], cosine, -sine_table),
            d_own[third:],
        ],
        axis=0,
    ).astype(half_type)
    d_unit_parts = dot_on(d_packed, qkv_heads, 0, 1)
    d_unit = ring_sum(
        [
            d_unit_parts[at * tok_rows : (at + 1) * tok_rows]
            for at in (arrival.index(k) for k in range(seq_count))
        ]
    )
    unit_one, scale_one = normalize(inputs)
    input_grad = (d_middle + normalize_back(d_unit, unit_one, scale_one)).astype(half_type)

    grad_heads = dot_on(unit_half, d_packed, 0, 1).reshape(
        seq_count, wt_count, own_rows, local_width
    )
    grad_pieces = cube_sum(grad_heads.transpose(1, 0, 2, 3)).astype(half_type)
    grad_rows = lax.all_to_all(
        grad_pieces, "seq", split_axis=0, concat_axis=0, tiled=True
    )
    qkv_unscaled = (
        grad_rows.reshape(seq_count, own_rows, 3, local_heads, HD)
        .transpose(1, 0, 3, 2, 4)
        .reshape(own_rows, 3 * model_width)
        .astype(jnp.float32)
    )
    qkv_owned = qkv_unscaled * gain_own
    gain_one_owned = jnp.sum(qkv_unscaled * w_qkv.astype(jnp.float32), axis=1)
    gain_two_owned = cube_sum(gain_two_part.reshape(wt_count, 1, own_rows)).reshape(own_rows)
    return (
        output.reshape(1, tok_rows, model_width),
        input_grad.reshape(1, tok_rows, model_width),
        qkv_owned,
        attn_owned,
        in_owned,
        mlp_owned,
        gain_one_owned,
        gain_two_owned,
    )


def solution(mesh):
    in_specs = (
        P("wt", "seq", None),
        P(("seq", "wt"), None),
        P(("seq", "wt"), None),
        P("seq", None, "wt"),
        P("seq", "wt"),
        P(("seq", "wt")),
        P(("seq", "wt")),
        P("wt", "seq", None),
    )
    out_specs = (
        P("wt", "seq", None),
        P("wt", "seq", None),
        P(("seq", "wt"), None),
        P(("seq", "wt"), None),
        P("seq", None, "wt"),
        P("seq", "wt"),
        P(("seq", "wt")),
        P(("seq", "wt")),
    )
    return jax.shard_map(shards, mesh=mesh, in_specs=in_specs, out_specs=out_specs, check_vma=False)
```

```python
import functools
import math

import jax
import jax.numpy as jnp
from jax import lax
from jax.experimental import pallas as pl
from jax.experimental.pallas import tpu as pltpu
from jax.sharding import PartitionSpec as P

H = 16
HD = 64


epsilon = 1e-05
rope_base = 160000.0
half_type = jnp.bfloat16


def ring_order(count):
    half = count // 2
    return [2 * p if p < half else 2 * (count - 1 - p) + 1 for p in range(count)]


def ring_pairs(count):
    order = ring_order(count)
    right = [(order[p], order[(p + 1) % count]) for p in range(count)]
    left = [(target, source) for source, target in right]
    return right, left


def cut_rows(rows):
    return rows // 32 * 16 if rows >= 32 else rows // 2


def ring_gather(block, held=(), axis="seq"):
    count = lax.axis_size(axis)
    right, left = ring_pairs(count)
    half = count // 2
    behind, ahead = [block], [block]
    for step in range(1, half):
        behind.append(lax.ppermute(behind[-1], axis, right))
        ahead.append(lax.ppermute(ahead[-1], axis, left))
        if step == 1 and held:
            behind[1], ahead[1], held = lax.optimization_barrier((behind[1], ahead[1], held))
    cut = cut_rows(block.shape[0])
    far = jnp.concatenate(
        [
            lax.ppermute(behind[-1][:cut], axis, right),
            lax.ppermute(ahead[-1][cut:], axis, left),
        ],
        axis=0,
    )
    blocks = ahead[:half] + [far] + [behind[count - k] for k in range(half + 1, count)]
    return (blocks, held) if held else blocks


def ring_sum(parts, held=(), axis="seq"):
    count = lax.axis_size(axis)
    right, left = ring_pairs(count)
    half = count // 2
    cut = cut_rows(parts[0].shape[0])
    top = lax.ppermute(parts[half][:cut].astype(half_type), axis, right)
    bottom = lax.ppermute(parts[half][cut:].astype(half_type), axis, left)
    for off in range(half - 1, 0, -1):
        up = parts[off].astype(jnp.float32)
        down = parts[count - off].astype(jnp.float32)
        if off == half - 1:
            up = jnp.concatenate([up[:cut] + top.astype(jnp.float32), up[cut:]], axis=0)
            down = jnp.concatenate([down[:cut], down[cut:] + bottom.astype(jnp.float32)], axis=0)
        else:
            up = up + top.astype(jnp.float32)
            down = down + bottom.astype(jnp.float32)
        up, down = up.astype(half_type), down.astype(half_type)
        if off == 2 and held:
            up, down, held = lax.optimization_barrier((up, down, held))
        top = lax.ppermute(up, axis, right)
        bottom = lax.ppermute(down, axis, left)
    total = parts[0].astype(jnp.float32) + top.astype(jnp.float32) + bottom.astype(jnp.float32)
    return (total, held) if held else total


def from_partner(value, axis, bit):
    mask = 2**bit
    pairs = [(source, source ^ mask) for source in range(lax.axis_size(axis))]
    return lax.ppermute(value, axis, pairs)


def bits_of(axis):
    return int(math.log2(lax.axis_size(axis)))


def cube_gather(block, axis="wt"):
    place = lax.axis_index(axis)
    bits = bits_of(axis)
    value = block
    for done, bit in enumerate(range(bits - 1, -1, -1)):
        other = from_partner(value, axis, bit)
        low = (place >> bit) % 2 == 0
        value = jnp.stack([jnp.where(low, value, other), jnp.where(low, other, value)], axis=done)
    return value.reshape((2**bits,) + block.shape)


def cube_sum(value, axis="wt"):
    place = lax.axis_index(axis)
    bits = bits_of(axis)
    value = value.reshape((2,) * bits + value.shape[1:])
    for bit in range(bits):
        at = bits - 1 - bit
        mine = (place >> bit) % 2
        keep = lax.dynamic_index_in_dim(value, mine, at, keepdims=False)
        give = lax.dynamic_index_in_dim(value, 1 - mine, at, keepdims=False)
        value = keep.astype(jnp.float32) + from_partner(give.astype(half_type), axis, bit).astype(
            jnp.float32
        )
    return value


def group_gather(rows, axis="wt"):
    for bit in range(bits_of(axis) - 1, -1, -1):
        rows = jnp.concatenate([rows, from_partner(rows, axis, bit)], axis=0)
    return rows


def group_sum(rows, axis="wt"):
    for bit in range(bits_of(axis)):
        half = rows.shape[0] // 2
        got = from_partner(rows[half:].astype(half_type), axis, bit)
        rows = rows[:half].astype(jnp.float32) + got.astype(jnp.float32)
    return rows


def normalize(features):
    average = jnp.mean(features, axis=-1, keepdims=True)
    centred = features - average
    spread = jnp.mean(centred * centred, axis=-1, keepdims=True)
    scale = lax.rsqrt(spread + epsilon)
    return centred * scale, scale


def normalize_back(d_unit, unit, scale):
    return scale * (
        d_unit
        - jnp.mean(d_unit, axis=-1, keepdims=True)
        - unit * jnp.mean(d_unit * unit, axis=-1, keepdims=True)
    )


def rotary_tables(positions, head_width):
    half_width = head_width // 2
    frequency = jnp.exp(
        jnp.arange(half_width).astype(jnp.float32) * (-2.0 * math.log(rope_base) / head_width)
    )
    angles = frequency[:, None] * positions[None, :]
    return jnp.cos(angles), jnp.sin(angles)


def rotate(vectors, cosine, sine_table):
    features, count = vectors.shape
    half_width = cosine.shape[0]
    split = vectors.reshape(features // (2 * half_width), 2, half_width, count)
    first, second = split[:, 0], split[:, 1]
    return jnp.stack(
        [first * cosine - second * sine_table, second * cosine + first * sine_table], axis=1
    ).reshape(features, count)


def exact_gelu(inner):
    return jax.nn.gelu(inner, approximate=False)


def dot_on(left, right, left_dim, right_dim):
    return lax.dot_general(
        left, right, (((left_dim,), (right_dim,)), ((), ())), preferred_element_type=jnp.float32
    )


def matmul(left, right):
    return jnp.dot(left, right, preferred_element_type=jnp.float32)


def head_rows(value, head):
    blank = jnp.zeros((HD, value.shape[1]), value.dtype)
    heads = value.shape[0] // HD
    if heads == 1:
        return value
    return jnp.concatenate(
        [value[h * HD : (h + 1) * HD] if h == head else blank for h in range(heads)], axis=0
    )


def head_columns(value, head):
    if value.shape[1] == HD:
        return value
    lane = lax.broadcasted_iota(jnp.int32, value.shape, 1)
    inside = (lane >= head * HD) & (lane < (head + 1) * HD)
    return jnp.where(inside, value, jnp.zeros_like(value))


def forward_kernel(at, q_ref, k_ref, vt_ref, w_ref, out_ref, lse_ref, branch_ref):
    features = w_ref.shape[0]
    count = out_ref.shape[1]
    length = k_ref.shape[0]
    span = math.gcd(length, 512)
    queries = q_ref[:, at : at + count]
    for head in range(features // HD):
        rows = slice(head * HD, (head + 1) * HD)
        query = head_rows(queries, head)
        top = total = accum = None
        for start in range(0, length, span):
            scores = matmul(k_ref[start : start + span, :], query)
            block_top = jnp.max(scores, axis=0, keepdims=True)
            new_top = block_top if top is None else jnp.maximum(top, block_top)
            raised = jnp.exp(scores - new_top)
            weight = jnp.sum(raised, axis=0, keepdims=True)
            part = matmul(vt_ref[rows, start : start + span], raised.astype(half_type))
            if top is None:
                total, accum = weight, part
            else:
                shrink = jnp.exp(top - new_top)
                total = total * shrink + weight
                accum = accum * shrink + part
            top = new_top
        out_ref[rows, :] = accum / total
        lse_ref[head : head + 1, :] = top + jnp.log(total)
    branch_ref[...] = dot_on(out_ref[...].astype(half_type), w_ref[...], 0, 0)


def backward_kernel(first, at, *refs):
    q_ref, qn_ref, near_ref, far_ref, w_ref, out_ref, lse_ref, k_ref, kt_ref, v_ref = refs[:10]
    dk_in, dv_in, gw_in = (None, None, None) if first else refs[10:13]
    dq_ref, dk_ref, dv_ref, gw_ref = refs[-4:]
    features, count = out_ref.shape
    length = k_ref.shape[0]
    span = math.gcd(length, 512)
    heads = features // HD
    weights = w_ref[...]
    blocks = [near_ref[...], far_ref[...]]
    d_out = jnp.concatenate([dot_on(weights, d, 1, 1) for d in blocks], axis=1).astype(half_type)
    d_out_rows = jnp.concatenate([dot_on(d, weights, 1, 1) for d in blocks], axis=0).astype(
        half_type
    )
    attended = out_ref[...].astype(half_type)
    rows = count // 2
    grad = matmul(attended[:, :rows], blocks[0]) + matmul(attended[:, rows:], blocks[1])
    gw_ref[...] = grad if first else gw_in[...] + grad
    queries = [head_rows(q_ref[:, at : at + count], h) for h in range(heads)]
    d_outs = [head_rows(d_out, h) for h in range(heads)]
    query_columns = [head_columns(qn_ref[at : at + count, :], h) for h in range(heads)]
    d_out_columns = [head_columns(d_out_rows, h) for h in range(heads)]
    weighed = d_out.astype(jnp.float32) * out_ref[...]
    deltas = [
        jnp.sum(weighed[h * HD : (h + 1) * HD], axis=0, keepdims=True) for h in range(heads)
    ]
    d_query = [None] * heads
    for start in range(0, length, span):
        stop = start + span
        d_key = None if first else dk_in[start:stop, :]
        d_value = None if first else dv_in[start:stop, :]
        for h in range(heads):
            scores = matmul(k_ref[start:stop, :], queries[h])
            probs = jnp.exp(scores - lse_ref[h : h + 1, :])
            d_probs = matmul(v_ref[start:stop, :], d_outs[h])
            d_scores = (probs * (d_probs - deltas[h])).astype(half_type)
            value_part = matmul(probs.astype(half_type), d_out_columns[h])
            key_part = matmul(d_scores, query_columns[h])
            d_value = value_part if d_value is None else d_value + value_part
            d_key = key_part if d_key is None else d_key + key_part
            part = matmul(kt_ref[h * HD : (h + 1) * HD, start:stop], d_scores)
            d_query[h] = part if d_query[h] is None else d_query[h] + part
        dk_ref[start:stop, :] = d_key
        dv_ref[start:stop, :] = d_value
    for h in range(heads):
        dq_ref[h * HD : (h + 1) * HD, :] = d_query[h] * (1.0 / math.sqrt(HD))


kernel_params = pltpu.CompilerParams(vmem_limit_bytes=20 * 2**20)


def attention_forward(at, count, queries, keys, values_t, weights):
    features = queries.shape[0]
    length = keys.shape[0]
    heads = features // HD
    return pl.pallas_call(
        functools.partial(forward_kernel, at),
        out_shape=(
            jax.ShapeDtypeStruct((features, count), jnp.float32),
            jax.ShapeDtypeStruct((heads, count), jnp.float32),
            jax.ShapeDtypeStruct((count, weights.shape[1]), jnp.float32),
        ),
        compiler_params=kernel_params,
        cost_estimate=pl.CostEstimate(
            flops=16 * features * count * length,
            bytes_accessed=4 * features * length + 6 * features * count,
            transcendentals=heads * count * length,
        ),
    )(queries, keys, values_t, weights)


def attention_backward(at, count, tensors, sums):
    queries, keys, weights = tensors[0], tensors[7], tensors[4]
    features = queries.shape[0]
    length = keys.shape[0]
    first = sums is None
    total = jax.ShapeDtypeStruct((length, features), jnp.float32)
    given = len(tensors)
    return pl.pallas_call(
        functools.partial(backward_kernel, first, at),
        out_shape=(
            jax.ShapeDtypeStruct((features, count), jnp.float32),
            total,
            total,
            jax.ShapeDtypeStruct(weights.shape, jnp.float32),
        ),
        input_output_aliases={} if first else {given + i: 1 + i for i in range(3)},
        compiler_params=kernel_params,
        cost_estimate=pl.CostEstimate(
            flops=40 * features * count * length,
            bytes_accessed=22 * features * length,
            transcendentals=features // HD * count * length,
        ),
    )(*tensors, *(sums or ()))


def shards(tokens, w_qkv, w_attn_out, w_in, w_mlp_out, gain_one, gain_two, cotangent):
    seq_tokens = tokens[0]
    seq_cot = cotangent[0]
    tok_rows, model_width = seq_tokens.shape
    seq_count = lax.axis_size("seq")
    wt_count = lax.axis_size("wt")
    seq_place = lax.axis_index("seq")
    wt_place = lax.axis_index("wt")
    half_place = wt_place % 2
    slice_len = tok_rows * seq_count
    local_heads = H // seq_count
    local_width = 3 * model_width // seq_count
    own_rows = w_qkv.shape[0]
    hidden_units = w_mlp_out.shape[1]
    score_scale = 1.0 / math.sqrt(HD)
    half_ring = seq_count // 2
    along, side = seq_place // 2, seq_place % 2
    ring_place = jnp.where(side == 0, along, seq_count - 1 - along)

    def ahead(k):
        at = (ring_place + k) % seq_count
        return jnp.where(at < half_ring, 2 * at, 2 * (seq_count - 1 - at) + 1)

    arrival = [0]
    for k in range(1, half_ring):
        arrival += [k, seq_count - k]
    arrival.append(half_ring)
    chunks = [tuple(arrival[c : c + 2]) for c in range(0, seq_count, 2)]
    span = 2 * tok_rows

    token_blocks, (w_attn_out, gain_two) = ring_gather(seq_tokens, (w_attn_out, gain_two))
    gain_own = gain_one.astype(jnp.float32)[:, None]
    scaled_qkv = (gain_own * w_qkv.astype(jnp.float32)).astype(half_type)
    qkv_pieces = lax.all_to_all(
        scaled_qkv.reshape(own_rows, seq_count, local_heads, 3, HD)
        .transpose(1, 0, 3, 2, 4)
        .reshape(seq_count, own_rows, local_width),
        "seq",
        split_axis=0,
        concat_axis=0,
        tiled=True,
    )
    qkv_heads = cube_gather(qkv_pieces).transpose(1, 0, 2, 3).reshape(model_width, local_width)
    out_heads = cube_gather(w_attn_out).reshape(wt_count * own_rows, model_width)
    gain_rows = cube_gather(gain_two.reshape(1, own_rows)).reshape(wt_count * own_rows)
    gain_rows = gain_rows.astype(jnp.float32)

    scaled_in = gain_rows[:, None, None] * w_in.astype(jnp.float32)
    mixed = jnp.concatenate(
        [
            scaled_in[:, 0].astype(half_type).T,
            scaled_in[:, 1].astype(half_type).T,
            w_mlp_out.T,
        ],
        axis=0,
    )
    mixed, token_blocks[half_ring] = lax.optimization_barrier((mixed, token_blocks[half_ring]))
    feed_rows = w_in.shape[0]
    in_rows = jnp.zeros((2 * hidden_units, model_width), half_type)
    out_rows = jnp.zeros((hidden_units, model_width), half_type)
    for k, block in enumerate(ring_gather(mixed)):
        at = (0, ahead(k) * feed_rows)
        in_rows = lax.dynamic_update_slice(in_rows, block[: 2 * hidden_units], at)
        out_rows = lax.dynamic_update_slice(out_rows, block[2 * hidden_units :], at)
    group_cot = group_gather(seq_cot)

    units = [
        normalize(
            jnp.concatenate([token_blocks[k] for k in chunk], axis=0).astype(jnp.float32)
        )[0].astype(half_type)
        for chunk in chunks
    ]
    packed = jnp.concatenate([dot_on(qkv_heads, unit, 0, 1) for unit in units], axis=1)
    positions = jnp.concatenate(
        [half_place * slice_len + ahead(k) * tok_rows + jnp.arange(tok_rows) for k in arrival]
    ).astype(jnp.float32)
    cosine, sine_table = rotary_tables(positions, HD)
    third = local_width // 3
    queries = (rotate(packed[:third], cosine, sine_table).astype(half_type) * score_scale).astype(
        half_type
    )
    own_pairs = jnp.concatenate(
        [rotate(packed[third : 2 * third], cosine, sine_table), packed[2 * third :]], axis=0
    ).astype(half_type)
    pairs = jnp.concatenate([own_pairs, from_partner(own_pairs, "wt", 0)], axis=1)
    keys_t, values_t = pairs[:third], pairs[third:]
    keys, values = keys_t.T, values_t.T

    attended, log_totals, parts = {}, {}, {}
    for c in range(len(chunks) - 1, -1, -1):
        attended[c], log_totals[c], branch = attention_forward(
            c * span, span, queries, keys, values_t, out_heads
        )
        for at, k in enumerate(chunks[c]):
            parts[k] = branch[at * tok_rows : (at + 1) * tok_rows]
    inputs = seq_tokens.astype(jnp.float32)
    middle = inputs + ring_sum([parts[k] for k in range(seq_count)])
    unit_two, scale_two = normalize(middle)
    group_unit = group_gather(unit_two.astype(half_type))

    projected = dot_on(in_rows, group_unit, 1, 1)
    activated, gelu_pull = jax.vjp(exact_gelu, projected[:hidden_units])
    gate = projected[hidden_units:]
    hidden = (activated * gate).astype(half_type)
    d_hidden = dot_on(out_rows, group_cot, 1, 1)
    d_projected = jnp.concatenate(
        [gelu_pull(d_hidden * gate)[0], d_hidden * activated], axis=0
    ).astype(half_type)
    d_unit_two = group_sum(dot_on(d_projected, in_rows, 0, 0))
    d_middle = seq_cot.astype(jnp.float32) + normalize_back(d_unit_two, unit_two, scale_two)
    d_branch, mlp_rows = lax.optimization_barrier(
        (d_middle.astype(half_type), dot_on(hidden, out_rows, 0, 0))
    )
    d_blocks = ring_gather(d_branch)
    output = (middle + group_sum(mlp_rows)).astype(half_type)
    query_rows = queries.T
    d_queries, sums = [], None
    for c, (near, far) in enumerate(chunks):
        d_query, *sums = attention_backward(
            c * span,
            span,
            (
                queries,
                query_rows,
                d_blocks[near],
                d_blocks[far],
                out_heads,
                attended[c],
                log_totals[c],
                keys,
                keys_t,
                values,
            ),
            sums,
        )
        d_queries.append(d_query)
    d_query = jnp.concatenate(d_queries, axis=1)
    *sums, grad_out = sums

    grad_mixed = jnp.concatenate(
        [dot_on(d_projected, group_unit, 1, 0), dot_on(hidden, group_cot, 1, 0)], axis=0
    ).astype(half_type)
    mixed_owned = ring_sum(
        [
            lax.dynamic_slice(
                grad_mixed, (0, ahead(k) * feed_rows), (3 * hidden_units, feed_rows)
            )
            for k in range(seq_count)
        ]
    )
    in_unscaled = jnp.stack(
        [mixed_owned[:hidden_units].T, mixed_owned[hidden_units : 2 * hidden_units].T], axis=1
    )
    in_owned = in_unscaled * gain_rows[:, None, None]
    mlp_owned = mixed_owned[2 * hidden_units :].T
    gain_two_part = jnp.sum(in_unscaled * w_in.astype(jnp.float32), axis=(1, 2))
    attn_owned = cube_sum(grad_out.reshape(wt_count, own_rows, model_width))

    d_pairs = jnp.concatenate(sums, axis=1).T
    d_own = d_pairs[:, :slice_len] + from_partner(
        d_pairs[:, slice_len:].astype(half_type), "wt", 0
    ).astype(jnp.float32)
    d_packed = jnp.concatenate(
        [
            rotate(d_query, cosine, -sine_table),
            rotate(d_own[:third], cosine, -sine_table),
            d_own[third:],
        ],
        axis=0,
    ).astype(half_type)
    grad_heads = dot_on(jnp.concatenate(units, axis=0), d_packed, 0, 1).reshape(
        seq_count, wt_count, own_rows, local_width
    )
    grad_pieces = cube_sum(grad_heads.transpose(1, 0, 2, 3)).astype(half_type)
    d_unit_parts = dot_on(d_packed, qkv_heads, 0, 1)
    d_unit, (grad_pieces,) = ring_sum(
        [
            d_unit_parts[at * tok_rows : (at + 1) * tok_rows]
            for at in (arrival.index(k) for k in range(seq_count))
        ],
        (grad_pieces,),
    )
    unit_one, scale_one = normalize(inputs)
    input_grad = (d_middle + normalize_back(d_unit, unit_one, scale_one)).astype(half_type)
    grad_rows = lax.all_to_all(grad_pieces, "seq", split_axis=0, concat_axis=0, tiled=True)
    qkv_unscaled = (
        grad_rows.reshape(seq_count, own_rows, 3, local_heads, HD)
        .transpose(1, 0, 3, 2, 4)
        .reshape(own_rows, 3 * model_width)
        .astype(jnp.float32)
    )
    qkv_owned = qkv_unscaled * gain_own
    gain_one_owned = jnp.sum(qkv_unscaled * w_qkv.astype(jnp.float32), axis=1)
    gain_two_owned = cube_sum(gain_two_part.reshape(wt_count, 1, own_rows)).reshape(own_rows)
    return (
        output.reshape(1, tok_rows, model_width),
        input_grad.reshape(1, tok_rows, model_width),
        qkv_owned,
        attn_owned,
        in_owned,
        mlp_owned,
        gain_one_owned,
        gain_two_owned,
    )


def solution(mesh):
    in_specs = (
        P("wt", "seq", None),
        P(("seq", "wt"), None),
        P(("seq", "wt"), None),
        P("seq", None, "wt"),
        P("seq", "wt"),
        P(("seq", "wt")),
        P(("seq", "wt")),
        P("wt", "seq", None),
    )
    out_specs = (
        P("wt", "seq", None),
        P("wt", "seq", None),
        P(("seq", "wt"), None),
        P(("seq", "wt"), None),
        P("seq", None, "wt"),
        P("seq", "wt"),
        P(("seq", "wt")),
        P(("seq", "wt")),
    )
    return jax.shard_map(shards, mesh=mesh, in_specs=in_specs, out_specs=out_specs, check_vma=False)
```

```python
import functools
import math

import jax
import jax.numpy as jnp
from jax import lax
from jax.experimental import pallas as pl
from jax.experimental.pallas import tpu as pltpu
from jax.sharding import PartitionSpec as P

H = 16
HD = 64


epsilon = 1e-05
rope_base = 160000.0
half_type = jnp.bfloat16


def ring_order(count):
    half = count // 2
    return [2 * p if p < half else 2 * (count - 1 - p) + 1 for p in range(count)]


def ring_pairs(count):
    order = ring_order(count)
    right = [(order[p], order[(p + 1) % count]) for p in range(count)]
    left = [(target, source) for source, target in right]
    return right, left


def cut_rows(rows):
    return rows // 32 * 16 if rows >= 32 else rows // 2


def ring_gather(block, held=(), axis="seq"):
    count = lax.axis_size(axis)
    right, left = ring_pairs(count)
    half = count // 2
    behind, ahead = [block], [block]
    for step in range(1, half):
        behind.append(lax.ppermute(behind[-1], axis, right))
        ahead.append(lax.ppermute(ahead[-1], axis, left))
        if step == 1 and held:
            behind[1], ahead[1], held = lax.optimization_barrier((behind[1], ahead[1], held))
    cut = cut_rows(block.shape[0])
    far = jnp.concatenate(
        [
            lax.ppermute(behind[-1][:cut], axis, right),
            lax.ppermute(ahead[-1][cut:], axis, left),
        ],
        axis=0,
    )
    blocks = ahead[:half] + [far] + [behind[count - k] for k in range(half + 1, count)]
    return (blocks, held) if held else blocks


def ring_sum(parts, held=(), axis="seq"):
    count = lax.axis_size(axis)
    right, left = ring_pairs(count)
    half = count // 2
    cut = cut_rows(parts[0].shape[0])
    top = lax.ppermute(parts[half][:cut].astype(half_type), axis, right)
    bottom = lax.ppermute(parts[half][cut:].astype(half_type), axis, left)
    for off in range(half - 1, 0, -1):
        up = parts[off].astype(jnp.float32)
        down = parts[count - off].astype(jnp.float32)
        if off == half - 1:
            up = jnp.concatenate([up[:cut] + top.astype(jnp.float32), up[cut:]], axis=0)
            down = jnp.concatenate([down[:cut], down[cut:] + bottom.astype(jnp.float32)], axis=0)
        else:
            up = up + top.astype(jnp.float32)
            down = down + bottom.astype(jnp.float32)
        up, down = up.astype(half_type), down.astype(half_type)
        if off == 2 and held:
            up, down, held = lax.optimization_barrier((up, down, held))
        top = lax.ppermute(up, axis, right)
        bottom = lax.ppermute(down, axis, left)
    total = parts[0].astype(jnp.float32) + top.astype(jnp.float32) + bottom.astype(jnp.float32)
    return (total, held) if held else total


def ring_shift(value, places, axis="seq"):
    count = lax.axis_size(axis)
    order = ring_order(count)
    pairs = [(order[p], order[(p + places) % count]) for p in range(count)]
    return lax.ppermute(value, axis, pairs)


def from_partner(value, axis, bit):
    mask = 2**bit
    pairs = [(source, source ^ mask) for source in range(lax.axis_size(axis))]
    return lax.ppermute(value, axis, pairs)


def bits_of(axis):
    return int(math.log2(lax.axis_size(axis)))


def cube_gather(block, axis="wt"):
    place = lax.axis_index(axis)
    bits = bits_of(axis)
    value = block
    for done, bit in enumerate(range(bits - 1, -1, -1)):
        other = from_partner(value, axis, bit)
        low = (place >> bit) % 2 == 0
        value = jnp.stack([jnp.where(low, value, other), jnp.where(low, other, value)], axis=done)
    return value.reshape((2**bits,) + block.shape)


def cube_sum(value, axis="wt"):
    place = lax.axis_index(axis)
    bits = bits_of(axis)
    value = value.reshape((2,) * bits + value.shape[1:])
    for bit in range(bits):
        at = bits - 1 - bit
        mine = (place >> bit) % 2
        keep = lax.dynamic_index_in_dim(value, mine, at, keepdims=False)
        give = lax.dynamic_index_in_dim(value, 1 - mine, at, keepdims=False)
        value = keep.astype(jnp.float32) + from_partner(give.astype(half_type), axis, bit).astype(
            jnp.float32
        )
    return value


def group_gather(rows, axis="wt"):
    for bit in range(bits_of(axis) - 1, -1, -1):
        rows = jnp.concatenate([rows, from_partner(rows, axis, bit)], axis=0)
    return rows


def group_sum(rows, held=(), axis="wt"):
    for bit in range(bits_of(axis)):
        half = rows.shape[0] // 2
        got = from_partner(rows[half:].astype(half_type), axis, bit)
        if bit == 0 and held:
            got, held = lax.optimization_barrier((got, held))
        rows = rows[:half].astype(jnp.float32) + got.astype(jnp.float32)
    return (rows, held) if held else rows


def normalize(features):
    average = jnp.mean(features, axis=-1, keepdims=True)
    centred = features - average
    spread = jnp.mean(centred * centred, axis=-1, keepdims=True)
    scale = lax.rsqrt(spread + epsilon)
    return centred * scale, scale


def normalize_back(d_unit, unit, scale):
    return scale * (
        d_unit
        - jnp.mean(d_unit, axis=-1, keepdims=True)
        - unit * jnp.mean(d_unit * unit, axis=-1, keepdims=True)
    )


def rotary_tables(positions, head_width):
    half_width = head_width // 2
    frequency = jnp.exp(
        jnp.arange(half_width).astype(jnp.float32) * (-2.0 * math.log(rope_base) / head_width)
    )
    angles = frequency[:, None] * positions[None, :]
    return jnp.cos(angles), jnp.sin(angles)


def rotate(vectors, cosine, sine_table):
    features, count = vectors.shape
    half_width = cosine.shape[0]
    split = vectors.reshape(features // (2 * half_width), 2, half_width, count)
    first, second = split[:, 0], split[:, 1]
    return jnp.stack(
        [first * cosine - second * sine_table, second * cosine + first * sine_table], axis=1
    ).reshape(features, count)


def exact_gelu(inner):
    return jax.nn.gelu(inner, approximate=False)


def dot_on(left, right, left_dim, right_dim):
    return lax.dot_general(
        left, right, (((left_dim,), (right_dim,)), ((), ())), preferred_element_type=jnp.float32
    )


def matmul(left, right):
    return jnp.dot(left, right, preferred_element_type=jnp.float32)


def head_rows(value, head):
    blank = jnp.zeros((HD, value.shape[1]), value.dtype)
    heads = value.shape[0] // HD
    if heads == 1:
        return value
    return jnp.concatenate(
        [value[h * HD : (h + 1) * HD] if h == head else blank for h in range(heads)], axis=0
    )


def head_columns(value, head):
    if value.shape[1] == HD:
        return value
    lane = lax.broadcasted_iota(jnp.int32, value.shape, 1)
    inside = (lane >= head * HD) & (lane < (head + 1) * HD)
    return jnp.where(inside, value, jnp.zeros_like(value))


def forward_kernel(at, q_ref, k_ref, vt_ref, out_ref, lse_ref, low_ref):
    features, count = out_ref.shape
    length = k_ref.shape[0]
    span = math.gcd(length, 512)
    queries = q_ref[:, at : at + count]
    for head in range(features // HD):
        rows = slice(head * HD, (head + 1) * HD)
        query = head_rows(queries, head)
        top = total = accum = None
        for start in range(0, length, span):
            scores = matmul(k_ref[start : start + span, :], query)
            block_top = jnp.max(scores, axis=0, keepdims=True)
            new_top = block_top if top is None else jnp.maximum(top, block_top)
            raised = jnp.exp(scores - new_top)
            weight = jnp.sum(raised, axis=0, keepdims=True)
            part = matmul(vt_ref[rows, start : start + span], raised.astype(half_type))
            if top is None:
                total, accum = weight, part
            else:
                shrink = jnp.exp(top - new_top)
                total = total * shrink + weight
                accum = accum * shrink + part
            top = new_top
        result = accum / total
        out_ref[rows, :] = result
        low_ref[rows, :] = result.astype(half_type)
        lse_ref[head : head + 1, :] = top + jnp.log(total)


def backward_kernel(first, at, *refs):
    q_ref, qn_ref, near_ref, far_ref, out_ref, lse_ref, k_ref, kt_ref, v_ref = refs[:9]
    dk_in, dv_in = (None, None) if first else refs[9:11]
    dq_ref, dk_ref, dv_ref = refs[-3:]
    features, count = out_ref.shape
    length = k_ref.shape[0]
    span = math.gcd(length, 512)
    heads = features // HD
    d_out = jnp.concatenate([near_ref[...], far_ref[...]], axis=1)
    d_out_rows = d_out.astype(jnp.float32).T.astype(half_type)
    queries = [head_rows(q_ref[:, at : at + count], h) for h in range(heads)]
    d_outs = [head_rows(d_out, h) for h in range(heads)]
    query_columns = [head_columns(qn_ref[at : at + count, :], h) for h in range(heads)]
    d_out_columns = [head_columns(d_out_rows, h) for h in range(heads)]
    weighed = d_out.astype(jnp.float32) * out_ref[...]
    deltas = [
        jnp.sum(weighed[h * HD : (h + 1) * HD], axis=0, keepdims=True) for h in range(heads)
    ]
    d_query = [None] * heads
    for start in range(0, length, span):
        stop = start + span
        d_key = None if first else dk_in[start:stop, :]
        d_value = None if first else dv_in[start:stop, :]
        for h in range(heads):
            scores = matmul(k_ref[start:stop, :], queries[h])
            probs = jnp.exp(scores - lse_ref[h : h + 1, :])
            d_probs = matmul(v_ref[start:stop, :], d_outs[h])
            d_scores = (probs * (d_probs - deltas[h])).astype(half_type)
            value_part = matmul(probs.astype(half_type), d_out_columns[h])
            key_part = matmul(d_scores, query_columns[h])
            d_value = value_part if d_value is None else d_value + value_part
            d_key = key_part if d_key is None else d_key + key_part
            part = matmul(kt_ref[h * HD : (h + 1) * HD, start:stop], d_scores)
            d_query[h] = part if d_query[h] is None else d_query[h] + part
        dk_ref[start:stop, :] = d_key
        dv_ref[start:stop, :] = d_value
    for h in range(heads):
        dq_ref[h * HD : (h + 1) * HD, :] = d_query[h] * (1.0 / math.sqrt(HD))


kernel_params = pltpu.CompilerParams(vmem_limit_bytes=20 * 2**20)


def attention_forward(at, count, queries, keys, values_t):
    features = queries.shape[0]
    length = keys.shape[0]
    heads = features // HD
    return pl.pallas_call(
        functools.partial(forward_kernel, at),
        out_shape=(
            jax.ShapeDtypeStruct((features, count), jnp.float32),
            jax.ShapeDtypeStruct((heads, count), jnp.float32),
            jax.ShapeDtypeStruct((features, count), half_type),
        ),
        compiler_params=kernel_params,
        cost_estimate=pl.CostEstimate(
            flops=16 * features * count * length,
            bytes_accessed=4 * features * length + 6 * features * count,
            transcendentals=heads * count * length,
        ),
    )(queries, keys, values_t)


def attention_backward(at, count, tensors, sums):
    queries, keys = tensors[0], tensors[6]
    features = queries.shape[0]
    length = keys.shape[0]
    first = sums is None
    total = jax.ShapeDtypeStruct((length, features), jnp.float32)
    given = len(tensors)
    return pl.pallas_call(
        functools.partial(backward_kernel, first, at),
        out_shape=(
            jax.ShapeDtypeStruct((features, count), jnp.float32),
            total,
            total,
        ),
        input_output_aliases={} if first else {given + i: 1 + i for i in range(2)},
        compiler_params=kernel_params,
        cost_estimate=pl.CostEstimate(
            flops=40 * features * count * length,
            bytes_accessed=22 * features * length,
            transcendentals=features // HD * count * length,
        ),
    )(*tensors, *(sums or ()))


def shards(tokens, w_qkv, w_attn_out, w_in, w_mlp_out, gain_one, gain_two, cotangent):
    seq_tokens = tokens[0]
    seq_cot = cotangent[0]
    tok_rows, model_width = seq_tokens.shape
    seq_count = lax.axis_size("seq")
    wt_count = lax.axis_size("wt")
    seq_place = lax.axis_index("seq")
    wt_place = lax.axis_index("wt")
    half_place = wt_place % 2
    slice_len = tok_rows * seq_count
    local_heads = H // seq_count
    local_width = 3 * model_width // seq_count
    own_rows = w_qkv.shape[0]
    hidden_units = w_mlp_out.shape[1]
    score_scale = 1.0 / math.sqrt(HD)
    half_ring = seq_count // 2
    along, side = seq_place // 2, seq_place % 2
    ring_place = jnp.where(side == 0, along, seq_count - 1 - along)

    def ahead(k):
        at = (ring_place + k) % seq_count
        return jnp.where(at < half_ring, 2 * at, 2 * (seq_count - 1 - at) + 1)

    arrival = [0]
    for k in range(1, half_ring):
        arrival += [k, seq_count - k]
    arrival.append(half_ring)
    chunks = [tuple(arrival[c : c + 2]) for c in range(0, seq_count, 2)]
    span = 2 * tok_rows

    token_blocks, (gain_two,) = ring_gather(seq_tokens, (gain_two,))
    gain_own = gain_one.astype(jnp.float32)[:, None]
    scaled_qkv = (gain_own * w_qkv.astype(jnp.float32)).astype(half_type)
    qkv_pieces = lax.all_to_all(
        scaled_qkv.reshape(own_rows, seq_count, local_heads, 3, HD)
        .transpose(1, 0, 3, 2, 4)
        .reshape(seq_count, own_rows, local_width),
        "seq",
        split_axis=0,
        concat_axis=0,
        tiled=True,
    )
    qkv_heads = cube_gather(qkv_pieces).transpose(1, 0, 2, 3).reshape(model_width, local_width)
    gain_rows = cube_gather(gain_two.reshape(1, own_rows)).reshape(wt_count * own_rows)
    gain_rows = gain_rows.astype(jnp.float32)

    scaled_in = gain_rows[:, None, None] * w_in.astype(jnp.float32)
    mixed = jnp.concatenate(
        [
            scaled_in[:, 0].astype(half_type).T,
            scaled_in[:, 1].astype(half_type).T,
            w_mlp_out.T,
        ],
        axis=0,
    )
    mixed, group_cot, w_attn_out, token_blocks[half_ring] = lax.optimization_barrier(
        (mixed, seq_cot, w_attn_out, token_blocks[half_ring])
    )
    feed_rows = w_in.shape[0]
    in_rows = jnp.zeros((2 * hidden_units, model_width), half_type)
    out_rows = jnp.zeros((hidden_units, model_width), half_type)
    for k, block in enumerate(ring_gather(mixed)):
        at = (0, ahead(k) * feed_rows)
        in_rows = lax.dynamic_update_slice(in_rows, block[: 2 * hidden_units], at)
        out_rows = lax.dynamic_update_slice(out_rows, block[2 * hidden_units :], at)
    group_cot = group_gather(group_cot)
    out_full = (
        cube_gather(jnp.stack(ring_gather(w_attn_out)))
        .transpose(1, 0, 2, 3)
        .reshape(model_width, model_width)
    )

    units = [
        normalize(
            jnp.concatenate([token_blocks[k] for k in chunk], axis=0).astype(jnp.float32)
        )[0].astype(half_type)
        for chunk in chunks
    ]
    packed = jnp.concatenate([dot_on(qkv_heads, unit, 0, 1) for unit in units], axis=1)
    positions = jnp.concatenate(
        [half_place * slice_len + ahead(k) * tok_rows + jnp.arange(tok_rows) for k in arrival]
    ).astype(jnp.float32)
    cosine, sine_table = rotary_tables(positions, HD)
    third = local_width // 3
    queries = (rotate(packed[:third], cosine, sine_table).astype(half_type) * score_scale).astype(
        half_type
    )
    own_pairs = jnp.concatenate(
        [rotate(packed[third : 2 * third], cosine, sine_table), packed[2 * third :]], axis=0
    ).astype(half_type)
    pairs = jnp.concatenate([own_pairs, from_partner(own_pairs, "wt", 0)], axis=1)
    keys_t, values_t = pairs[:third], pairs[third:]
    keys, values = keys_t.T, values_t.T

    attended, log_totals, arrived = {}, {}, [None] * seq_count
    for c in range(len(chunks) - 1, -1, -1):
        attended[c], log_totals[c], low = attention_forward(
            c * span, span, queries, keys, values_t
        )
        for at, k in enumerate(chunks[c]):
            block = low[:, at * tok_rows : (at + 1) * tok_rows]
            arrived[(seq_count - k) % seq_count] = ring_shift(block, k) if k else block
    arrived = jnp.concatenate(arrived, axis=0)
    inputs = seq_tokens.astype(jnp.float32)
    middle = inputs + dot_on(arrived, out_full, 0, 0)
    unit_two, scale_two = normalize(middle)
    group_unit = group_gather(unit_two.astype(half_type))

    projected = dot_on(in_rows, group_unit, 1, 1)
    activated, gelu_pull = jax.vjp(exact_gelu, projected[:hidden_units])
    gate = projected[hidden_units:]
    hidden = (activated * gate).astype(half_type)
    d_hidden = dot_on(out_rows, group_cot, 1, 1)
    d_projected = jnp.concatenate(
        [gelu_pull(d_hidden * gate)[0], d_hidden * activated], axis=0
    ).astype(half_type)
    d_unit_rows, d_projected, hidden = lax.optimization_barrier(
        (dot_on(d_projected, in_rows, 0, 0), d_projected, hidden)
    )
    grad_mixed = jnp.concatenate(
        [dot_on(d_projected, group_unit, 1, 0), dot_on(hidden, group_cot, 1, 0)], axis=0
    ).astype(half_type)
    d_unit_two, (grad_mixed,) = group_sum(d_unit_rows, (grad_mixed,))
    d_middle = seq_cot.astype(jnp.float32) + normalize_back(d_unit_two, unit_two, scale_two)
    d_branch = d_middle.astype(half_type)
    d_sent = dot_on(out_full, d_branch, 1, 1).astype(half_type)
    head_span = local_heads * HD
    d_blocks = [None] * seq_count
    for c in chunks:
        for k in c:
            j = (seq_count - k) % seq_count
            block = d_sent[j * head_span : (j + 1) * head_span]
            d_blocks[k] = ring_shift(block, j) if j else block
    d_blocks[0], mlp_rows = lax.optimization_barrier((d_blocks[0], dot_on(hidden, out_rows, 0, 0)))
    output = (middle + group_sum(mlp_rows)).astype(half_type)
    query_rows = queries.T
    d_queries, sums = [], None
    for c, (near, far) in enumerate(chunks):
        d_query, *sums = attention_backward(
            c * span,
            span,
            (
                queries,
                query_rows,
                d_blocks[near],
                d_blocks[far],
                attended[c],
                log_totals[c],
                keys,
                keys_t,
                values,
            ),
            sums,
        )
        if c == 0:
            d_query, d_out_branch = lax.optimization_barrier((d_query, d_branch))
        d_queries.append(d_query)
    d_query = jnp.concatenate(d_queries, axis=1)
    grad_out = dot_on(arrived, d_out_branch, 1, 0).reshape(
        seq_count, wt_count, own_rows, model_width
    )
    grad_out = cube_sum(grad_out.transpose(1, 0, 2, 3))
    attn_owned = ring_sum([grad_out[k] for k in range(seq_count)])

    mixed_owned = ring_sum(
        [
            lax.dynamic_slice(
                grad_mixed, (0, ahead(k) * feed_rows), (3 * hidden_units, feed_rows)
            )
            for k in range(seq_count)
        ]
    )
    d_pairs = jnp.concatenate(sums, axis=1).T
    d_own = d_pairs[:, :slice_len] + from_partner(
        d_pairs[:, slice_len:].astype(half_type), "wt", 0
    ).astype(jnp.float32)
    d_packed = jnp.concatenate(
        [
            rotate(d_query, cosine, -sine_table),
            rotate(d_own[:third], cosine, -sine_table),
            d_own[third:],
        ],
        axis=0,
    ).astype(half_type)
    grad_heads = dot_on(jnp.concatenate(units, axis=0), d_packed, 0, 1).reshape(
        seq_count, wt_count, own_rows, local_width
    )
    grad_pieces = cube_sum(grad_heads.transpose(1, 0, 2, 3)).astype(half_type)
    d_unit_parts = dot_on(d_packed, qkv_heads, 0, 1)
    d_unit, (grad_pieces, mixed_owned) = ring_sum(
        [
            d_unit_parts[at * tok_rows : (at + 1) * tok_rows]
            for at in (arrival.index(k) for k in range(seq_count))
        ],
        (grad_pieces, mixed_owned),
    )
    in_unscaled = jnp.stack(
        [mixed_owned[:hidden_units].T, mixed_owned[hidden_units : 2 * hidden_units].T], axis=1
    )
    in_owned = in_unscaled * gain_rows[:, None, None]
    mlp_owned = mixed_owned[2 * hidden_units :].T
    gain_two_part = jnp.sum(in_unscaled * w_in.astype(jnp.float32), axis=(1, 2))
    unit_one, scale_one = normalize(inputs)
    input_grad = (d_middle + normalize_back(d_unit, unit_one, scale_one)).astype(half_type)
    grad_rows = lax.all_to_all(grad_pieces, "seq", split_axis=0, concat_axis=0, tiled=True)
    qkv_unscaled = (
        grad_rows.reshape(seq_count, own_rows, 3, local_heads, HD)
        .transpose(1, 0, 3, 2, 4)
        .reshape(own_rows, 3 * model_width)
        .astype(jnp.float32)
    )
    qkv_owned = qkv_unscaled * gain_own
    gain_one_owned = jnp.sum(qkv_unscaled * w_qkv.astype(jnp.float32), axis=1)
    gain_two_owned = cube_sum(gain_two_part.reshape(wt_count, 1, own_rows)).reshape(own_rows)
    return (
        output.reshape(1, tok_rows, model_width),
        input_grad.reshape(1, tok_rows, model_width),
        qkv_owned,
        attn_owned,
        in_owned,
        mlp_owned,
        gain_one_owned,
        gain_two_owned,
    )


def solution(mesh):
    in_specs = (
        P("wt", "seq", None),
        P(("seq", "wt"), None),
        P(("seq", "wt"), None),
        P("seq", None, "wt"),
        P("seq", "wt"),
        P(("seq", "wt")),
        P(("seq", "wt")),
        P("wt", "seq", None),
    )
    out_specs = (
        P("wt", "seq", None),
        P("wt", "seq", None),
        P(("seq", "wt"), None),
        P(("seq", "wt"), None),
        P("seq", None, "wt"),
        P("seq", "wt"),
        P(("seq", "wt")),
        P(("seq", "wt")),
    )
    return jax.shard_map(shards, mesh=mesh, in_specs=in_specs, out_specs=out_specs, check_vma=False)
```

```python
import functools
import math

import jax
import jax.numpy as jnp
from jax import lax
from jax.experimental import pallas as pl
from jax.experimental.pallas import tpu as pltpu
from jax.sharding import PartitionSpec as P

H = 16
HD = 64


epsilon = 1e-05
rope_base = 160000.0
half_type = jnp.bfloat16


def ring_order(count):
    half = count // 2
    return [2 * p if p < half else 2 * (count - 1 - p) + 1 for p in range(count)]


def ring_pairs(count):
    order = ring_order(count)
    right = [(order[p], order[(p + 1) % count]) for p in range(count)]
    left = [(target, source) for source, target in right]
    return right, left


def cut_rows(rows):
    return rows // 32 * 16 if rows >= 32 else rows // 2


def ring_gather(block, held=(), axis="seq"):
    count = lax.axis_size(axis)
    right, left = ring_pairs(count)
    half = count // 2
    behind, ahead = [block], [block]
    for step in range(1, half):
        behind.append(lax.ppermute(behind[-1], axis, right))
        ahead.append(lax.ppermute(ahead[-1], axis, left))
        if step == 1 and held:
            behind[1], ahead[1], held = lax.optimization_barrier((behind[1], ahead[1], held))
    cut = cut_rows(block.shape[0])
    far = jnp.concatenate(
        [
            lax.ppermute(behind[-1][:cut], axis, right),
            lax.ppermute(ahead[-1][cut:], axis, left),
        ],
        axis=0,
    )
    blocks = ahead[:half] + [far] + [behind[count - k] for k in range(half + 1, count)]
    return (blocks, held) if held else blocks


def ring_sum(parts, held=(), axis="seq"):
    count = lax.axis_size(axis)
    right, left = ring_pairs(count)
    half = count // 2
    cut = cut_rows(parts[0].shape[0])
    top = lax.ppermute(parts[half][:cut].astype(half_type), axis, right)
    bottom = lax.ppermute(parts[half][cut:].astype(half_type), axis, left)
    for off in range(half - 1, 0, -1):
        up = parts[off].astype(jnp.float32)
        down = parts[count - off].astype(jnp.float32)
        if off == half - 1:
            up = jnp.concatenate([up[:cut] + top.astype(jnp.float32), up[cut:]], axis=0)
            down = jnp.concatenate([down[:cut], down[cut:] + bottom.astype(jnp.float32)], axis=0)
        else:
            up = up + top.astype(jnp.float32)
            down = down + bottom.astype(jnp.float32)
        up, down = up.astype(half_type), down.astype(half_type)
        if off == 2 and held:
            up, down, held = lax.optimization_barrier((up, down, held))
        top = lax.ppermute(up, axis, right)
        bottom = lax.ppermute(down, axis, left)
    total = parts[0].astype(jnp.float32) + top.astype(jnp.float32) + bottom.astype(jnp.float32)
    return (total, held) if held else total


def from_partner(value, axis, bit):
    mask = 2**bit
    pairs = [(source, source ^ mask) for source in range(lax.axis_size(axis))]
    return lax.ppermute(value, axis, pairs)


def bits_of(axis):
    return int(math.log2(lax.axis_size(axis)))


def cube_gather(block, axis="wt"):
    place = lax.axis_index(axis)
    bits = bits_of(axis)
    value = block
    for done, bit in enumerate(range(bits - 1, -1, -1)):
        other = from_partner(value, axis, bit)
        low = (place >> bit) % 2 == 0
        value = jnp.stack([jnp.where(low, value, other), jnp.where(low, other, value)], axis=done)
    return value.reshape((2**bits,) + block.shape)


def cube_sum(value, axis="wt"):
    place = lax.axis_index(axis)
    bits = bits_of(axis)
    value = value.reshape((2,) * bits + value.shape[1:])
    for bit in range(bits):
        at = bits - 1 - bit
        mine = (place >> bit) % 2
        keep = lax.dynamic_index_in_dim(value, mine, at, keepdims=False)
        give = lax.dynamic_index_in_dim(value, 1 - mine, at, keepdims=False)
        value = keep.astype(jnp.float32) + from_partner(give.astype(half_type), axis, bit).astype(
            jnp.float32
        )
    return value


def group_gather(rows, axis="wt"):
    for bit in range(bits_of(axis) - 1, -1, -1):
        rows = jnp.concatenate([rows, from_partner(rows, axis, bit)], axis=0)
    return rows


def group_sum(rows, held=(), axis="wt"):
    for bit in range(bits_of(axis)):
        half = rows.shape[0] // 2
        got = from_partner(rows[half:].astype(half_type), axis, bit)
        if bit == 0 and held:
            got, held = lax.optimization_barrier((got, held))
        rows = rows[:half].astype(jnp.float32) + got.astype(jnp.float32)
    return (rows, held) if held else rows


def normalize(features):
    average = jnp.mean(features, axis=-1, keepdims=True)
    centred = features - average
    spread = jnp.mean(centred * centred, axis=-1, keepdims=True)
    scale = lax.rsqrt(spread + epsilon)
    return centred * scale, scale


def normalize_back(d_unit, unit, scale):
    return scale * (
        d_unit
        - jnp.mean(d_unit, axis=-1, keepdims=True)
        - unit * jnp.mean(d_unit * unit, axis=-1, keepdims=True)
    )


def rotary_tables(positions, head_width):
    half_width = head_width // 2
    frequency = jnp.exp(
        jnp.arange(half_width).astype(jnp.float32) * (-2.0 * math.log(rope_base) / head_width)
    )
    angles = frequency[:, None] * positions[None, :]
    return jnp.cos(angles), jnp.sin(angles)


def rotate(vectors, cosine, sine_table):
    features, count = vectors.shape
    half_width = cosine.shape[0]
    split = vectors.reshape(features // (2 * half_width), 2, half_width, count)
    first, second = split[:, 0], split[:, 1]
    return jnp.stack(
        [first * cosine - second * sine_table, second * cosine + first * sine_table], axis=1
    ).reshape(features, count)


def exact_gelu(inner):
    return jax.nn.gelu(inner, approximate=False)


def dot_on(left, right, left_dim, right_dim):
    return lax.dot_general(
        left, right, (((left_dim,), (right_dim,)), ((), ())), preferred_element_type=jnp.float32
    )


def matmul(left, right):
    return jnp.dot(left, right, preferred_element_type=jnp.float32)


def head_rows(value, head):
    blank = jnp.zeros((HD, value.shape[1]), value.dtype)
    heads = value.shape[0] // HD
    if heads == 1:
        return value
    return jnp.concatenate(
        [value[h * HD : (h + 1) * HD] if h == head else blank for h in range(heads)], axis=0
    )


def head_columns(value, head):
    if value.shape[1] == HD:
        return value
    lane = lax.broadcasted_iota(jnp.int32, value.shape, 1)
    inside = (lane >= head * HD) & (lane < (head + 1) * HD)
    return jnp.where(inside, value, jnp.zeros_like(value))


def forward_kernel(at, q_ref, k_ref, vt_ref, out_ref, lse_ref, low_ref):
    features, count = out_ref.shape
    length = k_ref.shape[0]
    span = math.gcd(length, 512)
    queries = q_ref[:, at : at + count]
    for head in range(features // HD):
        rows = slice(head * HD, (head + 1) * HD)
        query = head_rows(queries, head)
        top = total = accum = None
        for start in range(0, length, span):
            scores = matmul(k_ref[start : start + span, :], query)
            block_top = jnp.max(scores, axis=0, keepdims=True)
            new_top = block_top if top is None else jnp.maximum(top, block_top)
            raised = jnp.exp(scores - new_top)
            weight = jnp.sum(raised, axis=0, keepdims=True)
            part = matmul(vt_ref[rows, start : start + span], raised.astype(half_type))
            if top is None:
                total, accum = weight, part
            else:
                shrink = jnp.exp(top - new_top)
                total = total * shrink + weight
                accum = accum * shrink + part
            top = new_top
        result = accum / total
        out_ref[rows, :] = result
        blocks, _, width = low_ref.shape
        for b in range(blocks):
            low_ref[b, rows, :] = result[:, b * width : (b + 1) * width].astype(half_type)
        lse_ref[head : head + 1, :] = top + jnp.log(total)


def backward_kernel(first, at, *refs):
    q_ref, qn_ref, do_ref, out_ref, lse_ref, k_ref, kt_ref, v_ref = refs[:8]
    dk_in, dv_in = (None, None) if first else refs[8:10]
    dq_ref, dk_ref, dv_ref = refs[-3:]
    features, count = out_ref.shape
    length = k_ref.shape[0]
    span = math.gcd(length, 512)
    heads = features // HD
    width = do_ref.shape[2]
    d_out = jnp.concatenate(
        [do_ref[b] for b in range(at // width, (at + count) // width)], axis=1
    )
    d_out_rows = d_out.astype(jnp.float32).T.astype(half_type)
    queries = [head_rows(q_ref[:, at : at + count], h) for h in range(heads)]
    d_outs = [head_rows(d_out, h) for h in range(heads)]
    query_columns = [head_columns(qn_ref[at : at + count, :], h) for h in range(heads)]
    d_out_columns = [head_columns(d_out_rows, h) for h in range(heads)]
    weighed = d_out.astype(jnp.float32) * out_ref[...]
    deltas = [
        jnp.sum(weighed[h * HD : (h + 1) * HD], axis=0, keepdims=True) for h in range(heads)
    ]
    d_query = [None] * heads
    for start in range(0, length, span):
        stop = start + span
        d_key = None if first else dk_in[start:stop, :]
        d_value = None if first else dv_in[start:stop, :]
        for h in range(heads):
            scores = matmul(k_ref[start:stop, :], queries[h])
            probs = jnp.exp(scores - lse_ref[h : h + 1, :])
            d_probs = matmul(v_ref[start:stop, :], d_outs[h])
            d_scores = (probs * (d_probs - deltas[h])).astype(half_type)
            value_part = matmul(probs.astype(half_type), d_out_columns[h])
            key_part = matmul(d_scores, query_columns[h])
            d_value = value_part if d_value is None else d_value + value_part
            d_key = key_part if d_key is None else d_key + key_part
            part = matmul(kt_ref[h * HD : (h + 1) * HD, start:stop], d_scores)
            d_query[h] = part if d_query[h] is None else d_query[h] + part
        dk_ref[start:stop, :] = d_key
        dv_ref[start:stop, :] = d_value
    for h in range(heads):
        dq_ref[h * HD : (h + 1) * HD, :] = d_query[h] * (1.0 / math.sqrt(HD))


kernel_params = pltpu.CompilerParams(vmem_limit_bytes=20 * 2**20)


def attention_forward(at, blocks, width, queries, keys, values_t):
    features = queries.shape[0]
    length = keys.shape[0]
    heads = features // HD
    count = blocks * width
    return pl.pallas_call(
        functools.partial(forward_kernel, at),
        out_shape=(
            jax.ShapeDtypeStruct((features, count), jnp.float32),
            jax.ShapeDtypeStruct((heads, count), jnp.float32),
            jax.ShapeDtypeStruct((blocks, features, width), half_type),
        ),
        compiler_params=kernel_params,
        cost_estimate=pl.CostEstimate(
            flops=16 * features * count * length,
            bytes_accessed=4 * features * length + 6 * features * count,
            transcendentals=heads * count * length,
        ),
    )(queries, keys, values_t)


def attention_backward(at, count, tensors, sums):
    queries, keys = tensors[0], tensors[5]
    features = queries.shape[0]
    length = keys.shape[0]
    first = sums is None
    total = jax.ShapeDtypeStruct((length, features), jnp.float32)
    given = len(tensors)
    return pl.pallas_call(
        functools.partial(backward_kernel, first, at),
        out_shape=(
            jax.ShapeDtypeStruct((features, count), jnp.float32),
            total,
            total,
        ),
        input_output_aliases={} if first else {given + i: 1 + i for i in range(2)},
        compiler_params=kernel_params,
        cost_estimate=pl.CostEstimate(
            flops=40 * features * count * length,
            bytes_accessed=22 * features * length,
            transcendentals=features // HD * count * length,
        ),
    )(*tensors, *(sums or ()))


def shards(tokens, w_qkv, w_attn_out, w_in, w_mlp_out, gain_one, gain_two, cotangent):
    seq_tokens = tokens[0]
    seq_cot = cotangent[0]
    tok_rows, model_width = seq_tokens.shape
    seq_count = lax.axis_size("seq")
    wt_count = lax.axis_size("wt")
    seq_place = lax.axis_index("seq")
    wt_place = lax.axis_index("wt")
    half_place = wt_place % 2
    slice_len = tok_rows * seq_count
    local_heads = H // seq_count
    local_width = 3 * model_width // seq_count
    own_rows = w_qkv.shape[0]
    hidden_units = w_mlp_out.shape[1]
    score_scale = 1.0 / math.sqrt(HD)
    half_ring = seq_count // 2
    along, side = seq_place // 2, seq_place % 2
    ring_place = jnp.where(side == 0, along, seq_count - 1 - along)

    def ahead(k):
        at = (ring_place + k) % seq_count
        return jnp.where(at < half_ring, 2 * at, 2 * (seq_count - 1 - at) + 1)

    blocks = 2
    span = blocks * tok_rows

    token_blocks, (gain_two,) = ring_gather(seq_tokens, (gain_two,))
    gain_own = gain_one.astype(jnp.float32)[:, None]
    scaled_qkv = (gain_own * w_qkv.astype(jnp.float32)).astype(half_type)
    qkv_pieces = lax.all_to_all(
        scaled_qkv.reshape(own_rows, seq_count, local_heads, 3, HD)
        .transpose(1, 0, 3, 2, 4)
        .reshape(seq_count, own_rows, local_width),
        "seq",
        split_axis=0,
        concat_axis=0,
        tiled=True,
    )
    qkv_heads = cube_gather(qkv_pieces).transpose(1, 0, 2, 3).reshape(model_width, local_width)
    gain_rows = cube_gather(gain_two.reshape(1, own_rows)).reshape(wt_count * own_rows)
    gain_rows = gain_rows.astype(jnp.float32)

    scaled_in = gain_rows[:, None, None] * w_in.astype(jnp.float32)
    mixed = jnp.concatenate(
        [
            scaled_in[:, 0].astype(half_type).T,
            scaled_in[:, 1].astype(half_type).T,
            w_mlp_out.T,
        ],
        axis=0,
    )
    mixed, group_cot, w_attn_out, token_blocks[half_ring] = lax.optimization_barrier(
        (mixed, seq_cot, w_attn_out, token_blocks[half_ring])
    )
    feed_rows = w_in.shape[0]
    in_rows = jnp.zeros((2 * hidden_units, model_width), half_type)
    out_rows = jnp.zeros((hidden_units, model_width), half_type)
    for k, block in enumerate(ring_gather(mixed)):
        at = (0, ahead(k) * feed_rows)
        in_rows = lax.dynamic_update_slice(in_rows, block[: 2 * hidden_units], at)
        out_rows = lax.dynamic_update_slice(out_rows, block[2 * hidden_units :], at)
    group_cot = group_gather(group_cot)
    out_full = (
        cube_gather(lax.all_gather(w_attn_out, "seq", axis=0))
        .transpose(1, 0, 2, 3)
        .reshape(model_width, model_width)
    )

    units = jnp.zeros((slice_len, model_width), half_type)
    for k, block in enumerate(token_blocks):
        unit = normalize(block.astype(jnp.float32))[0].astype(half_type)
        units = lax.dynamic_update_slice(units, unit, (ahead(k) * tok_rows, 0))
    packed = dot_on(qkv_heads, units, 0, 1)
    positions = (half_place * slice_len + jnp.arange(slice_len)).astype(jnp.float32)
    cosine, sine_table = rotary_tables(positions, HD)
    third = local_width // 3
    queries = (rotate(packed[:third], cosine, sine_table).astype(half_type) * score_scale).astype(
        half_type
    )
    own_pairs = jnp.concatenate(
        [rotate(packed[third : 2 * third], cosine, sine_table), packed[2 * third :]], axis=0
    ).astype(half_type)
    pairs = jnp.concatenate([own_pairs, from_partner(own_pairs, "wt", 0)], axis=1)
    pairs, group_cot = lax.optimization_barrier((pairs, group_cot))
    keys_t, values_t = pairs[:third], pairs[third:]
    keys, values = keys_t.T, values_t.T

    attended, log_totals, low = [], [], []
    for at in range(0, slice_len, span):
        results = attention_forward(at, blocks, tok_rows, queries, keys, values_t)
        for kept, result in zip((attended, log_totals, low), results):
            kept.append(result)
    arrived = lax.all_to_all(
        jnp.concatenate(low, axis=0), "seq", split_axis=0, concat_axis=0, tiled=True
    ).reshape(model_width, tok_rows)
    inputs = seq_tokens.astype(jnp.float32)
    middle = inputs + dot_on(arrived, out_full, 0, 0)
    unit_two, scale_two = normalize(middle)
    group_unit = group_gather(unit_two.astype(half_type))

    projected = dot_on(in_rows, group_unit, 1, 1)
    activated, gelu_pull = jax.vjp(exact_gelu, projected[:hidden_units])
    gate = projected[hidden_units:]
    hidden = (activated * gate).astype(half_type)
    d_hidden = dot_on(out_rows, group_cot, 1, 1)
    d_projected = jnp.concatenate(
        [gelu_pull(d_hidden * gate)[0], d_hidden * activated], axis=0
    ).astype(half_type)
    d_unit_rows, d_projected, hidden = lax.optimization_barrier(
        (dot_on(d_projected, in_rows, 0, 0), d_projected, hidden)
    )
    grad_mixed = jnp.concatenate(
        [dot_on(d_projected, group_unit, 1, 0), dot_on(hidden, group_cot, 1, 0)], axis=0
    ).astype(half_type)
    d_unit_two, (grad_mixed,) = group_sum(d_unit_rows, (grad_mixed,))
    d_middle = seq_cot.astype(jnp.float32) + normalize_back(d_unit_two, unit_two, scale_two)
    d_branch = d_middle.astype(half_type)
    d_heads = lax.all_to_all(
        dot_on(out_full, d_branch, 1, 1)
        .astype(half_type)
        .reshape(seq_count, local_heads * HD, tok_rows),
        "seq",
        split_axis=0,
        concat_axis=0,
        tiled=True,
    )
    d_heads, mlp_rows = lax.optimization_barrier((d_heads, dot_on(hidden, out_rows, 0, 0)))
    output = (middle + group_sum(mlp_rows)).astype(half_type)
    query_rows = queries.T
    d_queries, sums = [], None
    for c in range(slice_len // span):
        d_query, *sums = attention_backward(
            c * span,
            span,
            (
                queries,
                query_rows,
                d_heads,
                attended[c],
                log_totals[c],
                keys,
                keys_t,
                values,
            ),
            sums,
        )
        if c == 0:
            d_query, d_out_branch = lax.optimization_barrier((d_query, d_branch))
        d_queries.append(d_query)
    d_query = jnp.concatenate(d_queries, axis=1)
    grad_out = dot_on(arrived, d_out_branch, 1, 0).reshape(
        seq_count, wt_count, own_rows, model_width
    )
    grad_out = cube_sum(grad_out.transpose(1, 0, 2, 3))
    attn_owned = lax.psum_scatter(grad_out.astype(half_type), "seq", scatter_dimension=0).astype(
        jnp.float32
    )

    mixed_owned = ring_sum(
        [
            lax.dynamic_slice(
                grad_mixed, (0, ahead(k) * feed_rows), (3 * hidden_units, feed_rows)
            )
            for k in range(seq_count)
        ]
    )
    d_pairs = jnp.concatenate(sums, axis=1).T
    d_own = d_pairs[:, :slice_len] + from_partner(
        d_pairs[:, slice_len:].astype(half_type), "wt", 0
    ).astype(jnp.float32)
    d_packed = jnp.concatenate(
        [
            rotate(d_query, cosine, -sine_table),
            rotate(d_own[:third], cosine, -sine_table),
            d_own[third:],
        ],
        axis=0,
    ).astype(half_type)
    grad_heads = dot_on(units, d_packed, 0, 1).reshape(
        seq_count, wt_count, own_rows, local_width
    )
    grad_pieces = cube_sum(grad_heads.transpose(1, 0, 2, 3)).astype(half_type)
    d_unit_parts = dot_on(d_packed, qkv_heads, 0, 1)
    d_unit, (grad_pieces, mixed_owned) = ring_sum(
        [
            lax.dynamic_slice(d_unit_parts, (ahead(k) * tok_rows, 0), (tok_rows, model_width))
            for k in range(seq_count)
        ],
        (grad_pieces, mixed_owned),
    )
    in_unscaled = jnp.stack(
        [mixed_owned[:hidden_units].T, mixed_owned[hidden_units : 2 * hidden_units].T], axis=1
    )
    in_owned = in_unscaled * gain_rows[:, None, None]
    mlp_owned = mixed_owned[2 * hidden_units :].T
    gain_two_part = jnp.sum(in_unscaled * w_in.astype(jnp.float32), axis=(1, 2))
    unit_one, scale_one = normalize(inputs)
    input_grad = (d_middle + normalize_back(d_unit, unit_one, scale_one)).astype(half_type)
    grad_rows = lax.all_to_all(grad_pieces, "seq", split_axis=0, concat_axis=0, tiled=True)
    qkv_unscaled = (
        grad_rows.reshape(seq_count, own_rows, 3, local_heads, HD)
        .transpose(1, 0, 3, 2, 4)
        .reshape(own_rows, 3 * model_width)
        .astype(jnp.float32)
    )
    qkv_owned = qkv_unscaled * gain_own
    gain_one_owned = jnp.sum(qkv_unscaled * w_qkv.astype(jnp.float32), axis=1)
    gain_two_owned = cube_sum(gain_two_part.reshape(wt_count, 1, own_rows)).reshape(own_rows)
    return (
        output.reshape(1, tok_rows, model_width),
        input_grad.reshape(1, tok_rows, model_width),
        qkv_owned,
        attn_owned,
        in_owned,
        mlp_owned,
        gain_one_owned,
        gain_two_owned,
    )


def solution(mesh):
    in_specs = (
        P("wt", "seq", None),
        P(("seq", "wt"), None),
        P(("seq", "wt"), None),
        P("seq", None, "wt"),
        P("seq", "wt"),
        P(("seq", "wt")),
        P(("seq", "wt")),
        P("wt", "seq", None),
    )
    out_specs = (
        P("wt", "seq", None),
        P("wt", "seq", None),
        P(("seq", "wt"), None),
        P(("seq", "wt"), None),
        P("seq", None, "wt"),
        P("seq", "wt"),
        P(("seq", "wt")),
        P(("seq", "wt")),
    )
    return jax.shard_map(shards, mesh=mesh, in_specs=in_specs, out_specs=out_specs, check_vma=False)
```

```python
import functools
import math

import jax
import jax.numpy as jnp
from jax import lax
from jax.experimental import pallas as pl
from jax.experimental.pallas import tpu as pltpu
from jax.sharding import PartitionSpec as P

H = 16
HD = 64


epsilon = 1e-05
rope_base = 160000.0
half_type = jnp.bfloat16


def ring_order(count):
    half = count // 2
    return [2 * p if p < half else 2 * (count - 1 - p) + 1 for p in range(count)]


def ring_pairs(count):
    order = ring_order(count)
    right = [(order[p], order[(p + 1) % count]) for p in range(count)]
    left = [(target, source) for source, target in right]
    return right, left


def cut_rows(rows):
    return rows // 32 * 16 if rows >= 32 else rows // 2


class Steps:
    def __init__(self, steps):
        self.steps = steps
        self.result = None
        self.pending = next(steps)

    def advance(self):
        try:
            self.pending = self.steps.send(self.pending)
        except StopIteration as ended:
            self.result = ended.value

    def tie(self, value):
        if self.result is None:
            self.pending, value = lax.optimization_barrier((self.pending, value))
            self.advance()
        return value

    def finish(self):
        while self.result is None:
            self.advance()
        return self.result


def ring_gather(block, axis="seq"):
    count = lax.axis_size(axis)
    right, left = ring_pairs(count)
    half = count // 2
    behind, ahead = [block], [block]
    for _ in range(1, half):
        got = yield (lax.ppermute(behind[-1], axis, right), lax.ppermute(ahead[-1], axis, left))
        behind.append(got[0])
        ahead.append(got[1])
    cut = cut_rows(block.shape[0])
    far = yield (
        lax.ppermute(behind[-1][:cut], axis, right),
        lax.ppermute(ahead[-1][cut:], axis, left),
    )
    far = jnp.concatenate(far, axis=0)
    return ahead[:half] + [far] + [behind[count - k] for k in range(half + 1, count)]


def ring_sum(parts, axis="seq"):
    count = lax.axis_size(axis)
    right, left = ring_pairs(count)
    half = count // 2
    cut = cut_rows(parts[0].shape[0])
    top, bottom = yield (
        lax.ppermute(parts[half][:cut].astype(half_type), axis, right),
        lax.ppermute(parts[half][cut:].astype(half_type), axis, left),
    )
    for off in range(half - 1, 0, -1):
        up = parts[off].astype(jnp.float32)
        down = parts[count - off].astype(jnp.float32)
        if off == half - 1:
            up = jnp.concatenate([up[:cut] + top.astype(jnp.float32), up[cut:]], axis=0)
            down = jnp.concatenate([down[:cut], down[cut:] + bottom.astype(jnp.float32)], axis=0)
        else:
            up = up + top.astype(jnp.float32)
            down = down + bottom.astype(jnp.float32)
        top, bottom = yield (
            lax.ppermute(up.astype(half_type), axis, right),
            lax.ppermute(down.astype(half_type), axis, left),
        )
    return parts[0].astype(jnp.float32) + top.astype(jnp.float32) + bottom.astype(jnp.float32)


def from_partner(value, axis, bit):
    mask = 2**bit
    pairs = [(source, source ^ mask) for source in range(lax.axis_size(axis))]
    return lax.ppermute(value, axis, pairs)


def bits_of(axis):
    return int(math.log2(lax.axis_size(axis)))


def cube_gather(block, axis="wt"):
    place = lax.axis_index(axis)
    bits = bits_of(axis)
    value = block
    for done, bit in enumerate(range(bits - 1, -1, -1)):
        other = from_partner(value, axis, bit)
        low = (place >> bit) % 2 == 0
        value = jnp.stack([jnp.where(low, value, other), jnp.where(low, other, value)], axis=done)
    return value.reshape((2**bits,) + block.shape)


def cube_sum(value, axis="wt"):
    place = lax.axis_index(axis)
    bits = bits_of(axis)
    value = value.reshape((2,) * bits + value.shape[1:])
    for bit in range(bits):
        at = bits - 1 - bit
        mine = (place >> bit) % 2
        keep = lax.dynamic_index_in_dim(value, mine, at, keepdims=False)
        give = lax.dynamic_index_in_dim(value, 1 - mine, at, keepdims=False)
        value = keep.astype(jnp.float32) + from_partner(give.astype(half_type), axis, bit).astype(
            jnp.float32
        )
    return value


def group_gather(rows, axis="wt"):
    for bit in range(bits_of(axis) - 1, -1, -1):
        rows = jnp.concatenate([rows, from_partner(rows, axis, bit)], axis=0)
    return rows


def group_sum(rows, held=(), axis="wt"):
    for bit in range(bits_of(axis)):
        half = rows.shape[0] // 2
        got = from_partner(rows[half:].astype(half_type), axis, bit)
        if bit == 0 and held:
            got, held = lax.optimization_barrier((got, held))
        rows = rows[:half].astype(jnp.float32) + got.astype(jnp.float32)
    return (rows, held) if held else rows


def normalize(features):
    average = jnp.mean(features, axis=-1, keepdims=True)
    centred = features - average
    spread = jnp.mean(centred * centred, axis=-1, keepdims=True)
    scale = lax.rsqrt(spread + epsilon)
    return centred * scale, scale


def normalize_back(d_unit, unit, scale):
    return scale * (
        d_unit
        - jnp.mean(d_unit, axis=-1, keepdims=True)
        - unit * jnp.mean(d_unit * unit, axis=-1, keepdims=True)
    )


def rotary_tables(positions, head_width):
    half_width = head_width // 2
    frequency = jnp.exp(
        jnp.arange(half_width).astype(jnp.float32) * (-2.0 * math.log(rope_base) / head_width)
    )
    angles = frequency[:, None] * positions[None, :]
    return jnp.cos(angles), jnp.sin(angles)


def rotate(vectors, cosine, sine_table):
    features, count = vectors.shape
    half_width = cosine.shape[0]
    split = vectors.reshape(features // (2 * half_width), 2, half_width, count)
    first, second = split[:, 0], split[:, 1]
    return jnp.stack(
        [first * cosine - second * sine_table, second * cosine + first * sine_table], axis=1
    ).reshape(features, count)


def exact_gelu(inner):
    return jax.nn.gelu(inner, approximate=False)


def dot_on(left, right, left_dim, right_dim):
    return lax.dot_general(
        left, right, (((left_dim,), (right_dim,)), ((), ())), preferred_element_type=jnp.float32
    )


def matmul(left, right):
    return jnp.dot(left, right, preferred_element_type=jnp.float32)


def head_rows(value, head):
    blank = jnp.zeros((HD, value.shape[1]), value.dtype)
    heads = value.shape[0] // HD
    if heads == 1:
        return value
    return jnp.concatenate(
        [value[h * HD : (h + 1) * HD] if h == head else blank for h in range(heads)], axis=0
    )


def head_columns(value, head):
    if value.shape[1] == HD:
        return value
    lane = lax.broadcasted_iota(jnp.int32, value.shape, 1)
    inside = (lane >= head * HD) & (lane < (head + 1) * HD)
    return jnp.where(inside, value, jnp.zeros_like(value))


def forward_kernel(at, q_ref, k_ref, vt_ref, out_ref, lse_ref, low_ref):
    features, count = out_ref.shape
    length = k_ref.shape[0]
    span = math.gcd(length, 512)
    queries = q_ref[:, at : at + count]
    for head in range(features // HD):
        rows = slice(head * HD, (head + 1) * HD)
        query = head_rows(queries, head)
        top = total = accum = None
        for start in range(0, length, span):
            scores = matmul(k_ref[start : start + span, :], query)
            block_top = jnp.max(scores, axis=0, keepdims=True)
            new_top = block_top if top is None else jnp.maximum(top, block_top)
            raised = jnp.exp(scores - new_top)
            weight = jnp.sum(raised, axis=0, keepdims=True)
            part = matmul(vt_ref[rows, start : start + span], raised.astype(half_type))
            if top is None:
                total, accum = weight, part
            else:
                shrink = jnp.exp(top - new_top)
                total = total * shrink + weight
                accum = accum * shrink + part
            top = new_top
        result = accum / total
        out_ref[rows, :] = result
        blocks, _, width = low_ref.shape
        for b in range(blocks):
            low_ref[b, rows, :] = result[:, b * width : (b + 1) * width].astype(half_type)
        lse_ref[head : head + 1, :] = top + jnp.log(total)


def backward_kernel(first, at, *refs):
    q_ref, qn_ref, do_ref, out_ref, lse_ref, k_ref, kt_ref, v_ref = refs[:8]
    dk_in, dv_in = (None, None) if first else refs[8:10]
    dq_ref, dk_ref, dv_ref = refs[-3:]
    features, count = out_ref.shape
    length = k_ref.shape[0]
    span = math.gcd(length, 512)
    heads = features // HD
    width = do_ref.shape[2]
    d_out = jnp.concatenate(
        [do_ref[b] for b in range(at // width, (at + count) // width)], axis=1
    )
    d_out_rows = d_out.astype(jnp.float32).T.astype(half_type)
    queries = [head_rows(q_ref[:, at : at + count], h) for h in range(heads)]
    d_outs = [head_rows(d_out, h) for h in range(heads)]
    query_columns = [head_columns(qn_ref[at : at + count, :], h) for h in range(heads)]
    d_out_columns = [head_columns(d_out_rows, h) for h in range(heads)]
    weighed = d_out.astype(jnp.float32) * out_ref[...]
    deltas = [
        jnp.sum(weighed[h * HD : (h + 1) * HD], axis=0, keepdims=True) for h in range(heads)
    ]
    d_query = [None] * heads
    for start in range(0, length, span):
        stop = start + span
        d_key = None if first else dk_in[start:stop, :]
        d_value = None if first else dv_in[start:stop, :]
        for h in range(heads):
            scores = matmul(k_ref[start:stop, :], queries[h])
            probs = jnp.exp(scores - lse_ref[h : h + 1, :])
            d_probs = matmul(v_ref[start:stop, :], d_outs[h])
            d_scores = (probs * (d_probs - deltas[h])).astype(half_type)
            value_part = matmul(probs.astype(half_type), d_out_columns[h])
            key_part = matmul(d_scores, query_columns[h])
            d_value = value_part if d_value is None else d_value + value_part
            d_key = key_part if d_key is None else d_key + key_part
            part = matmul(kt_ref[h * HD : (h + 1) * HD, start:stop], d_scores)
            d_query[h] = part if d_query[h] is None else d_query[h] + part
        dk_ref[start:stop, :] = d_key
        dv_ref[start:stop, :] = d_value
    for h in range(heads):
        dq_ref[h * HD : (h + 1) * HD, :] = d_query[h] * (1.0 / math.sqrt(HD))


kernel_params = pltpu.CompilerParams(vmem_limit_bytes=20 * 2**20)


def attention_forward(at, blocks, width, queries, keys, values_t):
    features = queries.shape[0]
    length = keys.shape[0]
    heads = features // HD
    count = blocks * width
    return pl.pallas_call(
        functools.partial(forward_kernel, at),
        out_shape=(
            jax.ShapeDtypeStruct((features, count), jnp.float32),
            jax.ShapeDtypeStruct((heads, count), jnp.float32),
            jax.ShapeDtypeStruct((blocks, features, width), half_type),
        ),
        compiler_params=kernel_params,
        cost_estimate=pl.CostEstimate(
            flops=16 * features * count * length,
            bytes_accessed=4 * features * length + 6 * features * count,
            transcendentals=heads * count * length,
        ),
    )(queries, keys, values_t)


def attention_backward(at, count, tensors, sums):
    queries, keys = tensors[0], tensors[5]
    features = queries.shape[0]
    length = keys.shape[0]
    first = sums is None
    total = jax.ShapeDtypeStruct((length, features), jnp.float32)
    given = len(tensors)
    return pl.pallas_call(
        functools.partial(backward_kernel, first, at),
        out_shape=(
            jax.ShapeDtypeStruct((features, count), jnp.float32),
            total,
            total,
        ),
        input_output_aliases={} if first else {given + i: 1 + i for i in range(2)},
        compiler_params=kernel_params,
        cost_estimate=pl.CostEstimate(
            flops=40 * features * count * length,
            bytes_accessed=22 * features * length,
            transcendentals=features // HD * count * length,
        ),
    )(*tensors, *(sums or ()))


def shards(tokens, w_qkv, w_attn_out, w_in, w_mlp_out, gain_one, gain_two, cotangent):
    seq_tokens = tokens[0]
    seq_cot = cotangent[0]
    tok_rows, model_width = seq_tokens.shape
    seq_count = lax.axis_size("seq")
    wt_count = lax.axis_size("wt")
    seq_place = lax.axis_index("seq")
    wt_place = lax.axis_index("wt")
    half_place = wt_place % 2
    slice_len = tok_rows * seq_count
    local_heads = H // seq_count
    local_width = 3 * model_width // seq_count
    own_rows = w_qkv.shape[0]
    hidden_units = w_mlp_out.shape[1]
    score_scale = 1.0 / math.sqrt(HD)
    half_ring = seq_count // 2
    along, side = seq_place // 2, seq_place % 2
    ring_place = jnp.where(side == 0, along, seq_count - 1 - along)

    def ahead(k):
        at = (ring_place + k) % seq_count
        return jnp.where(at < half_ring, 2 * at, 2 * (seq_count - 1 - at) + 1)

    blocks = 2
    span = blocks * tok_rows

    token_ring = Steps(ring_gather(jnp.concatenate([seq_tokens, w_attn_out], axis=0)))
    gain_two = token_ring.tie(gain_two)
    token_blocks = token_ring.finish()
    gain_own = gain_one.astype(jnp.float32)[:, None]
    gain_own_two = gain_two.astype(jnp.float32)
    scaled_qkv = (gain_own * w_qkv.astype(jnp.float32)).astype(half_type)
    qkv_pieces = lax.all_to_all(
        scaled_qkv.reshape(own_rows, seq_count, local_heads, 3, HD)
        .transpose(1, 0, 3, 2, 4)
        .reshape(seq_count, own_rows, local_width),
        "seq",
        split_axis=0,
        concat_axis=0,
        tiled=True,
    )
    qkv_heads = cube_gather(qkv_pieces).transpose(1, 0, 2, 3).reshape(model_width, local_width)
    gain_rows = cube_gather(gain_two.reshape(1, own_rows)).reshape(wt_count * own_rows)
    gain_rows = gain_rows.astype(jnp.float32)

    scaled_in = gain_rows[:, None, None] * w_in.astype(jnp.float32)
    mixed = jnp.concatenate(
        [
            scaled_in[:, 0].astype(half_type).T,
            scaled_in[:, 1].astype(half_type).T,
            w_mlp_out.T,
        ],
        axis=0,
    )
    mixed, group_cot, token_blocks[half_ring] = lax.optimization_barrier(
        (mixed, seq_cot, token_blocks[half_ring])
    )
    mixed_ring = Steps(ring_gather(mixed))
    feed_rows = w_in.shape[0]
    group_cot = group_gather(group_cot)
    out_stack = jnp.zeros((seq_count, own_rows, model_width), half_type)
    for k, block in enumerate(token_blocks):
        out_stack = lax.dynamic_update_slice(out_stack, block[None, tok_rows:], (ahead(k), 0, 0))
    out_full = (
        cube_gather(out_stack).transpose(1, 0, 2, 3).reshape(model_width, model_width)
    )

    units = jnp.zeros((slice_len, model_width), half_type)
    for k, block in enumerate(token_blocks):
        unit = normalize(block[:tok_rows].astype(jnp.float32))[0].astype(half_type)
        units = lax.dynamic_update_slice(units, unit, (ahead(k) * tok_rows, 0))
    packed = dot_on(qkv_heads, units, 0, 1)
    positions = (half_place * slice_len + jnp.arange(slice_len)).astype(jnp.float32)
    cosine, sine_table = rotary_tables(positions, HD)
    third = local_width // 3
    queries = (rotate(packed[:third], cosine, sine_table).astype(half_type) * score_scale).astype(
        half_type
    )
    own_pairs = jnp.concatenate(
        [rotate(packed[third : 2 * third], cosine, sine_table), packed[2 * third :]], axis=0
    ).astype(half_type)
    pairs = jnp.concatenate([own_pairs, from_partner(own_pairs, "wt", 0)], axis=1)
    pairs, group_cot = lax.optimization_barrier((pairs, group_cot))
    keys_t, values_t = pairs[:third], pairs[third:]
    keys, values = keys_t.T, values_t.T

    attended, log_totals, low = [], [], []
    for at in range(0, slice_len, span):
        results = attention_forward(at, blocks, tok_rows, queries, keys, values_t)
        for kept, result in zip((attended, log_totals, low), results):
            kept.append(result)
        if at == 0:
            low[0], queries = mixed_ring.tie((low[0], queries))
    low = mixed_ring.tie(jnp.concatenate(low, axis=0))
    arrived = lax.all_to_all(low, "seq", split_axis=0, concat_axis=0, tiled=True).reshape(
        model_width, tok_rows
    )
    arrived = mixed_ring.tie(arrived)
    inputs = seq_tokens.astype(jnp.float32)
    middle = inputs + dot_on(arrived, out_full, 0, 0)
    unit_two, scale_two = normalize(middle)
    group_unit = group_gather(unit_two.astype(half_type))

    in_rows = jnp.zeros((2 * hidden_units, model_width), half_type)
    out_rows = jnp.zeros((hidden_units, model_width), half_type)
    for k, block in enumerate(mixed_ring.finish()):
        at = (0, ahead(k) * feed_rows)
        in_rows = lax.dynamic_update_slice(in_rows, block[: 2 * hidden_units], at)
        out_rows = lax.dynamic_update_slice(out_rows, block[2 * hidden_units :], at)
    projected = dot_on(in_rows, group_unit, 1, 1)
    activated, gelu_pull = jax.vjp(exact_gelu, projected[:hidden_units])
    gate = projected[hidden_units:]
    hidden = (activated * gate).astype(half_type)
    d_hidden = dot_on(out_rows, group_cot, 1, 1)
    d_projected = jnp.concatenate(
        [gelu_pull(d_hidden * gate)[0], d_hidden * activated], axis=0
    ).astype(half_type)
    d_unit_rows, d_projected, hidden = lax.optimization_barrier(
        (dot_on(d_projected, in_rows, 0, 0), d_projected, hidden)
    )
    grad_mixed = jnp.concatenate(
        [dot_on(d_projected, group_unit, 1, 0), dot_on(hidden, group_cot, 1, 0)], axis=0
    ).astype(half_type)
    d_unit_two, (grad_mixed,) = group_sum(d_unit_rows, (grad_mixed,))
    d_middle = seq_cot.astype(jnp.float32) + normalize_back(d_unit_two, unit_two, scale_two)
    d_branch = d_middle.astype(half_type)
    grad_ring = Steps(
        ring_sum(
            [
                lax.dynamic_slice(
                    grad_mixed, (0, ahead(k) * feed_rows), (3 * hidden_units, feed_rows)
                )
                for k in range(seq_count)
            ]
        )
    )
    d_sent = dot_on(out_full, d_branch, 1, 1).astype(half_type)
    d_sent = grad_ring.tie(d_sent.reshape(seq_count, local_heads * HD, tok_rows))
    d_heads = lax.all_to_all(d_sent, "seq", split_axis=0, concat_axis=0, tiled=True)
    d_heads, d_out_branch = grad_ring.tie((d_heads, d_branch))
    d_heads, mlp_rows = lax.optimization_barrier((d_heads, dot_on(hidden, out_rows, 0, 0)))
    output = (middle + group_sum(mlp_rows)).astype(half_type)
    query_rows = queries.T
    d_queries, sums = [], None
    for c in range(slice_len // span):
        d_query, *sums = attention_backward(
            c * span,
            span,
            (
                queries,
                query_rows,
                d_heads,
                attended[c],
                log_totals[c],
                keys,
                keys_t,
                values,
            ),
            sums,
        )
        d_queries.append(d_query)
    sums = grad_ring.tie(sums)
    d_query = jnp.concatenate(d_queries, axis=1)
    grad_out = dot_on(arrived, d_out_branch, 1, 0).reshape(
        seq_count, wt_count, own_rows, model_width
    )
    gain_row = jnp.sum(d_unit_two * unit_two, axis=0).reshape(seq_count, wt_count, 1, own_rows)
    gain_row = jnp.pad(gain_row, ((0, 0), (0, 0), (0, 7), (0, model_width - own_rows)))
    grad_out = jnp.concatenate([grad_out, gain_row], axis=2)
    grad_out = cube_sum(grad_out.transpose(1, 0, 2, 3))

    d_pairs = jnp.concatenate(sums, axis=1).T
    d_own = d_pairs[:, :slice_len] + from_partner(
        d_pairs[:, slice_len:].astype(half_type), "wt", 0
    ).astype(jnp.float32)
    d_packed = jnp.concatenate(
        [
            rotate(d_query, cosine, -sine_table),
            rotate(d_own[:third], cosine, -sine_table),
            d_own[third:],
        ],
        axis=0,
    ).astype(half_type)
    grad_heads = dot_on(units, d_packed, 0, 1).reshape(
        seq_count, wt_count, own_rows, local_width
    )
    grad_pieces = cube_sum(grad_heads.transpose(1, 0, 2, 3)).astype(half_type)
    d_unit_parts = dot_on(d_packed, qkv_heads, 0, 1)
    last_ring = Steps(
        ring_sum(
            [
                jnp.concatenate(
                    [
                        lax.dynamic_slice(
                            d_unit_parts, (ahead(k) * tok_rows, 0), (tok_rows, model_width)
                        ),
                        lax.dynamic_index_in_dim(grad_out, ahead(k), 0, keepdims=False),
                    ],
                    axis=0,
                )
                for k in range(seq_count)
            ]
        )
    )
    for _ in range(half_ring - 2):
        last_ring.advance()
    grad_pieces = last_ring.tie(grad_pieces)
    last_sum = last_ring.finish()
    d_unit = last_sum[:tok_rows]
    attn_owned = last_sum[tok_rows : tok_rows + own_rows]
    gain_two_owned = last_sum[tok_rows + own_rows, :own_rows] / gain_own_two
    mixed_owned = grad_ring.finish()
    in_unscaled = jnp.stack(
        [mixed_owned[:hidden_units].T, mixed_owned[hidden_units : 2 * hidden_units].T], axis=1
    )
    in_owned = in_unscaled * gain_rows[:, None, None]
    mlp_owned = mixed_owned[2 * hidden_units :].T
    unit_one, scale_one = normalize(inputs)
    input_grad = (d_middle + normalize_back(d_unit, unit_one, scale_one)).astype(half_type)
    grad_rows = lax.all_to_all(grad_pieces, "seq", split_axis=0, concat_axis=0, tiled=True)
    qkv_unscaled = (
        grad_rows.reshape(seq_count, own_rows, 3, local_heads, HD)
        .transpose(1, 0, 3, 2, 4)
        .reshape(own_rows, 3 * model_width)
        .astype(jnp.float32)
    )
    qkv_owned = qkv_unscaled * gain_own
    gain_one_owned = jnp.sum(qkv_unscaled * w_qkv.astype(jnp.float32), axis=1)
    return (
        output.reshape(1, tok_rows, model_width),
        input_grad.reshape(1, tok_rows, model_width),
        qkv_owned,
        attn_owned,
        in_owned,
        mlp_owned,
        gain_one_owned,
        gain_two_owned,
    )


def solution(mesh):
    in_specs = (
        P("wt", "seq", None),
        P(("seq", "wt"), None),
        P(("seq", "wt"), None),
        P("seq", None, "wt"),
        P("seq", "wt"),
        P(("seq", "wt")),
        P(("seq", "wt")),
        P("wt", "seq", None),
    )
    out_specs = (
        P("wt", "seq", None),
        P("wt", "seq", None),
        P(("seq", "wt"), None),
        P(("seq", "wt"), None),
        P("seq", None, "wt"),
        P("seq", "wt"),
        P(("seq", "wt")),
        P(("seq", "wt")),
    )
    return jax.shard_map(shards, mesh=mesh, in_specs=in_specs, out_specs=out_specs, check_vma=False)
```

```python
import functools
import math

import jax
import jax.numpy as jnp
from jax import lax
from jax.experimental import pallas as pl
from jax.experimental.pallas import tpu as pltpu
from jax.sharding import PartitionSpec as P

H = 16
HD = 64


epsilon = 1e-05
rope_base = 160000.0
half_type = jnp.bfloat16


def ring_order(count):
    half = count // 2
    return [2 * p if p < half else 2 * (count - 1 - p) + 1 for p in range(count)]


def ring_pairs(count):
    order = ring_order(count)
    right = [(order[p], order[(p + 1) % count]) for p in range(count)]
    left = [(target, source) for source, target in right]
    return right, left


def cut_rows(rows):
    return rows // 32 * 16 if rows >= 32 else rows // 2


class Steps:
    def __init__(self, steps):
        self.steps = steps
        self.result = None
        self.pending = next(steps)

    def advance(self):
        try:
            self.pending = self.steps.send(self.pending)
        except StopIteration as ended:
            self.result = ended.value

    def tie(self, value):
        if self.result is None:
            self.pending, value = lax.optimization_barrier((self.pending, value))
            self.advance()
        return value

    def finish(self):
        while self.result is None:
            self.advance()
        return self.result


def ring_gather(block, axis="seq"):
    count = lax.axis_size(axis)
    right, left = ring_pairs(count)
    half = count // 2
    behind, ahead = [block], [block]
    for _ in range(1, half):
        got = yield (lax.ppermute(behind[-1], axis, right), lax.ppermute(ahead[-1], axis, left))
        behind.append(got[0])
        ahead.append(got[1])
    cut = cut_rows(block.shape[0])
    far = yield (
        lax.ppermute(behind[-1][:cut], axis, right),
        lax.ppermute(ahead[-1][cut:], axis, left),
    )
    far = jnp.concatenate(far, axis=0)
    return ahead[:half] + [far] + [behind[count - k] for k in range(half + 1, count)]


def ring_sum(parts, axis="seq"):
    count = lax.axis_size(axis)
    right, left = ring_pairs(count)
    half = count // 2
    cut = cut_rows(parts[0].shape[0])
    top, bottom = yield (
        lax.ppermute(parts[half][:cut].astype(half_type), axis, right),
        lax.ppermute(parts[half][cut:].astype(half_type), axis, left),
    )
    for off in range(half - 1, 0, -1):
        up = parts[off].astype(jnp.float32)
        down = parts[count - off].astype(jnp.float32)
        if off == half - 1:
            up = jnp.concatenate([up[:cut] + top.astype(jnp.float32), up[cut:]], axis=0)
            down = jnp.concatenate([down[:cut], down[cut:] + bottom.astype(jnp.float32)], axis=0)
        else:
            up = up + top.astype(jnp.float32)
            down = down + bottom.astype(jnp.float32)
        top, bottom = yield (
            lax.ppermute(up.astype(half_type), axis, right),
            lax.ppermute(down.astype(half_type), axis, left),
        )
    return parts[0].astype(jnp.float32) + top.astype(jnp.float32) + bottom.astype(jnp.float32)


def from_partner(value, axis, bit):
    mask = 2**bit
    pairs = [(source, source ^ mask) for source in range(lax.axis_size(axis))]
    return lax.ppermute(value, axis, pairs)


def bits_of(axis):
    return int(math.log2(lax.axis_size(axis)))


def cube_gather(block, axis="wt"):
    place = lax.axis_index(axis)
    bits = bits_of(axis)
    value = block
    for done, bit in enumerate(range(bits - 1, -1, -1)):
        other = from_partner(value, axis, bit)
        low = (place >> bit) % 2 == 0
        value = jnp.stack([jnp.where(low, value, other), jnp.where(low, other, value)], axis=done)
    return value.reshape((2**bits,) + block.shape)


def cube_sum(value, axis="wt"):
    place = lax.axis_index(axis)
    bits = bits_of(axis)
    value = value.reshape((2,) * bits + value.shape[1:])
    for bit in range(bits):
        at = bits - 1 - bit
        mine = (place >> bit) % 2
        keep = lax.dynamic_index_in_dim(value, mine, at, keepdims=False)
        give = lax.dynamic_index_in_dim(value, 1 - mine, at, keepdims=False)
        value = keep.astype(jnp.float32) + from_partner(give.astype(half_type), axis, bit).astype(
            jnp.float32
        )
    return value


def group_gather(rows, axis="wt"):
    for bit in range(bits_of(axis) - 1, -1, -1):
        rows = jnp.concatenate([rows, from_partner(rows, axis, bit)], axis=0)
    return rows


def group_sum(rows, held=(), axis="wt"):
    for bit in range(bits_of(axis)):
        half = rows.shape[0] // 2
        got = from_partner(rows[half:].astype(half_type), axis, bit)
        if bit == 0 and held:
            got, held = lax.optimization_barrier((got, held))
        rows = rows[:half].astype(jnp.float32) + got.astype(jnp.float32)
    return (rows, held) if held else rows


def normalize(features):
    average = jnp.mean(features, axis=-1, keepdims=True)
    centred = features - average
    spread = jnp.mean(centred * centred, axis=-1, keepdims=True)
    scale = lax.rsqrt(spread + epsilon)
    return centred * scale, scale


def normalize_back(d_unit, unit, scale):
    return scale * (
        d_unit
        - jnp.mean(d_unit, axis=-1, keepdims=True)
        - unit * jnp.mean(d_unit * unit, axis=-1, keepdims=True)
    )


def rotary_tables(positions, head_width):
    half_width = head_width // 2
    frequency = jnp.exp(
        jnp.arange(half_width).astype(jnp.float32) * (-2.0 * math.log(rope_base) / head_width)
    )
    angles = frequency[:, None] * positions[None, :]
    return jnp.cos(angles), jnp.sin(angles)


def rotate(vectors, cosine, sine_table):
    features, count = vectors.shape
    half_width = cosine.shape[0]
    split = vectors.reshape(features // (2 * half_width), 2, half_width, count)
    first, second = split[:, 0], split[:, 1]
    return jnp.stack(
        [first * cosine - second * sine_table, second * cosine + first * sine_table], axis=1
    ).reshape(features, count)


def exact_gelu(inner):
    return jax.nn.gelu(inner, approximate=False)


def dot_on(left, right, left_dim, right_dim):
    return lax.dot_general(
        left, right, (((left_dim,), (right_dim,)), ((), ())), preferred_element_type=jnp.float32
    )


def matmul(left, right):
    return jnp.dot(left, right, preferred_element_type=jnp.float32)


def head_rows(value, head):
    blank = jnp.zeros((HD, value.shape[1]), value.dtype)
    heads = value.shape[0] // HD
    if heads == 1:
        return value
    return jnp.concatenate(
        [value[h * HD : (h + 1) * HD] if h == head else blank for h in range(heads)], axis=0
    )


def head_columns(value, head):
    if value.shape[1] == HD:
        return value
    lane = lax.broadcasted_iota(jnp.int32, value.shape, 1)
    inside = (lane >= head * HD) & (lane < (head + 1) * HD)
    return jnp.where(inside, value, jnp.zeros_like(value))


def forward_kernel(at, q_ref, k_ref, vt_ref, w_ref, out_ref, lse_ref, branch_ref):
    features = w_ref.shape[0]
    count = out_ref.shape[1]
    length = k_ref.shape[0]
    span = math.gcd(length, 512)
    queries = q_ref[:, at : at + count]
    for head in range(features // HD):
        rows = slice(head * HD, (head + 1) * HD)
        query = head_rows(queries, head)
        top = total = accum = None
        for start in range(0, length, span):
            scores = matmul(k_ref[start : start + span, :], query)
            block_top = jnp.max(scores, axis=0, keepdims=True)
            new_top = block_top if top is None else jnp.maximum(top, block_top)
            raised = jnp.exp(scores - new_top)
            weight = jnp.sum(raised, axis=0, keepdims=True)
            part = matmul(vt_ref[rows, start : start + span], raised.astype(half_type))
            if top is None:
                total, accum = weight, part
            else:
                shrink = jnp.exp(top - new_top)
                total = total * shrink + weight
                accum = accum * shrink + part
            top = new_top
        out_ref[rows, :] = accum / total
        lse_ref[head : head + 1, :] = top + jnp.log(total)
    branch_ref[...] = dot_on(out_ref[...].astype(half_type), w_ref[...], 0, 0)


def backward_kernel(first, at, *refs):
    q_ref, qn_ref, near_ref, far_ref, w_ref, out_ref, lse_ref, k_ref, kt_ref, v_ref = refs[:10]
    dk_in, dv_in, gw_in = (None, None, None) if first else refs[10:13]
    dq_ref, dk_ref, dv_ref, gw_ref = refs[-4:]
    features, count = out_ref.shape
    length = k_ref.shape[0]
    span = math.gcd(length, 512)
    heads = features // HD
    weights = w_ref[...]
    blocks = [near_ref[...], far_ref[...]]
    d_out = jnp.concatenate([dot_on(weights, d, 1, 1) for d in blocks], axis=1).astype(half_type)
    d_out_rows = jnp.concatenate([dot_on(d, weights, 1, 1) for d in blocks], axis=0).astype(
        half_type
    )
    attended = out_ref[...].astype(half_type)
    rows = count // 2
    grad = matmul(attended[:, :rows], blocks[0]) + matmul(attended[:, rows:], blocks[1])
    gw_ref[...] = grad if first else gw_in[...] + grad
    queries = [head_rows(q_ref[:, at : at + count], h) for h in range(heads)]
    d_outs = [head_rows(d_out, h) for h in range(heads)]
    query_columns = [head_columns(qn_ref[at : at + count, :], h) for h in range(heads)]
    d_out_columns = [head_columns(d_out_rows, h) for h in range(heads)]
    weighed = d_out.astype(jnp.float32) * out_ref[...]
    deltas = [
        jnp.sum(weighed[h * HD : (h + 1) * HD], axis=0, keepdims=True) for h in range(heads)
    ]
    d_query = [None] * heads
    for start in range(0, length, span):
        stop = start + span
        d_key = None if first else dk_in[start:stop, :]
        d_value = None if first else dv_in[start:stop, :]
        for h in range(heads):
            scores = matmul(k_ref[start:stop, :], queries[h])
            probs = jnp.exp(scores - lse_ref[h : h + 1, :])
            d_probs = matmul(v_ref[start:stop, :], d_outs[h])
            d_scores = (probs * (d_probs - deltas[h])).astype(half_type)
            value_part = matmul(probs.astype(half_type), d_out_columns[h])
            key_part = matmul(d_scores, query_columns[h])
            d_value = value_part if d_value is None else d_value + value_part
            d_key = key_part if d_key is None else d_key + key_part
            part = matmul(kt_ref[h * HD : (h + 1) * HD, start:stop], d_scores)
            d_query[h] = part if d_query[h] is None else d_query[h] + part
        dk_ref[start:stop, :] = d_key
        dv_ref[start:stop, :] = d_value
    for h in range(heads):
        dq_ref[h * HD : (h + 1) * HD, :] = d_query[h] * (1.0 / math.sqrt(HD))


kernel_params = pltpu.CompilerParams(vmem_limit_bytes=20 * 2**20)


def attention_forward(at, count, queries, keys, values_t, weights):
    features = queries.shape[0]
    length = keys.shape[0]
    heads = features // HD
    return pl.pallas_call(
        functools.partial(forward_kernel, at),
        out_shape=(
            jax.ShapeDtypeStruct((features, count), jnp.float32),
            jax.ShapeDtypeStruct((heads, count), jnp.float32),
            jax.ShapeDtypeStruct((count, weights.shape[1]), jnp.float32),
        ),
        compiler_params=kernel_params,
        cost_estimate=pl.CostEstimate(
            flops=16 * features * count * length,
            bytes_accessed=4 * features * length + 6 * features * count,
            transcendentals=heads * count * length,
        ),
    )(queries, keys, values_t, weights)


def attention_backward(at, count, tensors, sums):
    queries, keys, weights = tensors[0], tensors[7], tensors[4]
    features = queries.shape[0]
    length = keys.shape[0]
    first = sums is None
    total = jax.ShapeDtypeStruct((length, features), jnp.float32)
    given = len(tensors)
    return pl.pallas_call(
        functools.partial(backward_kernel, first, at),
        out_shape=(
            jax.ShapeDtypeStruct((features, count), jnp.float32),
            total,
            total,
            jax.ShapeDtypeStruct(weights.shape, jnp.float32),
        ),
        input_output_aliases={} if first else {given + i: 1 + i for i in range(3)},
        compiler_params=kernel_params,
        cost_estimate=pl.CostEstimate(
            flops=40 * features * count * length,
            bytes_accessed=22 * features * length,
            transcendentals=features // HD * count * length,
        ),
    )(*tensors, *(sums or ()))


def shards(tokens, w_qkv, w_attn_out, w_in, w_mlp_out, gain_one, gain_two, cotangent):
    seq_tokens = tokens[0]
    seq_cot = cotangent[0]
    tok_rows, model_width = seq_tokens.shape
    seq_count = lax.axis_size("seq")
    wt_count = lax.axis_size("wt")
    seq_place = lax.axis_index("seq")
    wt_place = lax.axis_index("wt")
    half_place = wt_place % 2
    slice_len = tok_rows * seq_count
    local_heads = H // seq_count
    local_width = 3 * model_width // seq_count
    own_rows = w_qkv.shape[0]
    hidden_units = w_mlp_out.shape[1]
    score_scale = 1.0 / math.sqrt(HD)
    half_ring = seq_count // 2
    along, side = seq_place // 2, seq_place % 2
    ring_place = jnp.where(side == 0, along, seq_count - 1 - along)

    def ahead(k):
        at = (ring_place + k) % seq_count
        return jnp.where(at < half_ring, 2 * at, 2 * (seq_count - 1 - at) + 1)

    arrival = [0]
    for k in range(1, half_ring):
        arrival += [k, seq_count - k]
    arrival.append(half_ring)
    chunks = [tuple(arrival[c : c + 2]) for c in range(0, seq_count, 2)]
    span = 2 * tok_rows

    token_ring = Steps(ring_gather(seq_tokens))
    gain_own = gain_one.astype(jnp.float32)[:, None]
    scaled_qkv = (gain_own * w_qkv.astype(jnp.float32)).astype(half_type)
    scaled_qkv, gain_two = token_ring.tie((scaled_qkv, gain_two))
    token_blocks = token_ring.finish()
    qkv_pieces = lax.all_to_all(
        scaled_qkv.reshape(own_rows, seq_count, local_heads, 3, HD)
        .transpose(1, 0, 3, 2, 4)
        .reshape(seq_count, own_rows, local_width),
        "seq",
        split_axis=0,
        concat_axis=0,
        tiled=True,
    )
    qkv_heads = cube_gather(qkv_pieces).transpose(1, 0, 2, 3).reshape(model_width, local_width)
    gain_rows = cube_gather(gain_two.reshape(1, own_rows)).reshape(wt_count * own_rows)
    gain_rows = gain_rows.astype(jnp.float32)

    scaled_in = gain_rows[:, None, None] * w_in.astype(jnp.float32)
    mixed = jnp.concatenate(
        [
            scaled_in[:, 0].astype(half_type).T,
            scaled_in[:, 1].astype(half_type).T,
            w_mlp_out.T,
        ],
        axis=0,
    )
    mixed, seq_cot, w_attn_out, token_blocks[half_ring] = lax.optimization_barrier(
        (mixed, seq_cot, w_attn_out, token_blocks[half_ring])
    )
    mixed_ring = Steps(ring_gather(mixed))
    out_heads = cube_gather(w_attn_out).reshape(wt_count * own_rows, model_width)
    feed_rows = w_in.shape[0]
    group_cot = group_gather(seq_cot)

    units = [
        normalize(
            jnp.concatenate([token_blocks[k] for k in chunk], axis=0).astype(jnp.float32)
        )[0].astype(half_type)
        for chunk in chunks
    ]
    packed = jnp.concatenate([dot_on(qkv_heads, unit, 0, 1) for unit in units], axis=1)
    positions = jnp.concatenate(
        [half_place * slice_len + ahead(k) * tok_rows + jnp.arange(tok_rows) for k in arrival]
    ).astype(jnp.float32)
    cosine, sine_table = rotary_tables(positions, HD)
    third = local_width // 3
    queries = (rotate(packed[:third], cosine, sine_table).astype(half_type) * score_scale).astype(
        half_type
    )
    own_pairs = jnp.concatenate(
        [rotate(packed[third : 2 * third], cosine, sine_table), packed[2 * third :]], axis=0
    ).astype(half_type)
    own_pairs = mixed_ring.tie(own_pairs)
    pairs = jnp.concatenate([own_pairs, from_partner(own_pairs, "wt", 0)], axis=1)
    keys_t, values_t = pairs[:third], pairs[third:]
    keys, values = keys_t.T, values_t.T

    attended, log_totals, parts = {}, {}, {}
    for c in range(len(chunks) - 1, -1, -1):
        attended[c], log_totals[c], branch = attention_forward(
            c * span, span, queries, keys, values_t, out_heads
        )
        if c == len(chunks) - 2:
            branch, queries = mixed_ring.tie((branch, queries))
        for at, k in enumerate(chunks[c]):
            parts[k] = branch[at * tok_rows : (at + 1) * tok_rows]
    in_rows = jnp.zeros((2 * hidden_units, model_width), half_type)
    out_rows = jnp.zeros((hidden_units, model_width), half_type)
    for k, block in enumerate(mixed_ring.finish()):
        at = (0, ahead(k) * feed_rows)
        in_rows = lax.dynamic_update_slice(in_rows, block[: 2 * hidden_units], at)
        out_rows = lax.dynamic_update_slice(out_rows, block[2 * hidden_units :], at)
    inputs = seq_tokens.astype(jnp.float32)
    middle = inputs + Steps(ring_sum([parts[k] for k in range(seq_count)])).finish()
    unit_two, scale_two = normalize(middle)
    group_unit = group_gather(unit_two.astype(half_type))

    projected = dot_on(in_rows, group_unit, 1, 1)
    activated, gelu_pull = jax.vjp(exact_gelu, projected[:hidden_units])
    gate = projected[hidden_units:]
    hidden = (activated * gate).astype(half_type)
    d_hidden = dot_on(out_rows, group_cot, 1, 1)
    d_projected = jnp.concatenate(
        [gelu_pull(d_hidden * gate)[0], d_hidden * activated], axis=0
    ).astype(half_type)
    d_unit_rows, d_projected, hidden = lax.optimization_barrier(
        (dot_on(d_projected, in_rows, 0, 0), d_projected, hidden)
    )
    grad_mixed = jnp.concatenate(
        [dot_on(d_projected, group_unit, 1, 0), dot_on(hidden, group_cot, 1, 0)], axis=0
    ).astype(half_type)
    d_unit_two, (grad_mixed,) = group_sum(d_unit_rows, (grad_mixed,))
    d_middle = seq_cot.astype(jnp.float32) + normalize_back(d_unit_two, unit_two, scale_two)
    d_branch, mlp_rows = lax.optimization_barrier(
        (d_middle.astype(half_type), dot_on(hidden, out_rows, 0, 0))
    )
    grad_ring = Steps(ring_sum(
        [
            lax.dynamic_slice(
                grad_mixed, (0, ahead(k) * feed_rows), (3 * hidden_units, feed_rows)
            )
            for k in range(seq_count)
        ]
    ))
    d_branch = grad_ring.tie(d_branch)
    d_blocks = Steps(ring_gather(d_branch)).finish()
    output = (middle + group_sum(mlp_rows)).astype(half_type)
    query_rows = queries.T
    d_queries, sums = [], None
    for c, (near, far) in enumerate(chunks):
        d_query, *sums = attention_backward(
            c * span,
            span,
            (
                queries,
                query_rows,
                d_blocks[near],
                d_blocks[far],
                out_heads,
                attended[c],
                log_totals[c],
                keys,
                keys_t,
                values,
            ),
            sums,
        )
        d_queries.append(d_query)
        if c < len(chunks) - 2:
            sums = grad_ring.tie(sums)
    d_query = jnp.concatenate(d_queries, axis=1)
    *sums, grad_out = sums

    mixed_owned = grad_ring.finish()
    in_unscaled = jnp.stack(
        [mixed_owned[:hidden_units].T, mixed_owned[hidden_units : 2 * hidden_units].T], axis=1
    )
    in_owned = in_unscaled * gain_rows[:, None, None]
    mlp_owned = mixed_owned[2 * hidden_units :].T
    gain_two_part = jnp.sum(in_unscaled * w_in.astype(jnp.float32), axis=(1, 2))

    d_pairs = jnp.concatenate(sums, axis=1).T
    d_own = d_pairs[:, :slice_len] + from_partner(
        d_pairs[:, slice_len:].astype(half_type), "wt", 0
    ).astype(jnp.float32)
    d_packed = jnp.concatenate(
        [
            rotate(d_query, cosine, -sine_table),
            rotate(d_own[:third], cosine, -sine_table),
            d_own[third:],
        ],
        axis=0,
    ).astype(half_type)
    grad_heads = dot_on(jnp.concatenate(units, axis=0), d_packed, 0, 1).reshape(
        seq_count, wt_count, own_rows, local_width
    )
    grad_pieces = cube_sum(grad_heads.transpose(1, 0, 2, 3)).astype(half_type)
    d_unit_parts = dot_on(d_packed, qkv_heads, 0, 1)
    last_ring = Steps(ring_sum(
        [
            d_unit_parts[at * tok_rows : (at + 1) * tok_rows]
            for at in (arrival.index(k) for k in range(seq_count))
        ]
    ))
    for _ in range(half_ring - 3):
        last_ring.advance()
    gain_two_part, grad_out, grad_pieces = last_ring.tie((gain_two_part, grad_out, grad_pieces))
    attn_owned = cube_sum(grad_out.reshape(wt_count, own_rows, model_width))
    gain_two_owned = cube_sum(gain_two_part.reshape(wt_count, 1, own_rows)).reshape(own_rows)
    d_unit = last_ring.finish()
    unit_one, scale_one = normalize(inputs)
    input_grad = (d_middle + normalize_back(d_unit, unit_one, scale_one)).astype(half_type)
    grad_rows = lax.all_to_all(grad_pieces, "seq", split_axis=0, concat_axis=0, tiled=True)
    qkv_unscaled = (
        grad_rows.reshape(seq_count, own_rows, 3, local_heads, HD)
        .transpose(1, 0, 3, 2, 4)
        .reshape(own_rows, 3 * model_width)
        .astype(jnp.float32)
    )
    qkv_owned = qkv_unscaled * gain_own
    gain_one_owned = jnp.sum(qkv_unscaled * w_qkv.astype(jnp.float32), axis=1)
    return (
        output.reshape(1, tok_rows, model_width),
        input_grad.reshape(1, tok_rows, model_width),
        qkv_owned,
        attn_owned,
        in_owned,
        mlp_owned,
        gain_one_owned,
        gain_two_owned,
    )


def solution(mesh):
    in_specs = (
        P("wt", "seq", None),
        P(("seq", "wt"), None),
        P(("seq", "wt"), None),
        P("seq", None, "wt"),
        P("seq", "wt"),
        P(("seq", "wt")),
        P(("seq", "wt")),
        P("wt", "seq", None),
    )
    out_specs = (
        P("wt", "seq", None),
        P("wt", "seq", None),
        P(("seq", "wt"), None),
        P(("seq", "wt"), None),
        P("seq", None, "wt"),
        P("seq", "wt"),
        P(("seq", "wt")),
        P(("seq", "wt")),
    )
    return jax.shard_map(shards, mesh=mesh, in_specs=in_specs, out_specs=out_specs, check_vma=False)
```

```python
import functools
import math

import jax
import jax.numpy as jnp
from jax import lax
from jax.experimental import pallas as pl
from jax.experimental.pallas import tpu as pltpu
from jax.sharding import PartitionSpec as P

H = 16
HD = 64


epsilon = 1e-05
rope_base = 160000.0
half_type = jnp.bfloat16


def ring_order(count):
    half = count // 2
    return [2 * p if p < half else 2 * (count - 1 - p) + 1 for p in range(count)]


def ring_pairs(count):
    order = ring_order(count)
    right = [(order[p], order[(p + 1) % count]) for p in range(count)]
    left = [(target, source) for source, target in right]
    return right, left


def cut_rows(rows):
    return rows // 32 * 16 if rows >= 32 else rows // 2


class Steps:
    def __init__(self, steps):
        self.steps = steps
        self.result = None
        self.pending = next(steps)

    def advance(self):
        try:
            self.pending = self.steps.send(self.pending)
        except StopIteration as ended:
            self.result = ended.value

    def tie(self, value):
        if self.result is None:
            self.pending, value = lax.optimization_barrier((self.pending, value))
            self.advance()
        return value

    def finish(self):
        while self.result is None:
            self.advance()
        return self.result


def ring_gather(block, axis="seq"):
    count = lax.axis_size(axis)
    right, left = ring_pairs(count)
    half = count // 2
    behind, ahead = [block], [block]
    for _ in range(1, half):
        got = yield (lax.ppermute(behind[-1], axis, right), lax.ppermute(ahead[-1], axis, left))
        behind.append(got[0])
        ahead.append(got[1])
    cut = cut_rows(block.shape[0])
    far = yield (
        lax.ppermute(behind[-1][:cut], axis, right),
        lax.ppermute(ahead[-1][cut:], axis, left),
    )
    far = jnp.concatenate(far, axis=0)
    return ahead[:half] + [far] + [behind[count - k] for k in range(half + 1, count)]


def ring_sum(parts, axis="seq"):
    count = lax.axis_size(axis)
    right, left = ring_pairs(count)
    half = count // 2
    cut = cut_rows(parts[0].shape[0])
    top, bottom = yield (
        lax.ppermute(parts[half][:cut].astype(half_type), axis, right),
        lax.ppermute(parts[half][cut:].astype(half_type), axis, left),
    )
    for off in range(half - 1, 0, -1):
        up = parts[off].astype(jnp.float32)
        down = parts[count - off].astype(jnp.float32)
        if off == half - 1:
            up = jnp.concatenate([up[:cut] + top.astype(jnp.float32), up[cut:]], axis=0)
            down = jnp.concatenate([down[:cut], down[cut:] + bottom.astype(jnp.float32)], axis=0)
        else:
            up = up + top.astype(jnp.float32)
            down = down + bottom.astype(jnp.float32)
        top, bottom = yield (
            lax.ppermute(up.astype(half_type), axis, right),
            lax.ppermute(down.astype(half_type), axis, left),
        )
    return parts[0].astype(jnp.float32) + top.astype(jnp.float32) + bottom.astype(jnp.float32)


def from_partner(value, axis, bit):
    mask = 2**bit
    pairs = [(source, source ^ mask) for source in range(lax.axis_size(axis))]
    return lax.ppermute(value, axis, pairs)


def bits_of(axis):
    return int(math.log2(lax.axis_size(axis)))


def cube_gather(block, axis="wt"):
    place = lax.axis_index(axis)
    bits = bits_of(axis)
    value = block
    for done, bit in enumerate(range(bits - 1, -1, -1)):
        other = from_partner(value, axis, bit)
        low = (place >> bit) % 2 == 0
        value = jnp.stack([jnp.where(low, value, other), jnp.where(low, other, value)], axis=done)
    return value.reshape((2**bits,) + block.shape)


def cube_sum(value, axis="wt"):
    place = lax.axis_index(axis)
    bits = bits_of(axis)
    value = value.reshape((2,) * bits + value.shape[1:])
    for bit in range(bits):
        at = bits - 1 - bit
        mine = (place >> bit) % 2
        keep = lax.dynamic_index_in_dim(value, mine, at, keepdims=False)
        give = lax.dynamic_index_in_dim(value, 1 - mine, at, keepdims=False)
        value = keep.astype(jnp.float32) + from_partner(give.astype(half_type), axis, bit).astype(
            jnp.float32
        )
    return value


def group_gather(rows, axis="wt"):
    for bit in range(bits_of(axis) - 1, -1, -1):
        rows = jnp.concatenate([rows, from_partner(rows, axis, bit)], axis=0)
    return rows


def group_sum(rows, held=(), axis="wt"):
    for bit in range(bits_of(axis)):
        half = rows.shape[0] // 2
        got = from_partner(rows[half:].astype(half_type), axis, bit)
        if bit == 0 and held:
            got, held = lax.optimization_barrier((got, held))
        rows = rows[:half].astype(jnp.float32) + got.astype(jnp.float32)
    return (rows, held) if held else rows


def normalize(features):
    average = jnp.mean(features, axis=-1, keepdims=True)
    centred = features - average
    spread = jnp.mean(centred * centred, axis=-1, keepdims=True)
    scale = lax.rsqrt(spread + epsilon)
    return centred * scale, scale


def normalize_back(d_unit, unit, scale):
    return scale * (
        d_unit
        - jnp.mean(d_unit, axis=-1, keepdims=True)
        - unit * jnp.mean(d_unit * unit, axis=-1, keepdims=True)
    )


def rotary_tables(positions, head_width):
    half_width = head_width // 2
    frequency = jnp.exp(
        jnp.arange(half_width).astype(jnp.float32) * (-2.0 * math.log(rope_base) / head_width)
    )
    angles = frequency[:, None] * positions[None, :]
    return jnp.cos(angles), jnp.sin(angles)


def rotate(vectors, cosine, sine_table):
    features, count = vectors.shape
    half_width = cosine.shape[0]
    split = vectors.reshape(features // (2 * half_width), 2, half_width, count)
    first, second = split[:, 0], split[:, 1]
    return jnp.stack(
        [first * cosine - second * sine_table, second * cosine + first * sine_table], axis=1
    ).reshape(features, count)


def exact_gelu(inner):
    return jax.nn.gelu(inner, approximate=False)


def dot_on(left, right, left_dim, right_dim):
    return lax.dot_general(
        left, right, (((left_dim,), (right_dim,)), ((), ())), preferred_element_type=jnp.float32
    )


def matmul(left, right):
    return jnp.dot(left, right, preferred_element_type=jnp.float32)


def head_rows(value, head):
    blank = jnp.zeros((HD, value.shape[1]), value.dtype)
    heads = value.shape[0] // HD
    if heads == 1:
        return value
    return jnp.concatenate(
        [value[h * HD : (h + 1) * HD] if h == head else blank for h in range(heads)], axis=0
    )


def head_columns(value, head):
    if value.shape[1] == HD:
        return value
    lane = lax.broadcasted_iota(jnp.int32, value.shape, 1)
    inside = (lane >= head * HD) & (lane < (head + 1) * HD)
    return jnp.where(inside, value, jnp.zeros_like(value))


def forward_kernel(at, q_ref, k_ref, vt_ref, w_ref, out_ref, lse_ref, branch_ref):
    features = w_ref.shape[0]
    count = out_ref.shape[1]
    length = k_ref.shape[0]
    span = math.gcd(length, 512)
    queries = q_ref[:, at : at + count]
    for head in range(features // HD):
        rows = slice(head * HD, (head + 1) * HD)
        query = head_rows(queries, head)
        top = total = accum = None
        for start in range(0, length, span):
            scores = matmul(k_ref[start : start + span, :], query)
            block_top = jnp.max(scores, axis=0, keepdims=True)
            new_top = block_top if top is None else jnp.maximum(top, block_top)
            raised = jnp.exp(scores - new_top)
            weight = jnp.sum(raised, axis=0, keepdims=True)
            part = matmul(vt_ref[rows, start : start + span], raised.astype(half_type))
            if top is None:
                total, accum = weight, part
            else:
                shrink = jnp.exp(top - new_top)
                total = total * shrink + weight
                accum = accum * shrink + part
            top = new_top
        out_ref[rows, :] = accum / total
        lse_ref[head : head + 1, :] = top + jnp.log(total)
    branch_ref[...] = dot_on(out_ref[...].astype(half_type), w_ref[...], 0, 0)


def backward_kernel(first, at, *refs):
    q_ref, qn_ref, near_ref, far_ref, w_ref, out_ref, lse_ref, k_ref, kt_ref, v_ref = refs[:10]
    dk_in, dv_in, gw_in = (None, None, None) if first else refs[10:13]
    dq_ref, dk_ref, dv_ref, gw_ref = refs[-4:]
    features, count = out_ref.shape
    length = k_ref.shape[0]
    span = math.gcd(length, 512)
    heads = features // HD
    weights = w_ref[...]
    blocks = [near_ref[...], far_ref[...]]
    d_out = jnp.concatenate([dot_on(weights, d, 1, 1) for d in blocks], axis=1).astype(half_type)
    d_out_rows = jnp.concatenate([dot_on(d, weights, 1, 1) for d in blocks], axis=0).astype(
        half_type
    )
    attended = out_ref[...].astype(half_type)
    rows = count // 2
    grad = matmul(attended[:, :rows], blocks[0]) + matmul(attended[:, rows:], blocks[1])
    gw_ref[...] = grad if first else gw_in[...] + grad
    queries = [head_rows(q_ref[:, at : at + count], h) for h in range(heads)]
    d_outs = [head_rows(d_out, h) for h in range(heads)]
    query_columns = [head_columns(qn_ref[at : at + count, :], h) for h in range(heads)]
    d_out_columns = [head_columns(d_out_rows, h) for h in range(heads)]
    weighed = d_out.astype(jnp.float32) * out_ref[...]
    deltas = [
        jnp.sum(weighed[h * HD : (h + 1) * HD], axis=0, keepdims=True) for h in range(heads)
    ]
    d_query = [None] * heads
    for start in range(0, length, span):
        stop = start + span
        d_key = None if first else dk_in[start:stop, :]
        d_value = None if first else dv_in[start:stop, :]
        for h in range(heads):
            scores = matmul(k_ref[start:stop, :], queries[h])
            probs = jnp.exp(scores - lse_ref[h : h + 1, :])
            d_probs = matmul(v_ref[start:stop, :], d_outs[h])
            d_scores = (probs * (d_probs - deltas[h])).astype(half_type)
            value_part = matmul(probs.astype(half_type), d_out_columns[h])
            key_part = matmul(d_scores, query_columns[h])
            d_value = value_part if d_value is None else d_value + value_part
            d_key = key_part if d_key is None else d_key + key_part
            part = matmul(kt_ref[h * HD : (h + 1) * HD, start:stop], d_scores)
            d_query[h] = part if d_query[h] is None else d_query[h] + part
        dk_ref[start:stop, :] = d_key
        dv_ref[start:stop, :] = d_value
    for h in range(heads):
        dq_ref[h * HD : (h + 1) * HD, :] = d_query[h] * (1.0 / math.sqrt(HD))


kernel_params = pltpu.CompilerParams(vmem_limit_bytes=20 * 2**20)


def attention_forward(at, count, queries, keys, values_t, weights):
    features = queries.shape[0]
    length = keys.shape[0]
    heads = features // HD
    return pl.pallas_call(
        functools.partial(forward_kernel, at),
        out_shape=(
            jax.ShapeDtypeStruct((features, count), jnp.float32),
            jax.ShapeDtypeStruct((heads, count), jnp.float32),
            jax.ShapeDtypeStruct((count, weights.shape[1]), jnp.float32),
        ),
        compiler_params=kernel_params,
        cost_estimate=pl.CostEstimate(
            flops=16 * features * count * length,
            bytes_accessed=4 * features * length + 6 * features * count,
            transcendentals=heads * count * length,
        ),
    )(queries, keys, values_t, weights)


def attention_backward(at, count, tensors, sums):
    queries, keys, weights = tensors[0], tensors[7], tensors[4]
    features = queries.shape[0]
    length = keys.shape[0]
    first = sums is None
    total = jax.ShapeDtypeStruct((length, features), jnp.float32)
    given = len(tensors)
    return pl.pallas_call(
        functools.partial(backward_kernel, first, at),
        out_shape=(
            jax.ShapeDtypeStruct((features, count), jnp.float32),
            total,
            total,
            jax.ShapeDtypeStruct(weights.shape, jnp.float32),
        ),
        input_output_aliases={} if first else {given + i: 1 + i for i in range(3)},
        compiler_params=kernel_params,
        cost_estimate=pl.CostEstimate(
            flops=40 * features * count * length,
            bytes_accessed=22 * features * length,
            transcendentals=features // HD * count * length,
        ),
    )(*tensors, *(sums or ()))


def shards(tokens, w_qkv, w_attn_out, w_in, w_mlp_out, gain_one, gain_two, cotangent):
    seq_tokens = tokens[0]
    seq_cot = cotangent[0]
    tok_rows, model_width = seq_tokens.shape
    seq_count = lax.axis_size("seq")
    wt_count = lax.axis_size("wt")
    seq_place = lax.axis_index("seq")
    wt_place = lax.axis_index("wt")
    half_place = wt_place % 2
    slice_len = tok_rows * seq_count
    local_heads = H // seq_count
    local_width = 3 * model_width // seq_count
    own_rows = w_qkv.shape[0]
    hidden_units = w_mlp_out.shape[1]
    score_scale = 1.0 / math.sqrt(HD)
    half_ring = seq_count // 2
    along, side = seq_place // 2, seq_place % 2
    ring_place = jnp.where(side == 0, along, seq_count - 1 - along)

    def ahead(k):
        at = (ring_place + k) % seq_count
        return jnp.where(at < half_ring, 2 * at, 2 * (seq_count - 1 - at) + 1)

    arrival = [0]
    for k in range(1, half_ring):
        arrival += [k, seq_count - k]
    arrival.append(half_ring)
    chunks = [tuple(arrival[c : c + 2]) for c in range(0, seq_count, 2)]
    span = 2 * tok_rows

    token_ring = Steps(ring_gather(seq_tokens))
    gain_own = gain_one.astype(jnp.float32)[:, None]
    scaled_qkv = (gain_own * w_qkv.astype(jnp.float32)).astype(half_type)
    scaled_qkv, gain_two = token_ring.tie((scaled_qkv, gain_two))
    token_blocks = token_ring.finish()
    qkv_pieces = lax.all_to_all(
        scaled_qkv.reshape(own_rows, seq_count, local_heads, 3, HD)
        .transpose(1, 0, 3, 2, 4)
        .reshape(seq_count, own_rows, local_width),
        "seq",
        split_axis=0,
        concat_axis=0,
        tiled=True,
    )
    qkv_heads = cube_gather(qkv_pieces).transpose(1, 0, 2, 3).reshape(model_width, local_width)
    gain_rows = cube_gather(gain_two.reshape(1, own_rows)).reshape(wt_count * own_rows)
    gain_rows = gain_rows.astype(jnp.float32)

    scaled_in = gain_rows[:, None, None] * w_in.astype(jnp.float32)
    mixed = jnp.concatenate(
        [
            scaled_in[:, 0].astype(half_type).T,
            scaled_in[:, 1].astype(half_type).T,
            w_mlp_out.T,
        ],
        axis=0,
    )
    mixed, seq_cot, w_attn_out, token_blocks[half_ring] = lax.optimization_barrier(
        (mixed, seq_cot, w_attn_out, token_blocks[half_ring])
    )
    mixed_ring = Steps(ring_gather(mixed))
    out_heads = cube_gather(w_attn_out).reshape(wt_count * own_rows, model_width)
    feed_rows = w_in.shape[0]
    group_cot = group_gather(seq_cot)

    units = [
        normalize(
            jnp.concatenate([token_blocks[k] for k in chunk], axis=0).astype(jnp.float32)
        )[0].astype(half_type)
        for chunk in chunks
    ]
    packed = jnp.concatenate([dot_on(qkv_heads, unit, 0, 1) for unit in units], axis=1)
    positions = jnp.concatenate(
        [half_place * slice_len + ahead(k) * tok_rows + jnp.arange(tok_rows) for k in arrival]
    ).astype(jnp.float32)
    cosine, sine_table = rotary_tables(positions, HD)
    third = local_width // 3
    queries = (rotate(packed[:third], cosine, sine_table).astype(half_type) * score_scale).astype(
        half_type
    )
    own_pairs = jnp.concatenate(
        [rotate(packed[third : 2 * third], cosine, sine_table), packed[2 * third :]], axis=0
    ).astype(half_type)
    pairs = jnp.concatenate([own_pairs, from_partner(own_pairs, "wt", 0)], axis=1)
    keys_t, values_t = pairs[:third], pairs[third:]
    keys, values = keys_t.T, values_t.T

    attended, log_totals, parts = {}, {}, {}
    for c in range(len(chunks) - 1, -1, -1):
        attended[c], log_totals[c], branch = attention_forward(
            c * span, span, queries, keys, values_t, out_heads
        )
        for at, k in enumerate(chunks[c]):
            parts[k] = branch[at * tok_rows : (at + 1) * tok_rows]
    in_rows = jnp.zeros((2 * hidden_units, model_width), half_type)
    out_rows = jnp.zeros((hidden_units, model_width), half_type)
    for k, block in enumerate(mixed_ring.finish()):
        at = (0, ahead(k) * feed_rows)
        in_rows = lax.dynamic_update_slice(in_rows, block[: 2 * hidden_units], at)
        out_rows = lax.dynamic_update_slice(out_rows, block[2 * hidden_units :], at)
    inputs = seq_tokens.astype(jnp.float32)
    middle = inputs + Steps(ring_sum([parts[k] for k in range(seq_count)])).finish()
    unit_two, scale_two = normalize(middle)
    group_unit = group_gather(unit_two.astype(half_type))

    projected = dot_on(in_rows, group_unit, 1, 1)
    activated, gelu_pull = jax.vjp(exact_gelu, projected[:hidden_units])
    gate = projected[hidden_units:]
    hidden = (activated * gate).astype(half_type)
    d_hidden = dot_on(out_rows, group_cot, 1, 1)
    d_projected = jnp.concatenate(
        [gelu_pull(d_hidden * gate)[0], d_hidden * activated], axis=0
    ).astype(half_type)
    d_unit_rows, d_projected, hidden = lax.optimization_barrier(
        (dot_on(d_projected, in_rows, 0, 0), d_projected, hidden)
    )
    grad_mixed = jnp.concatenate(
        [dot_on(d_projected, group_unit, 1, 0), dot_on(hidden, group_cot, 1, 0)], axis=0
    ).astype(half_type)
    d_unit_two, (grad_mixed,) = group_sum(d_unit_rows, (grad_mixed,))
    d_middle = seq_cot.astype(jnp.float32) + normalize_back(d_unit_two, unit_two, scale_two)
    d_branch = d_middle.astype(half_type)
    mlp_rows = dot_on(hidden, out_rows, 0, 0)
    grad_ring = Steps(ring_sum(
        [
            lax.dynamic_slice(
                grad_mixed, (0, ahead(k) * feed_rows), (3 * hidden_units, feed_rows)
            )
            for k in range(seq_count)
        ]
    ))
    d_ring = Steps(ring_gather(d_branch))
    for _ in range(2):
        d_ring.pending = grad_ring.tie(d_ring.pending)
        d_ring.advance()
    d_blocks = d_ring.finish()
    query_rows = queries.T
    d_queries, sums = [], None
    for c, (near, far) in enumerate(chunks):
        d_query, *sums = attention_backward(
            c * span,
            span,
            (
                queries,
                query_rows,
                d_blocks[near],
                d_blocks[far],
                out_heads,
                attended[c],
                log_totals[c],
                keys,
                keys_t,
                values,
            ),
            sums,
        )
        d_queries.append(d_query)
        if c == len(chunks) - 2:
            sums, mlp_rows = grad_ring.tie((sums, mlp_rows))
    d_query = jnp.concatenate(d_queries, axis=1)
    output = (middle + group_sum(mlp_rows)).astype(half_type)
    *sums, grad_out = sums

    mixed_owned = grad_ring.finish()
    in_unscaled = jnp.stack(
        [mixed_owned[:hidden_units].T, mixed_owned[hidden_units : 2 * hidden_units].T], axis=1
    )
    in_owned = in_unscaled * gain_rows[:, None, None]
    mlp_owned = mixed_owned[2 * hidden_units :].T
    gain_two_part = jnp.sum(in_unscaled * w_in.astype(jnp.float32), axis=(1, 2))

    d_pairs = jnp.concatenate(sums, axis=1).T
    d_own = d_pairs[:, :slice_len] + from_partner(
        d_pairs[:, slice_len:].astype(half_type), "wt", 0
    ).astype(jnp.float32)
    d_packed = jnp.concatenate(
        [
            rotate(d_query, cosine, -sine_table),
            rotate(d_own[:third], cosine, -sine_table),
            d_own[third:],
        ],
        axis=0,
    ).astype(half_type)
    grad_heads = dot_on(jnp.concatenate(units, axis=0), d_packed, 0, 1).reshape(
        seq_count, wt_count, own_rows, local_width
    )
    grad_pieces = cube_sum(grad_heads.transpose(1, 0, 2, 3)).astype(half_type)
    d_unit_parts = dot_on(d_packed, qkv_heads, 0, 1)
    last_ring = Steps(ring_sum(
        [
            d_unit_parts[at * tok_rows : (at + 1) * tok_rows]
            for at in (arrival.index(k) for k in range(seq_count))
        ]
    ))
    for _ in range(half_ring - 3):
        last_ring.advance()
    grad_pieces = last_ring.tie(grad_pieces)
    gain_two_part, grad_out = last_ring.tie((gain_two_part, grad_out))
    attn_owned = cube_sum(grad_out.reshape(wt_count, own_rows, model_width))
    gain_two_owned = cube_sum(gain_two_part.reshape(wt_count, 1, own_rows)).reshape(own_rows)
    d_unit = last_ring.finish()
    unit_one, scale_one = normalize(inputs)
    input_grad = (d_middle + normalize_back(d_unit, unit_one, scale_one)).astype(half_type)
    grad_rows = lax.all_to_all(grad_pieces, "seq", split_axis=0, concat_axis=0, tiled=True)
    qkv_unscaled = (
        grad_rows.reshape(seq_count, own_rows, 3, local_heads, HD)
        .transpose(1, 0, 3, 2, 4)
        .reshape(own_rows, 3 * model_width)
        .astype(jnp.float32)
    )
    qkv_owned = qkv_unscaled * gain_own
    gain_one_owned = jnp.sum(qkv_unscaled * w_qkv.astype(jnp.float32), axis=1)
    return (
        output.reshape(1, tok_rows, model_width),
        input_grad.reshape(1, tok_rows, model_width),
        qkv_owned,
        attn_owned,
        in_owned,
        mlp_owned,
        gain_one_owned,
        gain_two_owned,
    )


def solution(mesh):
    in_specs = (
        P("wt", "seq", None),
        P(("seq", "wt"), None),
        P(("seq", "wt"), None),
        P("seq", None, "wt"),
        P("seq", "wt"),
        P(("seq", "wt")),
        P(("seq", "wt")),
        P("wt", "seq", None),
    )
    out_specs = (
        P("wt", "seq", None),
        P("wt", "seq", None),
        P(("seq", "wt"), None),
        P(("seq", "wt"), None),
        P("seq", None, "wt"),
        P("seq", "wt"),
        P(("seq", "wt")),
        P(("seq", "wt")),
    )
    return jax.shard_map(shards, mesh=mesh, in_specs=in_specs, out_specs=out_specs, check_vma=False)
```

```python
import functools
import math

import jax
import jax.numpy as jnp
from jax import lax
from jax.experimental import pallas as pl
from jax.experimental.pallas import tpu as pltpu
from jax.sharding import PartitionSpec as P

H = 16
HD = 64


epsilon = 1e-05
rope_base = 160000.0
half_type = jnp.bfloat16


def ring_order(count):
    half = count // 2
    return [2 * p if p < half else 2 * (count - 1 - p) + 1 for p in range(count)]


def ring_pairs(count):
    order = ring_order(count)
    right = [(order[p], order[(p + 1) % count]) for p in range(count)]
    left = [(target, source) for source, target in right]
    return right, left


def cut_rows(rows):
    return rows // 32 * 16 if rows >= 32 else rows // 2


class Steps:
    def __init__(self, steps):
        self.steps = steps
        self.result = None
        self.pending = next(steps)

    def advance(self):
        try:
            self.pending = self.steps.send(self.pending)
        except StopIteration as ended:
            self.result = ended.value

    def tie(self, value):
        if self.result is None:
            self.pending, value = lax.optimization_barrier((self.pending, value))
            self.advance()
        return value

    def finish(self):
        while self.result is None:
            self.advance()
        return self.result


def ring_gather(block, axis="seq"):
    count = lax.axis_size(axis)
    right, left = ring_pairs(count)
    half = count // 2
    behind, ahead = [block], [block]
    for _ in range(1, half):
        got = yield (lax.ppermute(behind[-1], axis, right), lax.ppermute(ahead[-1], axis, left))
        behind.append(got[0])
        ahead.append(got[1])
    cut = cut_rows(block.shape[0])
    far = yield (
        lax.ppermute(behind[-1][:cut], axis, right),
        lax.ppermute(ahead[-1][cut:], axis, left),
    )
    far = jnp.concatenate(far, axis=0)
    return ahead[:half] + [far] + [behind[count - k] for k in range(half + 1, count)]


def ring_sum(parts, axis="seq"):
    count = lax.axis_size(axis)
    right, left = ring_pairs(count)
    half = count // 2
    cut = cut_rows(parts[0].shape[0])
    top, bottom = yield (
        lax.ppermute(parts[half][:cut].astype(half_type), axis, right),
        lax.ppermute(parts[half][cut:].astype(half_type), axis, left),
    )
    for off in range(half - 1, 0, -1):
        up = parts[off].astype(jnp.float32)
        down = parts[count - off].astype(jnp.float32)
        if off == half - 1:
            up = jnp.concatenate([up[:cut] + top.astype(jnp.float32), up[cut:]], axis=0)
            down = jnp.concatenate([down[:cut], down[cut:] + bottom.astype(jnp.float32)], axis=0)
        else:
            up = up + top.astype(jnp.float32)
            down = down + bottom.astype(jnp.float32)
        top, bottom = yield (
            lax.ppermute(up.astype(half_type), axis, right),
            lax.ppermute(down.astype(half_type), axis, left),
        )
    return parts[0].astype(jnp.float32) + top.astype(jnp.float32) + bottom.astype(jnp.float32)


def from_partner(value, axis, bit):
    mask = 2**bit
    pairs = [(source, source ^ mask) for source in range(lax.axis_size(axis))]
    return lax.ppermute(value, axis, pairs)


def bits_of(axis):
    return int(math.log2(lax.axis_size(axis)))


def cube_gather(block, axis="wt"):
    place = lax.axis_index(axis)
    bits = bits_of(axis)
    value = block
    for done, bit in enumerate(range(bits - 1, -1, -1)):
        other = from_partner(value, axis, bit)
        low = (place >> bit) % 2 == 0
        value = jnp.stack([jnp.where(low, value, other), jnp.where(low, other, value)], axis=done)
    return value.reshape((2**bits,) + block.shape)


def cube_sum(value, axis="wt"):
    place = lax.axis_index(axis)
    bits = bits_of(axis)
    value = value.reshape((2,) * bits + value.shape[1:])
    for bit in range(bits):
        at = bits - 1 - bit
        mine = (place >> bit) % 2
        keep = lax.dynamic_index_in_dim(value, mine, at, keepdims=False)
        give = lax.dynamic_index_in_dim(value, 1 - mine, at, keepdims=False)
        value = keep.astype(jnp.float32) + from_partner(give.astype(half_type), axis, bit).astype(
            jnp.float32
        )
    return value


def group_gather(rows, axis="wt"):
    for bit in range(bits_of(axis) - 1, -1, -1):
        rows = jnp.concatenate([rows, from_partner(rows, axis, bit)], axis=0)
    return rows


def group_sum(rows, axis="wt"):
    for bit in range(bits_of(axis)):
        half = rows.shape[0] // 2
        got = from_partner(rows[half:].astype(half_type), axis, bit)
        rows = rows[:half].astype(jnp.float32) + got.astype(jnp.float32)
    return rows


def normalize(features):
    average = jnp.mean(features, axis=-1, keepdims=True)
    centred = features - average
    spread = jnp.mean(centred * centred, axis=-1, keepdims=True)
    scale = lax.rsqrt(spread + epsilon)
    return centred * scale, scale


def normalize_back(d_unit, unit, scale):
    return scale * (
        d_unit
        - jnp.mean(d_unit, axis=-1, keepdims=True)
        - unit * jnp.mean(d_unit * unit, axis=-1, keepdims=True)
    )


def rotary_tables(positions, head_width):
    half_width = head_width // 2
    frequency = jnp.exp(
        jnp.arange(half_width).astype(jnp.float32) * (-2.0 * math.log(rope_base) / head_width)
    )
    angles = frequency[:, None] * positions[None, :]
    return jnp.cos(angles), jnp.sin(angles)


def rotate(vectors, cosine, sine_table):
    features, count = vectors.shape
    half_width = cosine.shape[0]
    split = vectors.reshape(features // (2 * half_width), 2, half_width, count)
    first, second = split[:, 0], split[:, 1]
    return jnp.stack(
        [first * cosine - second * sine_table, second * cosine + first * sine_table], axis=1
    ).reshape(features, count)


def exact_gelu(inner):
    return jax.nn.gelu(inner, approximate=False)


def dot_on(left, right, left_dim, right_dim):
    return lax.dot_general(
        left, right, (((left_dim,), (right_dim,)), ((), ())), preferred_element_type=jnp.float32
    )


def matmul(left, right):
    return jnp.dot(left, right, preferred_element_type=jnp.float32)


def head_rows(value, head):
    blank = jnp.zeros((HD, value.shape[1]), value.dtype)
    heads = value.shape[0] // HD
    if heads == 1:
        return value
    return jnp.concatenate(
        [value[h * HD : (h + 1) * HD] if h == head else blank for h in range(heads)], axis=0
    )


def head_columns(value, head):
    if value.shape[1] == HD:
        return value
    lane = lax.broadcasted_iota(jnp.int32, value.shape, 1)
    inside = (lane >= head * HD) & (lane < (head + 1) * HD)
    return jnp.where(inside, value, jnp.zeros_like(value))


def forward_kernel(at, q_ref, k_ref, vt_ref, w_ref, out_ref, lse_ref, branch_ref):
    features = w_ref.shape[0]
    count = out_ref.shape[1]
    length = k_ref.shape[0]
    span = math.gcd(length, 512)
    queries = q_ref[:, at : at + count]
    for head in range(features // HD):
        rows = slice(head * HD, (head + 1) * HD)
        query = head_rows(queries, head)
        top = total = accum = None
        for start in range(0, length, span):
            scores = matmul(k_ref[start : start + span, :], query)
            block_top = jnp.max(scores, axis=0, keepdims=True)
            new_top = block_top if top is None else jnp.maximum(top, block_top)
            raised = jnp.exp(scores - new_top)
            weight = jnp.sum(raised, axis=0, keepdims=True)
            part = matmul(vt_ref[rows, start : start + span], raised.astype(half_type))
            if top is None:
                total, accum = weight, part
            else:
                shrink = jnp.exp(top - new_top)
                total = total * shrink + weight
                accum = accum * shrink + part
            top = new_top
        out_ref[rows, :] = accum / total
        lse_ref[head : head + 1, :] = top + jnp.log(total)
    branch_ref[...] = dot_on(out_ref[...].astype(half_type), w_ref[...], 0, 0)


def backward_kernel(first, at, *refs):
    q_ref, qn_ref, near_ref, far_ref, w_ref, out_ref, lse_ref, k_ref, kt_ref, v_ref = refs[:10]
    dk_in, dv_in, gw_in = (None, None, None) if first else refs[10:13]
    dq_ref, dk_ref, dv_ref, gw_ref = refs[-4:]
    features, count = out_ref.shape
    length = k_ref.shape[0]
    span = math.gcd(length, 512)
    heads = features // HD
    weights = w_ref[...]
    blocks = [near_ref[...], far_ref[...]]
    d_out = jnp.concatenate([dot_on(weights, d, 1, 1) for d in blocks], axis=1).astype(half_type)
    d_out_rows = jnp.concatenate([dot_on(d, weights, 1, 1) for d in blocks], axis=0).astype(
        half_type
    )
    attended = out_ref[...].astype(half_type)
    rows = count // 2
    grad = matmul(attended[:, :rows], blocks[0]) + matmul(attended[:, rows:], blocks[1])
    gw_ref[...] = grad if first else gw_in[...] + grad
    queries = [head_rows(q_ref[:, at : at + count], h) for h in range(heads)]
    d_outs = [head_rows(d_out, h) for h in range(heads)]
    query_columns = [head_columns(qn_ref[at : at + count, :], h) for h in range(heads)]
    d_out_columns = [head_columns(d_out_rows, h) for h in range(heads)]
    weighed = d_out.astype(jnp.float32) * out_ref[...]
    deltas = [
        jnp.sum(weighed[h * HD : (h + 1) * HD], axis=0, keepdims=True) for h in range(heads)
    ]
    d_query = [None] * heads
    for start in range(0, length, span):
        stop = start + span
        d_key = None if first else dk_in[start:stop, :]
        d_value = None if first else dv_in[start:stop, :]
        for h in range(heads):
            scores = matmul(k_ref[start:stop, :], queries[h])
            probs = jnp.exp(scores - lse_ref[h : h + 1, :])
            d_probs = matmul(v_ref[start:stop, :], d_outs[h])
            d_scores = (probs * (d_probs - deltas[h])).astype(half_type)
            value_part = matmul(probs.astype(half_type), d_out_columns[h])
            key_part = matmul(d_scores, query_columns[h])
            d_value = value_part if d_value is None else d_value + value_part
            d_key = key_part if d_key is None else d_key + key_part
            part = matmul(kt_ref[h * HD : (h + 1) * HD, start:stop], d_scores)
            d_query[h] = part if d_query[h] is None else d_query[h] + part
        dk_ref[start:stop, :] = d_key
        dv_ref[start:stop, :] = d_value
    for h in range(heads):
        dq_ref[h * HD : (h + 1) * HD, :] = d_query[h] * (1.0 / math.sqrt(HD))


kernel_params = pltpu.CompilerParams(vmem_limit_bytes=20 * 2**20)


def attention_forward(at, count, queries, keys, values_t, weights):
    features = queries.shape[0]
    length = keys.shape[0]
    heads = features // HD
    return pl.pallas_call(
        functools.partial(forward_kernel, at),
        out_shape=(
            jax.ShapeDtypeStruct((features, count), jnp.float32),
            jax.ShapeDtypeStruct((heads, count), jnp.float32),
            jax.ShapeDtypeStruct((count, weights.shape[1]), jnp.float32),
        ),
        compiler_params=kernel_params,
        cost_estimate=pl.CostEstimate(
            flops=16 * features * count * length,
            bytes_accessed=4 * features * length + 6 * features * count,
            transcendentals=heads * count * length,
        ),
    )(queries, keys, values_t, weights)


def attention_backward(at, count, tensors, sums):
    queries, keys, weights = tensors[0], tensors[7], tensors[4]
    features = queries.shape[0]
    length = keys.shape[0]
    first = sums is None
    total = jax.ShapeDtypeStruct((length, features), jnp.float32)
    given = len(tensors)
    return pl.pallas_call(
        functools.partial(backward_kernel, first, at),
        out_shape=(
            jax.ShapeDtypeStruct((features, count), jnp.float32),
            total,
            total,
            jax.ShapeDtypeStruct(weights.shape, jnp.float32),
        ),
        input_output_aliases={} if first else {given + i: 1 + i for i in range(3)},
        compiler_params=kernel_params,
        cost_estimate=pl.CostEstimate(
            flops=40 * features * count * length,
            bytes_accessed=22 * features * length,
            transcendentals=features // HD * count * length,
        ),
    )(*tensors, *(sums or ()))


def shards(tokens, w_qkv, w_attn_out, w_in, w_mlp_out, gain_one, gain_two, cotangent):
    seq_tokens = tokens[0]
    seq_cot = cotangent[0]
    tok_rows, model_width = seq_tokens.shape
    seq_count = lax.axis_size("seq")
    wt_count = lax.axis_size("wt")
    seq_place = lax.axis_index("seq")
    wt_place = lax.axis_index("wt")
    half_place = wt_place % 2
    slice_len = tok_rows * seq_count
    local_heads = H // seq_count
    local_width = 3 * model_width // seq_count
    own_rows = w_qkv.shape[0]
    hidden_units = w_mlp_out.shape[1]
    score_scale = 1.0 / math.sqrt(HD)
    half_ring = seq_count // 2
    along, side = seq_place // 2, seq_place % 2
    ring_place = jnp.where(side == 0, along, seq_count - 1 - along)

    def ahead(k):
        at = (ring_place + k) % seq_count
        return jnp.where(at < half_ring, 2 * at, 2 * (seq_count - 1 - at) + 1)

    arrival = [0]
    for k in range(1, half_ring):
        arrival += [k, seq_count - k]
    arrival.append(half_ring)
    chunks = [tuple(arrival[c : c + 2]) for c in range(0, seq_count, 2)]
    span = 2 * tok_rows

    token_ring = Steps(ring_gather(seq_tokens))
    gain_own = gain_one.astype(jnp.float32)[:, None]
    scaled_qkv = (gain_own * w_qkv.astype(jnp.float32)).astype(half_type)
    scaled_qkv, gain_two = token_ring.tie((scaled_qkv, gain_two))
    w_attn_out, late_cot = token_ring.tie((w_attn_out, seq_cot))
    token_blocks = token_ring.finish()
    qkv_pieces = lax.all_to_all(
        scaled_qkv.reshape(own_rows, seq_count, local_heads, 3, HD)
        .transpose(1, 0, 3, 2, 4)
        .reshape(seq_count, own_rows, local_width),
        "seq",
        split_axis=0,
        concat_axis=0,
        tiled=True,
    )
    qkv_heads = cube_gather(qkv_pieces).transpose(1, 0, 2, 3).reshape(model_width, local_width)
    out_heads = cube_gather(w_attn_out).reshape(wt_count * own_rows, model_width)
    gain_rows = cube_gather(gain_two.reshape(1, own_rows)).reshape(wt_count * own_rows)
    gain_rows = gain_rows.astype(jnp.float32)

    scaled_in = gain_rows[:, None, None] * w_in.astype(jnp.float32)
    mixed = jnp.concatenate(
        [
            scaled_in[:, 0].astype(half_type).T,
            scaled_in[:, 1].astype(half_type).T,
            w_mlp_out.T,
        ],
        axis=0,
    )
    mixed, token_blocks[half_ring] = lax.optimization_barrier((mixed, token_blocks[half_ring]))
    feed_rows = w_in.shape[0]
    in_rows = jnp.zeros((2 * hidden_units, model_width), half_type)
    out_rows = jnp.zeros((hidden_units, model_width), half_type)
    for k, block in enumerate(Steps(ring_gather(mixed)).finish()):
        at = (0, ahead(k) * feed_rows)
        in_rows = lax.dynamic_update_slice(in_rows, block[: 2 * hidden_units], at)
        out_rows = lax.dynamic_update_slice(out_rows, block[2 * hidden_units :], at)
    group_cot = group_gather(late_cot)

    units = [
        normalize(
            jnp.concatenate([token_blocks[k] for k in chunk], axis=0).astype(jnp.float32)
        )[0].astype(half_type)
        for chunk in chunks
    ]
    packed = jnp.concatenate([dot_on(qkv_heads, unit, 0, 1) for unit in units], axis=1)
    positions = jnp.concatenate(
        [half_place * slice_len + ahead(k) * tok_rows + jnp.arange(tok_rows) for k in arrival]
    ).astype(jnp.float32)
    cosine, sine_table = rotary_tables(positions, HD)
    third = local_width // 3
    queries = (rotate(packed[:third], cosine, sine_table).astype(half_type) * score_scale).astype(
        half_type
    )
    own_pairs = jnp.concatenate(
        [rotate(packed[third : 2 * third], cosine, sine_table), packed[2 * third :]], axis=0
    ).astype(half_type)
    pairs = jnp.concatenate([own_pairs, from_partner(own_pairs, "wt", 0)], axis=1)
    keys_t, values_t = pairs[:third], pairs[third:]
    keys, values = keys_t.T, values_t.T

    attended, log_totals, parts = {}, {}, {}
    for c in range(len(chunks) - 1, -1, -1):
        attended[c], log_totals[c], branch = attention_forward(
            c * span, span, queries, keys, values_t, out_heads
        )
        for at, k in enumerate(chunks[c]):
            parts[k] = branch[at * tok_rows : (at + 1) * tok_rows]
    inputs = seq_tokens.astype(jnp.float32)
    middle = inputs + Steps(ring_sum([parts[k] for k in range(seq_count)])).finish()
    unit_two, scale_two = normalize(middle)
    group_unit = group_gather(unit_two.astype(half_type))

    projected = dot_on(in_rows, group_unit, 1, 1)
    activated, gelu_pull = jax.vjp(exact_gelu, projected[:hidden_units])
    gate = projected[hidden_units:]
    hidden = (activated * gate).astype(half_type)
    d_hidden = dot_on(out_rows, group_cot, 1, 1)
    d_projected = jnp.concatenate(
        [gelu_pull(d_hidden * gate)[0], d_hidden * activated], axis=0
    ).astype(half_type)
    d_unit_rows, d_projected, hidden = lax.optimization_barrier(
        (dot_on(d_projected, in_rows, 0, 0), d_projected, hidden)
    )
    d_unit_two = group_sum(d_unit_rows)
    d_middle = seq_cot.astype(jnp.float32) + normalize_back(d_unit_two, unit_two, scale_two)
    d_branch, mlp_rows = lax.optimization_barrier(
        (d_middle.astype(half_type), dot_on(hidden, out_rows, 0, 0))
    )
    d_blocks = Steps(ring_gather(d_branch)).finish()
    output = (middle + group_sum(mlp_rows)).astype(half_type)
    query_rows = queries.T
    d_queries, sums = [], None
    for c, (near, far) in enumerate(chunks):
        d_query, *sums = attention_backward(
            c * span,
            span,
            (
                queries,
                query_rows,
                d_blocks[near],
                d_blocks[far],
                out_heads,
                attended[c],
                log_totals[c],
                keys,
                keys_t,
                values,
            ),
            sums,
        )
        d_queries.append(d_query)
    d_query = jnp.concatenate(d_queries, axis=1)
    *sums, grad_out = sums

    grad_mixed = jnp.concatenate(
        [dot_on(d_projected, group_unit, 1, 0), dot_on(hidden, group_cot, 1, 0)], axis=0
    ).astype(half_type)
    mixed_owned = Steps(ring_sum(
        [
            lax.dynamic_slice(
                grad_mixed, (0, ahead(k) * feed_rows), (3 * hidden_units, feed_rows)
            )
            for k in range(seq_count)
        ]
    )).finish()
    sums, mixed_owned = lax.optimization_barrier((sums, mixed_owned))
    in_unscaled = jnp.stack(
        [mixed_owned[:hidden_units].T, mixed_owned[hidden_units : 2 * hidden_units].T], axis=1
    )
    in_owned = in_unscaled * gain_rows[:, None, None]
    mlp_owned = mixed_owned[2 * hidden_units :].T
    gain_two_part = jnp.sum(in_unscaled * w_in.astype(jnp.float32), axis=(1, 2))

    d_pairs = jnp.concatenate(sums, axis=1).T
    d_own = d_pairs[:, :slice_len] + from_partner(
        d_pairs[:, slice_len:].astype(half_type), "wt", 0
    ).astype(jnp.float32)
    d_packed = jnp.concatenate(
        [
            rotate(d_query, cosine, -sine_table),
            rotate(d_own[:third], cosine, -sine_table),
            d_own[third:],
        ],
        axis=0,
    ).astype(half_type)
    grad_heads = dot_on(jnp.concatenate(units, axis=0), d_packed, 0, 1).reshape(
        seq_count, wt_count, own_rows, local_width
    )
    grad_pieces = cube_sum(grad_heads.transpose(1, 0, 2, 3)).astype(half_type)
    d_unit_parts = dot_on(d_packed, qkv_heads, 0, 1)
    last_ring = Steps(ring_sum(
        [
            d_unit_parts[at * tok_rows : (at + 1) * tok_rows]
            for at in (arrival.index(k) for k in range(seq_count))
        ]
    ))
    for _ in range(half_ring - 3):
        last_ring.advance()
    grad_pieces = last_ring.tie(grad_pieces)
    gain_two_part, grad_out = last_ring.tie((gain_two_part, grad_out))
    attn_owned = cube_sum(grad_out.reshape(wt_count, own_rows, model_width))
    gain_two_owned = cube_sum(gain_two_part.reshape(wt_count, 1, own_rows)).reshape(own_rows)
    d_unit = last_ring.finish()
    unit_one, scale_one = normalize(inputs)
    input_grad = (d_middle + normalize_back(d_unit, unit_one, scale_one)).astype(half_type)
    grad_rows = lax.all_to_all(grad_pieces, "seq", split_axis=0, concat_axis=0, tiled=True)
    qkv_unscaled = (
        grad_rows.reshape(seq_count, own_rows, 3, local_heads, HD)
        .transpose(1, 0, 3, 2, 4)
        .reshape(own_rows, 3 * model_width)
        .astype(jnp.float32)
    )
    qkv_owned = qkv_unscaled * gain_own
    gain_one_owned = jnp.sum(qkv_unscaled * w_qkv.astype(jnp.float32), axis=1)
    return (
        output.reshape(1, tok_rows, model_width),
        input_grad.reshape(1, tok_rows, model_width),
        qkv_owned,
        attn_owned,
        in_owned,
        mlp_owned,
        gain_one_owned,
        gain_two_owned,
    )


def solution(mesh):
    in_specs = (
        P("wt", "seq", None),
        P(("seq", "wt"), None),
        P(("seq", "wt"), None),
        P("seq", None, "wt"),
        P("seq", "wt"),
        P(("seq", "wt")),
        P(("seq", "wt")),
        P("wt", "seq", None),
    )
    out_specs = (
        P("wt", "seq", None),
        P("wt", "seq", None),
        P(("seq", "wt"), None),
        P(("seq", "wt"), None),
        P("seq", None, "wt"),
        P("seq", "wt"),
        P(("seq", "wt")),
        P(("seq", "wt")),
    )
    return jax.shard_map(shards, mesh=mesh, in_specs=in_specs, out_specs=out_specs, check_vma=False)
```

```python
import functools
import math

import jax
import jax.numpy as jnp
from jax import lax
from jax.experimental import pallas as pl
from jax.experimental.pallas import tpu as pltpu
from jax.sharding import PartitionSpec as P

H = 16
HD = 64


epsilon = 1e-05
rope_base = 160000.0
half_type = jnp.bfloat16


def ring_order(count):
    half = count // 2
    return [2 * p if p < half else 2 * (count - 1 - p) + 1 for p in range(count)]


def ring_pairs(count):
    order = ring_order(count)
    right = [(order[p], order[(p + 1) % count]) for p in range(count)]
    left = [(target, source) for source, target in right]
    return right, left


def cut_rows(rows):
    return rows // 32 * 16 if rows >= 32 else rows // 2


def ring_gather(block, held=(), axis="seq"):
    count = lax.axis_size(axis)
    right, left = ring_pairs(count)
    half = count // 2
    behind, ahead = [block], [block]
    for step in range(1, half):
        behind.append(lax.ppermute(behind[-1], axis, right))
        ahead.append(lax.ppermute(ahead[-1], axis, left))
        if step == 1 and held:
            behind[1], ahead[1], held = lax.optimization_barrier((behind[1], ahead[1], held))
    cut = cut_rows(block.shape[0])
    far = jnp.concatenate(
        [
            lax.ppermute(behind[-1][:cut], axis, right),
            lax.ppermute(ahead[-1][cut:], axis, left),
        ],
        axis=0,
    )
    blocks = ahead[:half] + [far] + [behind[count - k] for k in range(half + 1, count)]
    return (blocks, held) if held else blocks


def ring_sum(parts, held=(), axis="seq"):
    count = lax.axis_size(axis)
    right, left = ring_pairs(count)
    half = count // 2
    cut = cut_rows(parts[0].shape[0])
    top = lax.ppermute(parts[half][:cut].astype(half_type), axis, right)
    bottom = lax.ppermute(parts[half][cut:].astype(half_type), axis, left)
    for off in range(half - 1, 0, -1):
        up = parts[off].astype(jnp.float32)
        down = parts[count - off].astype(jnp.float32)
        if off == half - 1:
            up = jnp.concatenate([up[:cut] + top.astype(jnp.float32), up[cut:]], axis=0)
            down = jnp.concatenate([down[:cut], down[cut:] + bottom.astype(jnp.float32)], axis=0)
        else:
            up = up + top.astype(jnp.float32)
            down = down + bottom.astype(jnp.float32)
        up, down = up.astype(half_type), down.astype(half_type)
        if off == 2 and held:
            up, down, held = lax.optimization_barrier((up, down, held))
        top = lax.ppermute(up, axis, right)
        bottom = lax.ppermute(down, axis, left)
    total = parts[0].astype(jnp.float32) + top.astype(jnp.float32) + bottom.astype(jnp.float32)
    return (total, held) if held else total


class Steps:
    def __init__(self, steps):
        self.steps = steps
        self.result = None
        self.pending = next(steps)

    def advance(self):
        try:
            self.pending = self.steps.send(self.pending)
        except StopIteration as ended:
            self.result = ended.value

    def tie(self, value):
        if self.result is None:
            self.pending, value = lax.optimization_barrier((self.pending, value))
            self.advance()
        return value

    def finish(self):
        while self.result is None:
            self.advance()
        return self.result


def ring_sum_steps(parts, axis="seq"):
    count = lax.axis_size(axis)
    right, left = ring_pairs(count)
    half = count // 2
    cut = cut_rows(parts[0].shape[0])
    top, bottom = yield (
        lax.ppermute(parts[half][:cut].astype(half_type), axis, right),
        lax.ppermute(parts[half][cut:].astype(half_type), axis, left),
    )
    for off in range(half - 1, 0, -1):
        up = parts[off].astype(jnp.float32)
        down = parts[count - off].astype(jnp.float32)
        if off == half - 1:
            up = jnp.concatenate([up[:cut] + top.astype(jnp.float32), up[cut:]], axis=0)
            down = jnp.concatenate([down[:cut], down[cut:] + bottom.astype(jnp.float32)], axis=0)
        else:
            up = up + top.astype(jnp.float32)
            down = down + bottom.astype(jnp.float32)
        top, bottom = yield (
            lax.ppermute(up.astype(half_type), axis, right),
            lax.ppermute(down.astype(half_type), axis, left),
        )
    return parts[0].astype(jnp.float32) + top.astype(jnp.float32) + bottom.astype(jnp.float32)


def from_partner(value, axis, bit):
    mask = 2**bit
    pairs = [(source, source ^ mask) for source in range(lax.axis_size(axis))]
    return lax.ppermute(value, axis, pairs)


def bits_of(axis):
    return int(math.log2(lax.axis_size(axis)))


def cube_gather(block, axis="wt"):
    place = lax.axis_index(axis)
    bits = bits_of(axis)
    value = block
    for done, bit in enumerate(range(bits - 1, -1, -1)):
        other = from_partner(value, axis, bit)
        low = (place >> bit) % 2 == 0
        value = jnp.stack([jnp.where(low, value, other), jnp.where(low, other, value)], axis=done)
    return value.reshape((2**bits,) + block.shape)


def cube_sum(value, axis="wt"):
    place = lax.axis_index(axis)
    bits = bits_of(axis)
    value = value.reshape((2,) * bits + value.shape[1:])
    for bit in range(bits):
        at = bits - 1 - bit
        mine = (place >> bit) % 2
        keep = lax.dynamic_index_in_dim(value, mine, at, keepdims=False)
        give = lax.dynamic_index_in_dim(value, 1 - mine, at, keepdims=False)
        value = keep.astype(jnp.float32) + from_partner(give.astype(half_type), axis, bit).astype(
            jnp.float32
        )
    return value


def group_gather(rows, axis="wt"):
    for bit in range(bits_of(axis) - 1, -1, -1):
        rows = jnp.concatenate([rows, from_partner(rows, axis, bit)], axis=0)
    return rows


def group_sum(rows, axis="wt"):
    for bit in range(bits_of(axis)):
        half = rows.shape[0] // 2
        got = from_partner(rows[half:].astype(half_type), axis, bit)
        rows = rows[:half].astype(jnp.float32) + got.astype(jnp.float32)
    return rows


def normalize(features):
    average = jnp.mean(features, axis=-1, keepdims=True)
    centred = features - average
    spread = jnp.mean(centred * centred, axis=-1, keepdims=True)
    scale = lax.rsqrt(spread + epsilon)
    return centred * scale, scale


def normalize_back(d_unit, unit, scale):
    return scale * (
        d_unit
        - jnp.mean(d_unit, axis=-1, keepdims=True)
        - unit * jnp.mean(d_unit * unit, axis=-1, keepdims=True)
    )


def rotary_tables(positions, head_width):
    half_width = head_width // 2
    frequency = jnp.exp(
        jnp.arange(half_width).astype(jnp.float32) * (-2.0 * math.log(rope_base) / head_width)
    )
    angles = frequency[:, None] * positions[None, :]
    return jnp.cos(angles), jnp.sin(angles)


def rotate(vectors, cosine, sine_table):
    features, count = vectors.shape
    half_width = cosine.shape[0]
    split = vectors.reshape(features // (2 * half_width), 2, half_width, count)
    first, second = split[:, 0], split[:, 1]
    return jnp.stack(
        [first * cosine - second * sine_table, second * cosine + first * sine_table], axis=1
    ).reshape(features, count)


def exact_gelu(inner):
    return jax.nn.gelu(inner, approximate=False)


def dot_on(left, right, left_dim, right_dim):
    return lax.dot_general(
        left, right, (((left_dim,), (right_dim,)), ((), ())), preferred_element_type=jnp.float32
    )


def matmul(left, right):
    return jnp.dot(left, right, preferred_element_type=jnp.float32)


def head_rows(value, head):
    blank = jnp.zeros((HD, value.shape[1]), value.dtype)
    heads = value.shape[0] // HD
    if heads == 1:
        return value
    return jnp.concatenate(
        [value[h * HD : (h + 1) * HD] if h == head else blank for h in range(heads)], axis=0
    )


def head_columns(value, head):
    if value.shape[1] == HD:
        return value
    lane = lax.broadcasted_iota(jnp.int32, value.shape, 1)
    inside = (lane >= head * HD) & (lane < (head + 1) * HD)
    return jnp.where(inside, value, jnp.zeros_like(value))


def forward_kernel(at, q_ref, k_ref, vt_ref, w_ref, out_ref, lse_ref, branch_ref):
    features = w_ref.shape[0]
    count = out_ref.shape[1]
    length = k_ref.shape[0]
    span = math.gcd(length, 512)
    queries = q_ref[:, at : at + count]
    for head in range(features // HD):
        rows = slice(head * HD, (head + 1) * HD)
        query = head_rows(queries, head)
        top = total = accum = None
        for start in range(0, length, span):
            scores = matmul(k_ref[start : start + span, :], query)
            block_top = jnp.max(scores, axis=0, keepdims=True)
            new_top = block_top if top is None else jnp.maximum(top, block_top)
            raised = jnp.exp(scores - new_top)
            weight = jnp.sum(raised, axis=0, keepdims=True)
            part = matmul(vt_ref[rows, start : start + span], raised.astype(half_type))
            if top is None:
                total, accum = weight, part
            else:
                shrink = jnp.exp(top - new_top)
                total = total * shrink + weight
                accum = accum * shrink + part
            top = new_top
        out_ref[rows, :] = accum / total
        lse_ref[head : head + 1, :] = top + jnp.log(total)
    branch_ref[...] = dot_on(out_ref[...].astype(half_type), w_ref[...], 0, 0)


def backward_kernel(first, at, *refs):
    q_ref, qn_ref, near_ref, far_ref, w_ref, out_ref, lse_ref, k_ref, kt_ref, v_ref = refs[:10]
    dk_in, dv_in, gw_in = (None, None, None) if first else refs[10:13]
    dq_ref, dk_ref, dv_ref, gw_ref = refs[-4:]
    features, count = out_ref.shape
    length = k_ref.shape[0]
    span = math.gcd(length, 512)
    heads = features // HD
    weights = w_ref[...]
    blocks = [near_ref[...], far_ref[...]]
    d_out = jnp.concatenate([dot_on(weights, d, 1, 1) for d in blocks], axis=1).astype(half_type)
    d_out_rows = jnp.concatenate([dot_on(d, weights, 1, 1) for d in blocks], axis=0).astype(
        half_type
    )
    attended = out_ref[...].astype(half_type)
    rows = count // 2
    grad = matmul(attended[:, :rows], blocks[0]) + matmul(attended[:, rows:], blocks[1])
    gw_ref[...] = grad if first else gw_in[...] + grad
    queries = [head_rows(q_ref[:, at : at + count], h) for h in range(heads)]
    d_outs = [head_rows(d_out, h) for h in range(heads)]
    query_columns = [head_columns(qn_ref[at : at + count, :], h) for h in range(heads)]
    d_out_columns = [head_columns(d_out_rows, h) for h in range(heads)]
    weighed = d_out.astype(jnp.float32) * out_ref[...]
    deltas = [
        jnp.sum(weighed[h * HD : (h + 1) * HD], axis=0, keepdims=True) for h in range(heads)
    ]
    d_query = [None] * heads
    for start in range(0, length, span):
        stop = start + span
        d_key = None if first else dk_in[start:stop, :]
        d_value = None if first else dv_in[start:stop, :]
        for h in range(heads):
            scores = matmul(k_ref[start:stop, :], queries[h])
            probs = jnp.exp(scores - lse_ref[h : h + 1, :])
            d_probs = matmul(v_ref[start:stop, :], d_outs[h])
            d_scores = (probs * (d_probs - deltas[h])).astype(half_type)
            value_part = matmul(probs.astype(half_type), d_out_columns[h])
            key_part = matmul(d_scores, query_columns[h])
            d_value = value_part if d_value is None else d_value + value_part
            d_key = key_part if d_key is None else d_key + key_part
            part = matmul(kt_ref[h * HD : (h + 1) * HD, start:stop], d_scores)
            d_query[h] = part if d_query[h] is None else d_query[h] + part
        dk_ref[start:stop, :] = d_key
        dv_ref[start:stop, :] = d_value
    for h in range(heads):
        dq_ref[h * HD : (h + 1) * HD, :] = d_query[h] * (1.0 / math.sqrt(HD))


kernel_params = pltpu.CompilerParams(vmem_limit_bytes=20 * 2**20)


def attention_forward(at, count, queries, keys, values_t, weights):
    features = queries.shape[0]
    length = keys.shape[0]
    heads = features // HD
    return pl.pallas_call(
        functools.partial(forward_kernel, at),
        out_shape=(
            jax.ShapeDtypeStruct((features, count), jnp.float32),
            jax.ShapeDtypeStruct((heads, count), jnp.float32),
            jax.ShapeDtypeStruct((count, weights.shape[1]), jnp.float32),
        ),
        compiler_params=kernel_params,
        cost_estimate=pl.CostEstimate(
            flops=16 * features * count * length,
            bytes_accessed=4 * features * length + 6 * features * count,
            transcendentals=heads * count * length,
        ),
    )(queries, keys, values_t, weights)


def attention_backward(at, count, tensors, sums):
    queries, keys, weights = tensors[0], tensors[7], tensors[4]
    features = queries.shape[0]
    length = keys.shape[0]
    first = sums is None
    total = jax.ShapeDtypeStruct((length, features), jnp.float32)
    given = len(tensors)
    return pl.pallas_call(
        functools.partial(backward_kernel, first, at),
        out_shape=(
            jax.ShapeDtypeStruct((features, count), jnp.float32),
            total,
            total,
            jax.ShapeDtypeStruct(weights.shape, jnp.float32),
        ),
        input_output_aliases={} if first else {given + i: 1 + i for i in range(3)},
        compiler_params=kernel_params,
        cost_estimate=pl.CostEstimate(
            flops=40 * features * count * length,
            bytes_accessed=22 * features * length,
            transcendentals=features // HD * count * length,
        ),
    )(*tensors, *(sums or ()))


def shards(tokens, w_qkv, w_attn_out, w_in, w_mlp_out, gain_one, gain_two, cotangent):
    seq_tokens = tokens[0]
    seq_cot = cotangent[0]
    tok_rows, model_width = seq_tokens.shape
    seq_count = lax.axis_size("seq")
    wt_count = lax.axis_size("wt")
    seq_place = lax.axis_index("seq")
    wt_place = lax.axis_index("wt")
    half_place = wt_place % 2
    slice_len = tok_rows * seq_count
    local_heads = H // seq_count
    local_width = 3 * model_width // seq_count
    own_rows = w_qkv.shape[0]
    hidden_units = w_mlp_out.shape[1]
    score_scale = 1.0 / math.sqrt(HD)
    half_ring = seq_count // 2
    along, side = seq_place // 2, seq_place % 2
    ring_place = jnp.where(side == 0, along, seq_count - 1 - along)

    def ahead(k):
        at = (ring_place + k) % seq_count
        return jnp.where(at < half_ring, 2 * at, 2 * (seq_count - 1 - at) + 1)

    arrival = [0]
    for k in range(1, half_ring):
        arrival += [k, seq_count - k]
    arrival.append(half_ring)
    chunks = [tuple(arrival[c : c + 2]) for c in range(0, seq_count, 2)]
    span = 2 * tok_rows

    token_blocks, (w_attn_out, gain_two) = ring_gather(seq_tokens, (w_attn_out, gain_two))
    gain_own = gain_one.astype(jnp.float32)[:, None]
    scaled_qkv = (gain_own * w_qkv.astype(jnp.float32)).astype(half_type)
    qkv_pieces = lax.all_to_all(
        scaled_qkv.reshape(own_rows, seq_count, local_heads, 3, HD)
        .transpose(1, 0, 3, 2, 4)
        .reshape(seq_count, own_rows, local_width),
        "seq",
        split_axis=0,
        concat_axis=0,
        tiled=True,
    )
    qkv_heads = cube_gather(qkv_pieces).transpose(1, 0, 2, 3).reshape(model_width, local_width)
    out_heads = cube_gather(w_attn_out).reshape(wt_count * own_rows, model_width)
    gain_rows = cube_gather(gain_two.reshape(1, own_rows)).reshape(wt_count * own_rows)
    gain_rows = gain_rows.astype(jnp.float32)

    scaled_in = gain_rows[:, None, None] * w_in.astype(jnp.float32)
    mixed = jnp.concatenate(
        [
            scaled_in[:, 0].astype(half_type).T,
            scaled_in[:, 1].astype(half_type).T,
            w_mlp_out.T,
        ],
        axis=0,
    )
    mixed, token_blocks[half_ring] = lax.optimization_barrier((mixed, token_blocks[half_ring]))
    feed_rows = w_in.shape[0]
    in_rows = jnp.zeros((2 * hidden_units, model_width), half_type)
    out_rows = jnp.zeros((hidden_units, model_width), half_type)
    for k, block in enumerate(ring_gather(mixed)):
        at = (0, ahead(k) * feed_rows)
        in_rows = lax.dynamic_update_slice(in_rows, block[: 2 * hidden_units], at)
        out_rows = lax.dynamic_update_slice(out_rows, block[2 * hidden_units :], at)
    group_cot = group_gather(seq_cot)

    units = [
        normalize(
            jnp.concatenate([token_blocks[k] for k in chunk], axis=0).astype(jnp.float32)
        )[0].astype(half_type)
        for chunk in chunks
    ]
    packed = jnp.concatenate([dot_on(qkv_heads, unit, 0, 1) for unit in units], axis=1)
    positions = jnp.concatenate(
        [half_place * slice_len + ahead(k) * tok_rows + jnp.arange(tok_rows) for k in arrival]
    ).astype(jnp.float32)
    cosine, sine_table = rotary_tables(positions, HD)
    third = local_width // 3
    queries = (rotate(packed[:third], cosine, sine_table).astype(half_type) * score_scale).astype(
        half_type
    )
    own_pairs = jnp.concatenate(
        [rotate(packed[third : 2 * third], cosine, sine_table), packed[2 * third :]], axis=0
    ).astype(half_type)
    pairs = jnp.concatenate([own_pairs, from_partner(own_pairs, "wt", 0)], axis=1)
    keys_t, values_t = pairs[:third], pairs[third:]
    keys, values = keys_t.T, values_t.T

    attended, log_totals, parts = {}, {}, {}
    for c in range(len(chunks) - 1, -1, -1):
        attended[c], log_totals[c], branch = attention_forward(
            c * span, span, queries, keys, values_t, out_heads
        )
        for at, k in enumerate(chunks[c]):
            parts[k] = branch[at * tok_rows : (at + 1) * tok_rows]
    inputs = seq_tokens.astype(jnp.float32)
    middle = inputs + ring_sum([parts[k] for k in range(seq_count)])
    unit_two, scale_two = normalize(middle)
    group_unit = group_gather(unit_two.astype(half_type))

    projected = dot_on(in_rows, group_unit, 1, 1)
    activated, gelu_pull = jax.vjp(exact_gelu, projected[:hidden_units])
    gate = projected[hidden_units:]
    hidden = (activated * gate).astype(half_type)
    d_hidden = dot_on(out_rows, group_cot, 1, 1)
    d_projected = jnp.concatenate(
        [gelu_pull(d_hidden * gate)[0], d_hidden * activated], axis=0
    ).astype(half_type)
    d_unit_two = group_sum(dot_on(d_projected, in_rows, 0, 0))
    d_middle = seq_cot.astype(jnp.float32) + normalize_back(d_unit_two, unit_two, scale_two)
    d_branch, mlp_rows = lax.optimization_barrier(
        (d_middle.astype(half_type), dot_on(hidden, out_rows, 0, 0))
    )
    d_blocks = ring_gather(d_branch)
    output = (middle + group_sum(mlp_rows)).astype(half_type)
    query_rows = queries.T
    d_queries, sums = [], None
    for c, (near, far) in enumerate(chunks):
        d_query, *sums = attention_backward(
            c * span,
            span,
            (
                queries,
                query_rows,
                d_blocks[near],
                d_blocks[far],
                out_heads,
                attended[c],
                log_totals[c],
                keys,
                keys_t,
                values,
            ),
            sums,
        )
        d_queries.append(d_query)
    d_query = jnp.concatenate(d_queries, axis=1)
    *sums, grad_out = sums

    grad_mixed = jnp.concatenate(
        [dot_on(d_projected, group_unit, 1, 0), dot_on(hidden, group_cot, 1, 0)], axis=0
    ).astype(half_type)
    grad_ring = Steps(ring_sum_steps(
        [
            lax.dynamic_slice(
                grad_mixed, (0, ahead(k) * feed_rows), (3 * hidden_units, feed_rows)
            )
            for k in range(seq_count)
        ]
    ))
    for _ in range(seq_count // 2 - 2):
        grad_ring.advance()
    sums = grad_ring.tie(sums)
    attn_owned = cube_sum(grad_out.reshape(wt_count, own_rows, model_width))

    d_pairs = jnp.concatenate(sums, axis=1).T
    d_own = d_pairs[:, :slice_len] + from_partner(
        d_pairs[:, slice_len:].astype(half_type), "wt", 0
    ).astype(jnp.float32)
    d_packed = jnp.concatenate(
        [
            rotate(d_query, cosine, -sine_table),
            rotate(d_own[:third], cosine, -sine_table),
            d_own[third:],
        ],
        axis=0,
    ).astype(half_type)
    grad_heads = dot_on(jnp.concatenate(units, axis=0), d_packed, 0, 1).reshape(
        seq_count, wt_count, own_rows, local_width
    )
    d_unit_parts = dot_on(d_packed, qkv_heads, 0, 1)
    last_ring = Steps(ring_sum_steps(
        [
            d_unit_parts[at * tok_rows : (at + 1) * tok_rows]
            for at in (arrival.index(k) for k in range(seq_count))
        ]
    ))
    last_ring.pending = grad_ring.tie(last_ring.pending)
    last_ring.advance()
    mixed_owned = grad_ring.finish()
    in_unscaled = jnp.stack(
        [mixed_owned[:hidden_units].T, mixed_owned[hidden_units : 2 * hidden_units].T], axis=1
    )
    in_owned = in_unscaled * gain_rows[:, None, None]
    mlp_owned = mixed_owned[2 * hidden_units :].T
    gain_two_part = jnp.sum(in_unscaled * w_in.astype(jnp.float32), axis=(1, 2))
    gain_row = jnp.pad(
        gain_two_part.reshape(wt_count, 1, own_rows),
        ((0, 0), (0, 7), (0, local_width - own_rows)),
    )
    summed = cube_sum(
        jnp.concatenate(
            [
                grad_heads.transpose(1, 0, 2, 3).reshape(wt_count, model_width // wt_count, -1),
                gain_row,
            ],
            axis=1,
        )
    )
    gain_two_owned = summed[model_width // wt_count, :own_rows]
    grad_pieces = (
        summed[: model_width // wt_count]
        .reshape(seq_count, own_rows, local_width)
        .astype(half_type)
    )
    for _ in range(seq_count // 2 - 4):
        last_ring.advance()
    grad_pieces = last_ring.tie(grad_pieces)
    d_unit = last_ring.finish()
    unit_one, scale_one = normalize(inputs)
    input_grad = (d_middle + normalize_back(d_unit, unit_one, scale_one)).astype(half_type)
    grad_rows = lax.all_to_all(grad_pieces, "seq", split_axis=0, concat_axis=0, tiled=True)
    qkv_unscaled = (
        grad_rows.reshape(seq_count, own_rows, 3, local_heads, HD)
        .transpose(1, 0, 3, 2, 4)
        .reshape(own_rows, 3 * model_width)
        .astype(jnp.float32)
    )
    qkv_owned = qkv_unscaled * gain_own
    gain_one_owned = jnp.sum(qkv_unscaled * w_qkv.astype(jnp.float32), axis=1)
    return (
        output.reshape(1, tok_rows, model_width),
        input_grad.reshape(1, tok_rows, model_width),
        qkv_owned,
        attn_owned,
        in_owned,
        mlp_owned,
        gain_one_owned,
        gain_two_owned,
    )


def solution(mesh):
    in_specs = (
        P("wt", "seq", None),
        P(("seq", "wt"), None),
        P(("seq", "wt"), None),
        P("seq", None, "wt"),
        P("seq", "wt"),
        P(("seq", "wt")),
        P(("seq", "wt")),
        P("wt", "seq", None),
    )
    out_specs = (
        P("wt", "seq", None),
        P("wt", "seq", None),
        P(("seq", "wt"), None),
        P(("seq", "wt"), None),
        P("seq", None, "wt"),
        P("seq", "wt"),
        P(("seq", "wt")),
        P(("seq", "wt")),
    )
    return jax.shard_map(shards, mesh=mesh, in_specs=in_specs, out_specs=out_specs, check_vma=False)
```
